512 devices in a mesh: region: 32 (over z, x), sub: 16 (over y, core).
Axes of the slice: x: 4, y: 8, z: 8, core: 2. Of those that a mesh axis runs over, the one named last changes fastest.
Arguments:
- coords: float32 [3, 524288], P(None, ('region', 'sub')), may hold values from 0 to 2051, as said below
- noise_var: float32 [524288], P(('region', 'sub')), may hold values from 3 to 6
- pair_list: int32 [3, 2048], P(None, ('region', 'sub')), may hold values from 0 to 1, as said below
- probes: float32 [64, 524288], P(None, ('region', 'sub')), may hold values from -15 to 15
Outputs:
- solution: float32 [64, 524288], P(None, ('region', 'sub'))
- residual: float32 [64, 524288], P(None, ('region', 'sub'))
The draws below stay inside these ranges and needn't reach their ends.
Inputs may be any that keep to these rules, and one draw needn't show every extreme that they name: `coords`: row 0 of column p lies in [p // 256, p // 256 + 4); rows 1 and 2 lie in [0, 4). `pair_list`: entry k, b is 0 wherever b + k + 1 >= 2048.
All inputs are finite; a program needn't handle non-finite values.
Results may differ from the reference program's by a relative error of at most 0.0003.
Values sent between devices are 32-bit elements; how exact they have to be, the bound alone decides.
No kernel may reach another device: no remote copies, remote signals or barrier semaphores. Data moves between devices by JAX's collectives and lax.ppermute only.
A program may use at most 64 MiB of HBM per device.

```python
import jax
import jax.numpy as jnp
from jax import lax

BLOCK = 256
BPD = 4
LINKS = 3
PROBES = 64
ITERS = 3
NBLOCKS = 2048
NPTS = 524288


def draw_coords(key, part):
    key = jax.random.fold_in(key, 11)
    spread = jax.random.uniform(key, (3, NPTS), jnp.float32, 0.0, 4.0)
    block_pos = (jnp.arange(NPTS) // BLOCK).astype(jnp.float32)
    along = jnp.stack([block_pos, jnp.zeros_like(block_pos), jnp.zeros_like(block_pos)], axis=0)
    return spread + along


def draw_pair_list(key, part):
    key = jax.random.fold_in(key, 12)
    rolls = jax.random.randint(key, (LINKS, NBLOCKS), 0, 4)
    ahead = jnp.arange(LINKS)[:, None] + 1 + jnp.arange(NBLOCKS)[None, :]
    return jnp.where((rolls < 3) & (ahead < NBLOCKS), 1, 0).astype(jnp.int32)


def draw_probes(key, part):
    key = jax.random.fold_in(key, 13)
    position = jnp.arange(NPTS, dtype=jnp.float32) / NPTS
    values = jnp.clip(jax.random.normal(key, (PROBES, NPTS), jnp.float32), -5.0, 5.0) * (1.0 + 2.0 * position)[None, :]
    return values


def steps_of(key, extent, cuts, low, high):
    def one(axis_at, shards_of):
        draws = jax.random.uniform(jax.random.fold_in(jax.random.fold_in(key, 6), axis_at), (shards_of,), jnp.float32, low / len(cuts), high / len(cuts))
        return jnp.repeat(jnp.exp(draws), extent[axis_at] // shards_of).reshape((-1,) + (1,) * (len(extent) - axis_at - 1))

    level = one(*cuts[0])
    for cut in cuts[1:]:
        level = level * one(*cut)
    return level


def setup_inputs(seed: int = 0) -> dict:
    splits = jax.random.split(jax.random.key(seed), 5)
    return {
        "coords": draw_coords(jax.random.fold_in(splits[4], 71), 0),
        "noise_var": jnp.clip(3.0 + 3.0 * jax.random.uniform(splits[1], (NPTS,), jnp.float32) ** steps_of(splits[1], (NPTS,), ((0, 512),), -0.2, 0.2), 3.0, 6.0),
        "pair_list": draw_pair_list(jax.random.fold_in(splits[4], 71), 0),
        "probes": draw_probes(jax.random.fold_in(splits[4], 71), 0),
    }


def wendland(left, right):
    squared = (left[0][..., :, None] - right[0][..., None, :]) ** 2
    squared = squared + (left[1][..., :, None] - right[1][..., None, :]) ** 2
    squared = squared + (left[2][..., :, None] - right[2][..., None, :]) ** 2
    distance = jnp.sqrt(squared)
    support = jnp.maximum(1.0 - distance, 0.0)
    return support ** 4 * (4.0 * distance + 1.0)

def block_products(left_c, right_c, left_v, right_v, weight, transpose):
    groups = NBLOCKS // BPD

    def regroup(array):
        return jnp.moveaxis(array.reshape(array.shape[0], groups, BPD, BLOCK), 1, 0)

    def one_group(items):
        lc, rc, lv, rv, wt = items
        kernel_block = wendland(lc, rc) * wt[:, None, None]
        forward = jnp.einsum('pbj,bij->pbi', rv, kernel_block, precision=lax.Precision.HIGHEST)
        if transpose:
            backward = jnp.einsum('pbi,bij->pbj', lv, kernel_block, precision=lax.Precision.HIGHEST)
        else:
            backward = jnp.zeros_like(forward)
        return (forward, backward)
    forward, backward = lax.map(one_group, (regroup(left_c), regroup(right_c), regroup(left_v), regroup(right_v), weight.reshape(groups, BPD)))

    def ungroup(array):
        return jnp.moveaxis(array, 0, 1).reshape(PROBES, NBLOCKS, BLOCK)
    return (ungroup(forward), ungroup(backward))

def apply_operator(vector, noise_var, coords, pair_list):
    blocks_c = coords.reshape(3, NBLOCKS, BLOCK)
    blocks_v = vector.reshape(PROBES, NBLOCKS, BLOCK)
    result = (noise_var[None, :] * vector).reshape(PROBES, NBLOCKS, BLOCK)
    for offset in range(LINKS + 1):
        if offset == 0:
            forward, unused = block_products(blocks_c, blocks_c, blocks_v, blocks_v, jnp.ones((NBLOCKS,), vector.dtype), False)
            result = result + forward
        else:
            partner_c = jnp.concatenate([blocks_c[:, offset:], jnp.zeros((3, offset, BLOCK), coords.dtype)], axis=1)
            partner_v = jnp.concatenate([blocks_v[:, offset:], jnp.zeros((PROBES, offset, BLOCK), vector.dtype)], axis=1)
            weight = pair_list[offset - 1].astype(vector.dtype)
            forward, backward = block_products(blocks_c, partner_c, blocks_v, partner_v, weight, True)
            shifted = jnp.concatenate([jnp.zeros((PROBES, offset, BLOCK), vector.dtype), backward[:, :NBLOCKS - offset]], axis=1)
            result = result + forward + shifted
    return result.reshape(PROBES, NPTS)

def reference(coords, noise_var, pair_list, probes):
    solution = jnp.zeros_like(probes)
    residual = probes
    direction = probes
    res_norm = lax.optimization_barrier(jnp.sum(residual * residual, axis=1))
    for step in range(ITERS):
        product = apply_operator(direction, noise_var, coords, pair_list)
        step_size = res_norm / lax.optimization_barrier(jnp.sum(direction * product, axis=1))
        solution = solution + step_size[:, None] * direction
        residual = residual - step_size[:, None] * product
        next_norm = lax.optimization_barrier(jnp.sum(residual * residual, axis=1))
        direction = residual + (next_norm / res_norm)[:, None] * direction
        res_norm = next_norm
    return (solution, residual)
```

```python
import functools

import jax
import jax.numpy as jnp
from jax import lax
from jax.experimental import pallas as pl
from jax.experimental.pallas import tpu as pltpu
from jax.sharding import PartitionSpec as P

ITERS = 3
AXES = ("region", "sub")
SHIFT = 6.0
MAX_AMP = 100.0
MAX_NORM = 30.0
F32 = jnp.float32
BF16 = jnp.bfloat16
VMEM_LIMIT = 40 * 1024 * 1024


def shifted(array, by):
    count = lax.axis_size(AXES)
    pairs = [(i, i + by) for i in range(count) if 0 <= i + by < count]
    return lax.ppermute(array, AXES, pairs)


def wendland(left, right):
    squared = (left[0][..., :, None] - right[0][..., None, :]) ** 2
    squared = squared + (left[1][..., :, None] - right[1][..., None, :]) ** 2
    squared = squared + (left[2][..., :, None] - right[2][..., None, :]) ** 2
    distance = jnp.sqrt(squared)
    support = jnp.maximum(1.0 - distance, 0.0)
    return support**4 * (4.0 * distance + 1.0)


def squares(residual):
    return lax.psum(jnp.sum(residual * residual, axis=1), AXES)


def plain(coords, noise_var, pair_list, probes):
    probe_count, points_here = probes.shape
    links = pair_list.shape[0]
    blocks_here = pair_list.shape[1]
    block_len = points_here // blocks_here
    span_cols = links * block_len
    local_c = coords.reshape(3, blocks_here, block_len)
    weights = pair_list.astype(F32)
    ahead_c = shifted(coords[:, :span_cols], -1)
    ext_c = jnp.concatenate([local_c, ahead_c.reshape(3, links, block_len)], axis=1)

    def step(_, state):
        solution, residual, direction, res_norm = state
        ahead_v = shifted(direction[:, :span_cols], -1)
        ext_v = jnp.concatenate([direction, ahead_v], axis=1).reshape(probe_count, blocks_here + links, block_len)
        local_v = ext_v[:, :blocks_here]
        result = (noise_var[None, :] * direction).reshape(probe_count, blocks_here, block_len)
        spill = jnp.zeros((probe_count, blocks_here + links, block_len), F32)
        for offset in range(links + 1):
            kernel_block = wendland(local_c, ext_c[:, offset : offset + blocks_here])
            if offset > 0:
                kernel_block = kernel_block * weights[offset - 1][:, None, None]
            result = result + jnp.einsum(
                "pbj,bij->pbi", ext_v[:, offset : offset + blocks_here], kernel_block, precision=lax.Precision.HIGHEST
            )
            if offset > 0:
                spill = spill.at[:, offset : offset + blocks_here].add(
                    jnp.einsum("pbi,bij->pbj", local_v, kernel_block, precision=lax.Precision.HIGHEST)
                )
        result = result + spill[:, :blocks_here]
        result = result.at[:, :links].add(shifted(spill[:, blocks_here:], 1))
        product = result.reshape(probe_count, points_here)
        step_size = res_norm / lax.psum(jnp.sum(direction * product, axis=1), AXES)
        solution = solution + step_size[:, None] * direction
        residual = residual - step_size[:, None] * product
        next_norm = squares(residual)
        direction = residual + (next_norm / res_norm)[:, None] * direction
        return solution, residual, direction, next_norm

    state = (jnp.zeros_like(probes), probes, probes, squares(probes))
    solution, residual, _, _ = lax.fori_loop(0, ITERS, step, state)
    return solution, residual


def pack_kernel(coords, noise, pair, probes, to_left, to_right):
    links, blocks = pair.shape
    length = coords.shape[1] // blocks
    span = links * length
    start = coords.shape[1] - span
    rows = probes.shape[0]
    to_left[0:rows, :] = probes[:, 0:span]
    to_right[0:rows, :] = probes[:, start:]
    to_left[rows : rows + 8, :] = jnp.concatenate([coords[:, 0:span], jnp.zeros((5, span), F32)], axis=0)
    flags = [
        jnp.concatenate(
            [jnp.full((1, length), pair[k, b].astype(F32), F32) for b in range(blocks - links, blocks)], axis=1
        )
        for k in range(links)
    ]
    to_right[rows : rows + 8, :] = jnp.concatenate(
        [coords[:, start:]] + flags + [jnp.zeros((8 - 3 - links, span), F32)], axis=0
    )


def split(value):
    high = value.astype(BF16)
    return high, (value - high.astype(F32)).astype(BF16)


def spread(halves, low, middle, high, rows, span, here):
    for ref, at, size in ((low, 0, span), (middle, span, here), (high, span + here, span)):
        top, rest = split(ref[0:rows, 0:size])
        halves[0:rows, at : at + size] = top
        halves[rows : 2 * rows, at : at + size] = rest


def product(halves, k_high, k_low, noise, vector, out, to_left, to_right, rows, length, blocks, links):
    depth = (2 * links + 1) * length
    span = links * length
    start = blocks * length - span
    for i in range(blocks):
        window = slice(i * length, i * length + depth)
        at = slice(i * length, (i + 1) * length)
        both = jnp.dot(halves[:, window], k_high[i], preferred_element_type=F32)
        rest = jnp.dot(halves[0:rows, window], k_low[i], preferred_element_type=F32)
        value = both[0:rows] + (both[rows : 2 * rows] + rest) + (noise[:, at] - SHIFT) * vector[:, at]
        out[:, at] = value
        if to_left is not None:
            if i < links:
                to_left[:, at] = value
            if i >= blocks - links:
                to_right[:, i * length - start : (i + 1) * length - start] = value


def first_kernel(
    coords, noise, pair, probes, low, high, k_high, k_low, out, to_left, to_right, halves, columns, *, strip
):
    links, blocks = pair.shape
    rows, here = probes.shape
    length = here // blocks
    span = links * length
    for ref, at, size, row in ((low, 0, span, rows), (coords, span, here, 0), (high, span + here, span, rows)):
        turned = jnp.transpose(jnp.concatenate([ref[row : row + 3, 0:size], jnp.zeros((5, size), F32)], axis=0))
        for d in range(3):
            columns[d, at : at + size, :] = jnp.broadcast_to(turned[:, d : d + 1], (size, 128))
    spread(halves, low, probes, high, rows, span, here)
    for i in range(blocks):
        mine = [coords[d : d + 1, i * length : (i + 1) * length] for d in range(3)]
        for o in range(2 * links + 1):
            j = i + o
            k = abs(o - links) - 1
            if o == links:
                flag = jnp.ones((1, length), F32)
            elif o > links:
                flag = jnp.full((1, length), pair[k, i].astype(F32), F32)
            elif j >= links:
                flag = jnp.full((1, length), pair[k, j - links].astype(F32), F32)
            else:
                flag = low[rows + 3 + k : rows + 4 + k, j * length : (j + 1) * length]
            flag4 = 4.0 * flag

            def body(s, _):
                at = pl.multiple_of(s * strip, strip)
                from_row = pl.multiple_of(j * length + s * strip, strip)
                squared = None
                for d in range(3):
                    column = columns[d, pl.ds(from_row, strip), :]
                    away = jnp.concatenate([column] * (length // 128), axis=1) - mine[d]
                    squared = away * away if squared is None else squared + away * away
                squared = jnp.maximum(squared, 1e-30)
                distance = squared * lax.rsqrt(squared)
                support = jnp.maximum(1.0 - distance, 0.0)
                support = support * support
                value = support * support * (flag4 * distance + flag)
                top, rest = split(value)
                k_high[i, pl.ds(o * length + at, strip), :] = top
                k_low[i, pl.ds(o * length + at, strip), :] = rest
                return 0

            lax.fori_loop(0, length // strip, body, 0)
    product(halves, k_high, k_low, noise, probes, out, to_left, to_right, rows, length, blocks, links)


def next_kernel(noise, vector, low, high, k_high, k_low, out, to_left, to_right, halves):
    rows, here = vector.shape
    blocks, depth, length = k_high.shape
    span = low.shape[1]
    spread(halves, low, vector, high, rows, span, here)
    product(halves, k_high, k_low, noise, vector, out, to_left, to_right, rows, length, blocks, span // length)


def last_kernel(noise, first, second, vector, low, high, k_high, k_low, out, sums, halves):
    rows, here = vector.shape
    blocks, depth, length = k_high.shape
    span = low.shape[1]
    spread(halves, low, vector, high, rows, span, here)
    product(halves, k_high, k_low, noise, vector, out, None, None, rows, length, blocks, span // length)
    basis = (first, second, vector, out)
    lane = lax.broadcasted_iota(jnp.int32, (rows, 128), 1)
    table = jnp.zeros((rows, 128), F32)
    for power in range(2 * ITERS + 1):
        left, right = basis[power // 2], basis[power - power // 2]
        part = None
        for at in range(0, here, 128):
            term = left[:, at : at + 128] * right[:, at : at + 128]
            part = term if part is None else part + term
        table = jnp.where(lane == power, jnp.sum(part, axis=1, keepdims=True), table)
    turned = jnp.transpose(table)[0:8, :]
    compact = jnp.concatenate([turned[0:4], turned[4:8]], axis=1)
    sums[...] = jnp.broadcast_to(compact[None], sums.shape)


def polynomials(moment):
    def dot(p, q):
        total, size = 0.0, 0.0
        for i, x in enumerate(p):
            for j, y in enumerate(q):
                term = x * y * moment[i + j]
                total, size = total + term, size + jnp.abs(term)
        return total, size

    def add(p, q, factor):
        count = max(len(p), len(q))
        p, q = p + [0.0] * (count - len(p)), q + [0.0] * (count - len(q))
        return [x + factor * y for x, y in zip(p, q)]

    one = jnp.ones_like(moment[0])
    solution, residual, direction = [jnp.zeros_like(one)], [one], [one]
    norm = moment[0]
    good = norm > 0.0
    for step in range(ITERS):
        image = add([0.0 * one] + direction, direction, SHIFT)
        curvature, size = dot(direction, image)
        good = good & (size <= MAX_AMP * curvature)
        step_size = norm / curvature
        solution = add(solution, direction, step_size)
        residual = add(residual, image, -step_size)
        new, size = dot(residual, residual)
        if step < ITERS - 1:
            good = good & (size <= MAX_AMP * new)
            direction = add(residual, direction, new / norm)
        norm = new
    size = sum(jnp.abs(x) * jnp.sqrt(moment[2 * i]) for i, x in enumerate(residual))
    good = good & (size * size <= MAX_NORM * MAX_NORM * norm)
    return solution, residual, good


def small_kernel(sums, coefficients, good):
    total = jnp.sum(sums[...], axis=0)
    moment = [total[k : k + 1, 0:64] for k in range(4)] + [total[k : k + 1, 64:128] for k in range(3)]
    solution, residual, fine = polynomials(moment)
    table = jnp.concatenate(solution + residual + [jnp.zeros_like(moment[0])], axis=0)
    table = jnp.concatenate([table, jnp.zeros_like(table)], axis=1)
    coefficients[...] = jnp.transpose(jnp.concatenate([table, jnp.zeros((120, 128), F32)], axis=0))[0:64]
    good[...] = jnp.min(jnp.where(fine, 1.0, 0.0), axis=1, keepdims=True)


def combine_kernel(coefficients, first, second, third, fourth, solution, residual):
    basis = (first[...], second[...], third[...], fourth[...])

    def mix(at, count):
        total = coefficients[:, at : at + 1] * basis[0]
        for k in range(1, count):
            total = total + coefficients[:, at + k : at + k + 1] * basis[k]
        return total

    solution[...] = mix(0, ITERS)
    residual[...] = mix(ITERS, ITERS + 1)


def in_vmem(array):
    return pltpu.with_memory_space_constraint(array, pltpu.VMEM)


def call(kernel, name, out_shape, in_specs=None, scratch_shapes=()):
    kwargs = {} if in_specs is None else {"in_specs": in_specs}
    return pl.pallas_call(
        kernel,
        out_shape=out_shape,
        scratch_shapes=scratch_shapes,
        compiler_params=pltpu.CompilerParams(vmem_limit_bytes=VMEM_LIMIT),
        name=name,
        **kwargs,
    )


def per_device(coords, noise_var, pair_list, probes):
    rows, here = probes.shape
    links, blocks = pair_list.shape
    length = here // blocks
    span = links * length
    depth = (2 * links + 1) * length
    noise = noise_var.reshape(1, here)
    vmem, smem = pl.BlockSpec(memory_space=pltpu.VMEM), pl.BlockSpec(memory_space=pltpu.SMEM)
    whole = jax.ShapeDtypeStruct((rows, here), F32)
    part = jax.ShapeDtypeStruct((rows, span), F32)
    halves = pltpu.VMEM((2 * rows, here + 2 * span), BF16)
    table = jax.ShapeDtypeStruct((blocks, depth, length), BF16)

    packed = jax.ShapeDtypeStruct((rows + 8, span), F32)
    to_left, to_right = call(pack_kernel, "pack", (packed, packed), [vmem, vmem, smem, vmem])(
        coords, noise, pair_list, probes
    )
    low, high = shifted(to_right, 1), shifted(to_left, -1)
    k_high, k_low, second, to_left, to_right = call(
        functools.partial(first_kernel, strip=32),
        "first",
        (table, table, whole, part, part),
        [vmem, vmem, smem, vmem, vmem, vmem],
        [halves, pltpu.VMEM((3, here + 2 * span, 128), F32)],
    )(coords, noise, pair_list, probes, low, high)
    low, high = shifted(to_right, 1), shifted(to_left, -1)
    third, to_left, to_right = call(next_kernel, "next", (whole, part, part), None, [halves])(
        noise, second, low, high, k_high, k_low
    )
    low, high = shifted(to_right, 1), shifted(to_left, -1)
    regions, subs = lax.axis_size("region"), lax.axis_size("sub")
    fourth, sums = call(
        last_kernel, "last", (whole, jax.ShapeDtypeStruct((regions, 4, 128), F32)), None, [halves]
    )(noise, probes, second, third, low, high, k_high, k_low)
    sums = jnp.sum(lax.all_to_all(sums, "region", 0, 0), axis=0)
    sums = lax.all_to_all(jnp.broadcast_to(sums[None], (subs, 4, 128)), "sub", 0, 0)
    coefficients, good = call(
        small_kernel, "small", (jax.ShapeDtypeStruct((rows, 128), F32), jax.ShapeDtypeStruct((1, 1), F32))
    )(sums)

    def combine(coords, noise_var, pair_list, probes, second, third, fourth, coefficients):
        return tuple(call(combine_kernel, "combine", (whole, whole))(coefficients, probes, second, third, fourth))

    def loop(coords, noise_var, pair_list, probes, second, third, fourth, coefficients):
        return plain(coords, noise_var, pair_list, probes)

    return lax.cond(
        good[0, 0] > 0, combine, loop, coords, noise_var, pair_list, probes, second, third, fourth, coefficients
    )


def solution(mesh):
    in_specs = (P(None, AXES), P(AXES), P(None, AXES), P(None, AXES))
    out_specs = (P(None, AXES), P(None, AXES))
    return jax.shard_map(per_device, mesh=mesh, in_specs=in_specs, out_specs=out_specs, check_vma=False)
```

```python
import functools

import jax
import jax.numpy as jnp
from jax import lax
from jax.experimental import pallas as pl
from jax.experimental.pallas import tpu as pltpu
from jax.sharding import PartitionSpec as P

ITERS = 3
AXES = ("region", "sub")
SHIFT = 6.0
MAX_AMP = 100.0
MAX_NORM = 30.0
STRIP = 32
PACKS = 4
F32 = jnp.float32
BF16 = jnp.bfloat16
VMEM_LIMIT = 40 * 1024 * 1024


def shifted(array, by):
    count = lax.axis_size(AXES)
    pairs = [(i, i + by) for i in range(count) if 0 <= i + by < count]
    return lax.ppermute(array, AXES, pairs)


def wendland(left, right):
    squared = (left[0][..., :, None] - right[0][..., None, :]) ** 2
    squared = squared + (left[1][..., :, None] - right[1][..., None, :]) ** 2
    squared = squared + (left[2][..., :, None] - right[2][..., None, :]) ** 2
    distance = jnp.sqrt(squared)
    support = jnp.maximum(1.0 - distance, 0.0)
    return support**4 * (4.0 * distance + 1.0)


def squares(residual):
    return lax.psum(jnp.sum(residual * residual, axis=1), AXES)


def plain(coords, noise_var, pair_list, probes):
    probe_count, points_here = probes.shape
    links = pair_list.shape[0]
    blocks_here = pair_list.shape[1]
    block_len = points_here // blocks_here
    span_cols = links * block_len
    local_c = coords.reshape(3, blocks_here, block_len)
    weights = pair_list.astype(F32)
    ahead_c = shifted(coords[:, :span_cols], -1)
    ext_c = jnp.concatenate([local_c, ahead_c.reshape(3, links, block_len)], axis=1)

    def step(_, state):
        solution, residual, direction, res_norm = state
        ahead_v = shifted(direction[:, :span_cols], -1)
        ext_v = jnp.concatenate([direction, ahead_v], axis=1).reshape(probe_count, blocks_here + links, block_len)
        local_v = ext_v[:, :blocks_here]
        result = (noise_var[None, :] * direction).reshape(probe_count, blocks_here, block_len)
        spill = jnp.zeros((probe_count, blocks_here + links, block_len), F32)
        for offset in range(links + 1):
            kernel_block = wendland(local_c, ext_c[:, offset : offset + blocks_here])
            if offset > 0:
                kernel_block = kernel_block * weights[offset - 1][:, None, None]
            result = result + jnp.einsum(
                "pbj,bij->pbi", ext_v[:, offset : offset + blocks_here], kernel_block, precision=lax.Precision.HIGHEST
            )
            if offset > 0:
                spill = spill.at[:, offset : offset + blocks_here].add(
                    jnp.einsum("pbi,bij->pbj", local_v, kernel_block, precision=lax.Precision.HIGHEST)
                )
        result = result + spill[:, :blocks_here]
        result = result.at[:, :links].add(shifted(spill[:, blocks_here:], 1))
        product = result.reshape(probe_count, points_here)
        step_size = res_norm / lax.psum(jnp.sum(direction * product, axis=1), AXES)
        solution = solution + step_size[:, None] * direction
        residual = residual - step_size[:, None] * product
        next_norm = squares(residual)
        direction = residual + (next_norm / res_norm)[:, None] * direction
        return solution, residual, direction, next_norm

    state = (jnp.zeros_like(probes), probes, probes, squares(probes))
    solution, residual, _, _ = lax.fori_loop(0, ITERS, step, state)
    return solution, residual


def split(value):
    high = value.astype(BF16)
    return high, (value - high.astype(F32)).astype(BF16)


def pack_kernel(odd, coords, pair, probes, to_mate, to_next, sem):
    links, blocks = pair.shape
    length = coords.shape[1] // blocks
    span = links * length
    rows = probes.shape[0]
    far = (blocks - links) * length
    is_odd = odd[0] == 1
    copies = []
    for slot, (out, start) in enumerate(
        ((to_next, jnp.where(is_odd, far, 0)), (to_mate, jnp.where(is_odd, 0, far)))
    ):
        at = pl.ds(pl.multiple_of(start, 128), span)
        for n in range(PACKS):
            share = pl.ds(n * (rows // PACKS), rows // PACKS)
            copies.append(pltpu.make_async_copy(probes.at[share, at], out.at[share], sem.at[slot * PACKS + n]))
            copies[-1].start()
    flags = []
    for k in range(links):
        flags.append(
            jnp.concatenate([jnp.full((1, length), pair[k, b].astype(F32), F32) for b in range(blocks)], axis=1)
        )
    extra = jnp.concatenate([coords[...]] + flags + [jnp.zeros((8 - 3 - links, blocks * length), F32)], axis=0)
    first, last = extra[:, 0:span], extra[:, far:]
    to_next[rows : rows + 8, :] = jnp.where(is_odd, last, first)
    to_mate[rows : rows + 8, :] = jnp.where(is_odd, first, last)
    for copy in copies:
        copy.wait()


def fill_columns(columns, at, block):
    turned = jnp.transpose(block)
    for d in range(3):
        columns[d, at : at + turned.shape[0], :] = jnp.broadcast_to(turned[:, d : d + 1], (turned.shape[0], 128))


def fill_rows(rows, coords):
    for d in range(3):
        rows[d] = jnp.broadcast_to(coords[d : d + 1, :], rows.shape[1:])


def fill_strip(columns, from_row, strip, rows, lanes, flag, stores):
    column = [columns[d, pl.ds(from_row, strip), :].reshape(strip // 8, 8, 128) for d in range(3)]
    for lane, one_flag, store in zip(lanes, flag, stores):
        squared = None
        for d in range(3):
            away = column[d] - rows[d, :, pl.ds(lane, 128)][None]
            squared = away * away if squared is None else squared + away * away
        squared = jnp.maximum(squared, 1e-30)
        distance = squared * lax.rsqrt(squared)
        support = jnp.maximum(1.0 - distance, 0.0)
        support = support * support
        value = support * support * ((4.0 * one_flag)[None] * distance + one_flag[None])
        store(*split(value.reshape(strip, 128)))


def store_halves(halves, at, vector):
    rows, size = vector.shape
    top, rest = split(vector)
    halves[0:rows, at : at + size] = top
    halves[rows : 2 * rows, at : at + size] = rest


def multiply(halves, rows, depth, k_high, k_low):
    both = jnp.dot(halves[:, 0:depth], k_high, preferred_element_type=F32)
    rest = jnp.dot(halves[0:rows, 0:depth], k_low, preferred_element_type=F32)
    return both[0:rows] + (both[rows : 2 * rows] + rest)


def local_product(noise, vector, k_high, k_low, out, halves):
    rows, here = vector.shape
    blocks, _, length = k_high.shape
    store_halves(halves, 0, vector[...])
    for i in range(blocks):
        at = slice(i * length, (i + 1) * length)
        value = multiply(halves, rows, here, k_high[i], k_low[i])
        out[:, at] = value + (noise[:, at] - SHIFT) * vector[:, at]


def local_first_kernel(coords, noise, pair, probes, k_high, k_low, out, first, halves, columns, rows, flags):
    links, blocks = pair.shape
    here = probes.shape[1]
    length = here // blocks
    for j in range(blocks):
        own = coords[:, j * length : (j + 1) * length]
        fill_columns(columns, j * length, jnp.concatenate([own, jnp.zeros((5, length), F32)], axis=0))
    fill_rows(rows, coords)
    for j in range(blocks):
        for i in range(blocks):
            if i == j:
                flag = 1.0
            elif abs(i - j) <= links:
                flag = pair[abs(i - j) - 1, min(i, j)].astype(F32)
            else:
                flag = 0.0
            flags[j, :, i * length : (i + 1) * length] = jnp.full((8, length), flag, F32)

    def store_to(i, row, lane):
        def store(top, rest):
            k_high[i, pl.ds(row, STRIP), lane : lane + 128] = top
            k_low[i, pl.ds(row, STRIP), lane : lane + 128] = rest

        return store

    def body(s, _):
        row = pl.multiple_of(s * STRIP, STRIP)
        block = s // (length // STRIP)
        lanes = list(range(0, here, 128))
        fill_strip(
            columns,
            row,
            STRIP,
            rows,
            lanes,
            [flags[block, :, pl.ds(lane, 128)] for lane in lanes],
            [store_to(lane // length, row, lane % length) for lane in lanes],
        )
        return 0

    lax.fori_loop(0, here // STRIP, body, 0)
    local_product(noise, probes, k_high, k_low, out, halves)
    first[...] = probes[...]


def halo_place(right, blocks, links, length, n):
    own = jnp.where(right, blocks - 1 - links + n, links - n) * length
    halo = jnp.where(right, n, links - 1 - n) * length
    return pl.multiple_of(own, 128), pl.multiple_of(halo, 128)


def halo_product(right, received, k_high, k_low, out, halves, blocks, length):
    rows = out.shape[0]
    links = received.shape[1] // length
    for n in range(links):
        _, halo = halo_place(right, blocks, links, length, n)
        store_halves(halves, n * length, received[0:rows, pl.ds(halo, length)])
    row = 0
    for n in range(1, links + 1):
        depth = n * length
        own, _ = halo_place(right, blocks, links, length, n)
        value = multiply(halves, rows, depth, k_high[row : row + depth], k_low[row : row + depth])
        out[:, pl.ds(own, length)] = out[:, pl.ds(own, length)] + value
        row += depth


def store_sends(is_odd, out, to_mate, to_next):
    span = to_mate.shape[1]
    far = out.shape[1] - span
    to_mate[...] = out[:, pl.ds(pl.multiple_of(jnp.where(is_odd, 0, far), 128), span)]
    to_next[...] = out[:, pl.ds(pl.multiple_of(jnp.where(is_odd, far, 0), 128), span)]


def halo_first_kernel(odd, coords, pair, partial, received, k_high, k_low, out, *rest, mate):
    *sends, halves, columns, rows = rest
    links, blocks = pair.shape
    probe_count, here = out.shape
    length = here // blocks
    right = odd[0] == (0 if mate else 1)
    out[...] = partial[...]
    fill_rows(rows, coords)
    for h in range(links):
        _, halo = halo_place(right, blocks, links, length, h)
        fill_columns(columns, h * length, received[probe_count : probe_count + 8, pl.ds(halo, length)])
        lanes, flags, starts = [], [], []
        for n in range(h + 1, links + 1):
            own, _ = halo_place(right, blocks, links, length, n)
            lower = jnp.where(right, blocks - 1 - links + n, 0)
            k = links - n + h
            ours = jnp.full((1, 128), pair[k, lower].astype(F32), F32)
            theirs = received[probe_count + 3 + k : probe_count + 4 + k, pl.ds(halo, 128)]
            flag = jnp.broadcast_to(jnp.where(right, ours, theirs), (8, 128))
            for lane in range(0, length, 128):
                lanes.append(pl.multiple_of(own + lane, 128))
                flags.append(flag)
                starts.append(((n * (n - 1) // 2 + h) * length, lane))

        def store_to(start, lane, row):
            def store(top, rest):
                k_high[pl.ds(start + row, STRIP), lane : lane + 128] = top
                k_low[pl.ds(start + row, STRIP), lane : lane + 128] = rest

            return store

        def body(s, _):
            row = pl.multiple_of(s * STRIP, STRIP)
            stores = [store_to(start, lane, row) for start, lane in starts]
            fill_strip(columns, h * length + row, STRIP, rows, lanes, flags, stores)
            return 0

        lax.fori_loop(0, length // STRIP, body, 0)
    halo_product(right, received, k_high, k_low, out, halves, blocks, length)
    if sends:
        store_sends(odd[0] == 1, out, *sends)


def add_sums(table, terms):
    lane = lax.broadcasted_iota(jnp.int32, table.shape, 1)
    for power, left, right in terms:
        part = None
        for at in range(0, left.shape[1], 128):
            term = left[:, at : at + 128] * right[:, at : at + 128]
            part = term if part is None else part + term
        table = jnp.where(lane == power, jnp.sum(part, axis=1, keepdims=True), table)
    return table


def local_second_kernel(noise, first, second, k_high, k_low, out, table, halves):
    local_product(noise, second, k_high, k_low, out, halves)
    table[...] = add_sums(jnp.zeros(table.shape, F32), ((0, first, first), (1, first, second), (2, second, second)))


def local_third_kernel(noise, second, third, table_in, k_high, k_low, out, table, halves):
    local_product(noise, third, k_high, k_low, out, halves)
    table[...] = add_sums(table_in[...], ((3, second, third), (4, third, third)))


def halo_second_kernel(odd, partial, beyond, mate, mate_high, mate_low, next_high, next_low, out, to_mate, to_next, halves):
    out[...] = partial[...]
    links = mate.shape[1] // mate_high.shape[1]
    length = mate_high.shape[1]
    blocks = out.shape[1] // length
    halo_product(odd[0] == 0, mate, mate_high, mate_low, out, halves, blocks, length)
    halo_product(odd[0] == 1, beyond, next_high, next_low, out, halves, blocks, length)
    store_sends(odd[0] == 1, out, to_mate, to_next)


def halo_third_kernel(
    odd, partial, beyond, mate, mate_high, mate_low, next_high, next_low, third, table, out, sums, halves
):
    out[...] = partial[...]
    length = mate_high.shape[1]
    blocks = out.shape[1] // length
    halo_product(odd[0] == 0, mate, mate_high, mate_low, out, halves, blocks, length)
    halo_product(odd[0] == 1, beyond, next_high, next_low, out, halves, blocks, length)
    full = add_sums(table[...], ((5, third, out), (6, out, out)))
    turned = jnp.transpose(full)[0:8, :]
    compact = jnp.concatenate([turned[0:4], turned[4:8]], axis=1)
    sums[...] = jnp.broadcast_to(compact[None], sums.shape)


def polynomials(moment):
    def dot(p, q):
        total, size = 0.0, 0.0
        for i, x in enumerate(p):
            for j, y in enumerate(q):
                term = x * y * moment[i + j]
                total, size = total + term, size + jnp.abs(term)
        return total, size

    def add(p, q, factor):
        count = max(len(p), len(q))
        p, q = p + [0.0] * (count - len(p)), q + [0.0] * (count - len(q))
        return [x + factor * y for x, y in zip(p, q)]

    one = jnp.ones_like(moment[0])
    solution, residual, direction = [jnp.zeros_like(one)], [one], [one]
    norm = moment[0]
    good = norm > 0.0
    for step in range(ITERS):
        image = add([0.0 * one] + direction, direction, SHIFT)
        curvature, size = dot(direction, image)
        good = good & (size <= MAX_AMP * curvature)
        step_size = norm / curvature
        solution = add(solution, direction, step_size)
        residual = add(residual, image, -step_size)
        new, size = dot(residual, residual)
        if step < ITERS - 1:
            good = good & (size <= MAX_AMP * new)
            direction = add(residual, direction, new / norm)
        norm = new
    size = sum(jnp.abs(x) * jnp.sqrt(moment[2 * i]) for i, x in enumerate(residual))
    good = good & (size * size <= MAX_NORM * MAX_NORM * norm)
    return solution, residual, good


def finish_kernel(sums, first, second, third, fourth, solution, residual, good):
    total = jnp.sum(sums[...], axis=0)
    rows = first.shape[0]
    moment = [total[k : k + 1, 0:rows] for k in range(4)] + [total[k : k + 1, rows : 2 * rows] for k in range(3)]
    mix_solution, mix_residual, fine = polynomials(moment)
    table = jnp.concatenate(mix_solution + mix_residual + [jnp.zeros_like(moment[0])], axis=0)
    table = jnp.concatenate([table, jnp.zeros_like(table)], axis=1)
    table = jnp.transpose(jnp.concatenate([table, jnp.zeros((120, 128), F32)], axis=0))[0:rows]
    basis = (first[...], second[...], third[...], fourth[...])

    def mix(at, count):
        total = table[:, at : at + 1] * basis[0]
        for k in range(1, count):
            total = total + table[:, at + k : at + k + 1] * basis[k]
        return total

    solution[...] = mix(0, ITERS)
    residual[...] = mix(ITERS, ITERS + 1)
    good[0, 0] = jnp.min(jnp.where(fine, 1.0, 0.0))


VMEM = pl.BlockSpec(memory_space=pltpu.VMEM)
SMEM = pl.BlockSpec(memory_space=pltpu.SMEM)
ANY = pl.BlockSpec(memory_space=pl.ANY)


def call(kernel, name, out_shape, in_specs, scratch_shapes=(), out_specs=None):
    kwargs = {} if out_specs is None else {"out_specs": out_specs}
    return pl.pallas_call(
        kernel,
        out_shape=out_shape,
        in_specs=in_specs,
        scratch_shapes=scratch_shapes,
        compiler_params=pltpu.CompilerParams(vmem_limit_bytes=VMEM_LIMIT),
        name=name,
        **kwargs,
    )


def exchange(to_mate, to_next):
    count = lax.axis_size(AXES)
    beyond = [(i, i + 1 if i % 2 else i - 1) for i in range(1, count - 1)]
    mate = [(i, i ^ 1) for i in range(count)]
    to_mate = lax.ppermute(to_mate, AXES, mate)
    return lax.ppermute(to_next, AXES, beyond), to_mate


def per_device(coords, noise_var, pair_list, probes):
    rows, here = probes.shape
    links, blocks = pair_list.shape
    length = here // blocks
    span = links * length
    tiles = links * (links + 1) // 2
    noise = noise_var.reshape(1, here)
    odd = (lax.axis_index(AXES) % 2).reshape(1)

    whole = jax.ShapeDtypeStruct((rows, here), F32)
    part = jax.ShapeDtypeStruct((rows, span), F32)
    packed = jax.ShapeDtypeStruct((rows + 8, span), F32)
    sums_table = jax.ShapeDtypeStruct((rows, 128), F32)
    local_table = jax.ShapeDtypeStruct((blocks, here, length), BF16)
    halo_table = jax.ShapeDtypeStruct((tiles * length, length), BF16)
    local_halves = pltpu.VMEM((2 * rows, here), BF16)
    halo_halves = pltpu.VMEM((2 * rows, span), BF16)

    to_mate, to_next = call(
        pack_kernel, "pack", (packed, packed), [SMEM, VMEM, SMEM, ANY], [pltpu.SemaphoreType.DMA((2 * PACKS,))]
    )(odd, coords, pair_list, probes)
    beyond, mate = exchange(to_mate, to_next)
    k_high, k_low, partial, first = call(
        local_first_kernel,
        "local_first",
        (local_table, local_table, whole, whole),
        [VMEM, VMEM, SMEM, VMEM],
        [
            local_halves,
            pltpu.VMEM((3, here, 128), F32),
            pltpu.VMEM((3, 8, here), F32),
            pltpu.VMEM((blocks, 8, here), F32),
        ],
    )(coords, noise, pair_list, probes)
    halo_scratch = [halo_halves, pltpu.VMEM((3, span, 128), F32), pltpu.VMEM((3, 8, here), F32)]
    mate_high, mate_low, partial = call(
        functools.partial(halo_first_kernel, mate=True),
        "mate_first",
        (halo_table, halo_table, whole),
        [SMEM, VMEM, SMEM, VMEM, VMEM],
        halo_scratch,
    )(odd, coords, pair_list, partial, mate)
    next_high, next_low, second, to_mate, to_next = call(
        functools.partial(halo_first_kernel, mate=False),
        "next_first",
        (halo_table, halo_table, whole, part, part),
        [SMEM, VMEM, SMEM, VMEM, VMEM],
        halo_scratch,
    )(odd, coords, pair_list, partial, beyond)

    beyond, mate = exchange(to_mate, to_next)
    partial, table = call(local_second_kernel, "local_second", (whole, sums_table), [VMEM] * 5, [local_halves])(
        noise, first, second, k_high, k_low
    )
    third, to_mate, to_next = call(
        halo_second_kernel, "halo_second", (whole, part, part), [SMEM] + [VMEM] * 7, [halo_halves]
    )(odd, partial, beyond, mate, mate_high, mate_low, next_high, next_low)

    beyond, mate = exchange(to_mate, to_next)
    partial, table = call(local_third_kernel, "local_third", (whole, sums_table), [VMEM] * 6, [local_halves])(
        noise, second, third, table, k_high, k_low
    )
    regions, subs = lax.axis_size("region"), lax.axis_size("sub")
    fourth, sums = call(
        halo_third_kernel,
        "halo_third",
        (whole, jax.ShapeDtypeStruct((regions, 4, 128), F32)),
        [SMEM] + [VMEM] * 9,
        [halo_halves],
    )(odd, partial, beyond, mate, mate_high, mate_low, next_high, next_low, third, table)

    sums = jnp.sum(lax.all_to_all(sums, "region", 0, 0), axis=0)
    sums = lax.all_to_all(jnp.broadcast_to(sums[None], (subs, 4, 128)), "sub", 0, 0)
    solution, residual, good = call(
        finish_kernel,
        "finish",
        (whole, whole, jax.ShapeDtypeStruct((1, 1), F32)),
        [VMEM] * 5,
        out_specs=(VMEM, VMEM, SMEM),
    )(sums, first, second, third, fourth)

    def again(state):
        solution, residual = plain(coords, noise_var, pair_list, probes)
        return jnp.ones_like(state[0]), solution, residual

    _, solution, residual = lax.while_loop(lambda state: state[0][0, 0] < 0.5, again, (good, solution, residual))
    return solution, residual


def solution(mesh):
    in_specs = (P(None, AXES), P(AXES), P(None, AXES), P(None, AXES))
    out_specs = (P(None, AXES), P(None, AXES))
    return jax.shard_map(per_device, mesh=mesh, in_specs=in_specs, out_specs=out_specs, check_vma=False)
```

```python
import functools

import jax
import jax.numpy as jnp
from jax import lax
from jax.experimental import pallas as pl
from jax.experimental.pallas import tpu as pltpu
from jax.sharding import PartitionSpec as P

ITERS = 3
AXES = ("region", "sub")
SHIFT = 6.0
MAX_AMP = 100.0
MAX_NORM = 30.0
F32 = jnp.float32
BF16 = jnp.bfloat16
VMEM_LIMIT = 40 * 1024 * 1024


def shifted(array, by):
    count = lax.axis_size(AXES)
    pairs = [(i, i + by) for i in range(count) if 0 <= i + by < count]
    return lax.ppermute(array, AXES, pairs)


def wendland(left, right):
    squared = (left[0][..., :, None] - right[0][..., None, :]) ** 2
    squared = squared + (left[1][..., :, None] - right[1][..., None, :]) ** 2
    squared = squared + (left[2][..., :, None] - right[2][..., None, :]) ** 2
    distance = jnp.sqrt(squared)
    support = jnp.maximum(1.0 - distance, 0.0)
    return support**4 * (4.0 * distance + 1.0)


def squares(residual):
    return lax.psum(jnp.sum(residual * residual, axis=1), AXES)


def plain(coords, noise_var, pair_list, probes):
    probe_count, points_here = probes.shape
    links = pair_list.shape[0]
    blocks_here = pair_list.shape[1]
    block_len = points_here // blocks_here
    span_cols = links * block_len
    local_c = coords.reshape(3, blocks_here, block_len)
    weights = pair_list.astype(F32)
    ahead_c = shifted(coords[:, :span_cols], -1)
    ext_c = jnp.concatenate([local_c, ahead_c.reshape(3, links, block_len)], axis=1)

    def step(_, state):
        solution, residual, direction, res_norm = state
        ahead_v = shifted(direction[:, :span_cols], -1)
        ext_v = jnp.concatenate([direction, ahead_v], axis=1).reshape(probe_count, blocks_here + links, block_len)
        local_v = ext_v[:, :blocks_here]
        result = (noise_var[None, :] * direction).reshape(probe_count, blocks_here, block_len)
        spill = jnp.zeros((probe_count, blocks_here + links, block_len), F32)
        for offset in range(links + 1):
            kernel_block = wendland(local_c, ext_c[:, offset : offset + blocks_here])
            if offset > 0:
                kernel_block = kernel_block * weights[offset - 1][:, None, None]
            result = result + jnp.einsum(
                "pbj,bij->pbi", ext_v[:, offset : offset + blocks_here], kernel_block, precision=lax.Precision.HIGHEST
            )
            if offset > 0:
                spill = spill.at[:, offset : offset + blocks_here].add(
                    jnp.einsum("pbi,bij->pbj", local_v, kernel_block, precision=lax.Precision.HIGHEST)
                )
        result = result + spill[:, :blocks_here]
        result = result.at[:, :links].add(shifted(spill[:, blocks_here:], 1))
        product = result.reshape(probe_count, points_here)
        step_size = res_norm / lax.psum(jnp.sum(direction * product, axis=1), AXES)
        solution = solution + step_size[:, None] * direction
        residual = residual - step_size[:, None] * product
        next_norm = squares(residual)
        direction = residual + (next_norm / res_norm)[:, None] * direction
        return solution, residual, direction, next_norm

    state = (jnp.zeros_like(probes), probes, probes, squares(probes))
    solution, residual, _, _ = lax.fori_loop(0, ITERS, step, state)
    return solution, residual


def is_right(mate):
    return lax.axis_index("sub") % 2 == (0 if mate else 1)


def own_place(right, blocks, links, length, n):
    return pl.multiple_of(jnp.where(right, blocks - 1 - links + n, links - n) * length, 128)


def halo_place(right, links, length, h):
    return pl.multiple_of(jnp.where(right, h, links - 1 - h) * length, 128)


def send_place(right, here, span):
    return pl.multiple_of(jnp.where(right, here - span, 0), 128)


def split(value):
    high = value.astype(BF16)
    return high, (value - high.astype(F32)).astype(BF16)


def start_all(copies):
    for copy in copies:
        copy.start()
    return copies


def pack_kernel(coords, pair, probes, to_mate, to_next, points, flags, sem):
    links, blocks = pair.shape
    here = coords.shape[1]
    length = here // blocks
    rows, span = probes.shape[0], links * length
    place = [send_place(is_right(mate), here, span) for mate in (True, False)]
    copies = start_all(
        [
            pltpu.make_async_copy(pair, flags, sem.at[0]),
            pltpu.make_async_copy(coords, points, sem.at[1]),
            pltpu.make_async_copy(probes.at[:, pl.ds(place[0], span)], to_mate.at[0:rows], sem.at[2]),
            pltpu.make_async_copy(probes.at[:, pl.ds(place[1], span)], to_next.at[0:rows], sem.at[3]),
        ]
    )
    copies[0].wait()
    copies[1].wait()
    right = is_right(True)
    extra = [points[...]]
    for k in range(links):
        flag = [flags[k, b].astype(F32) for b in range(blocks)]
        extra.append(jnp.concatenate([jnp.full((1, length), f, F32) for f in flag], axis=1))
    extra = jnp.concatenate(extra + [jnp.zeros((8 - 3 - links, here), F32)], axis=0)
    low, high = extra[:, 0:span], extra[:, here - span :]
    to_mate[rows : rows + 8, :] = jnp.where(right, high, low)
    to_next[rows : rows + 8, :] = jnp.where(right, low, high)
    copies[2].wait()
    copies[3].wait()


def fill_columns(columns, at, block):
    turned = jnp.transpose(block)
    for d in range(3):
        columns[d, at : at + turned.shape[0], :] = jnp.broadcast_to(turned[:, d : d + 1], (turned.shape[0], 128))


def fill_strip(columns, from_row, strip, rows, lanes, flag, stores):
    column = [columns[d, pl.ds(from_row, strip), :].reshape(strip // 8, 8, 128) for d in range(3)]
    for lane, one_flag, store in zip(lanes, flag, stores):
        squared = None
        for d in range(3):
            away = column[d] - rows[d, :, lane : lane + 128][None]
            squared = away * away if squared is None else squared + away * away
        squared = jnp.maximum(squared, 1e-30)
        distance = squared * lax.rsqrt(squared)
        support = jnp.maximum(1.0 - distance, 0.0)
        support = support * support
        value = support * support * ((4.0 * one_flag)[None] * distance + one_flag[None])
        store(*split(value.reshape(strip, 128)))


def store_halves(halves, at, vector):
    rows, size = vector.shape
    top, rest = split(vector)
    halves[0:rows, at : at + size] = top
    halves[rows : 2 * rows, at : at + size] = rest


def multiply(both, k_high, k_low, turned=False):
    rows = both.shape[0] // 2
    dims = (((1,), (1 if turned else 0,)), ((), ()))
    most = lax.dot_general(both, k_high, dims, preferred_element_type=F32)
    rest = lax.dot_general(both[0:rows], k_low, dims, preferred_element_type=F32)
    return most[0:rows] + (most[rows : 2 * rows] + rest)


def local_product(noise, vector, k_high, k_low, out, halves):
    blocks, _, length = k_high.shape
    store_halves(halves, 0, vector[...])
    for i in range(blocks):
        at = slice(i * length, (i + 1) * length)
        value = multiply(halves[...], k_high[i], k_low[i])
        out[:, at] = value + (noise[:, at] - SHIFT) * vector[:, at]


def local_first_kernel(coords, noise, pair, probes, k_high, k_low, out, first, columns, halves, rows, flags, sem):
    links, blocks = pair.shape
    here = probes.shape[1]
    length = here // blocks
    copy = pltpu.make_async_copy(probes, first, sem.at[0])
    copy.start()
    for j in range(blocks):
        own = coords[:, j * length : (j + 1) * length]
        fill_columns(columns, j * length, jnp.concatenate([own, jnp.zeros((5, length), F32)], axis=0))
    for d in range(3):
        rows[d] = jnp.broadcast_to(coords[d : d + 1, :], rows.shape[1:])
    for j in range(blocks):
        for i in range(blocks):
            if i == j:
                flag = 1.0
            elif abs(i - j) <= links:
                flag = pair[abs(i - j) - 1, min(i, j)].astype(F32)
            else:
                flag = 0.0
            flags[j, :, i * length : (i + 1) * length] = jnp.full((8, length), flag, F32)
    strip = 32

    def store_to(i, row, lane):
        def store(top, rest):
            k_high[i, pl.ds(row, strip), lane : lane + 128] = top
            k_low[i, pl.ds(row, strip), lane : lane + 128] = rest

        return store

    def body(s, _):
        row = pl.multiple_of(s * strip, strip)
        block = s // (length // strip)
        lanes = list(range(0, here, 128))
        fill_strip(
            columns,
            row,
            strip,
            rows,
            lanes,
            [flags[block, :, lane : lane + 128] for lane in lanes],
            [store_to(lane // length, row, lane % length) for lane in lanes],
        )
        return 0

    lax.fori_loop(0, here // strip, body, 0)
    copy.wait()
    local_product(noise, first, k_high, k_low, out, halves)


def fill_halo(right, pair, received, columns, k_high, k_low, rows):
    links, blocks = pair.shape
    span = received.shape[1]
    length = span // links
    at = received.shape[0] - 8
    place = [pl.ds(halo_place(right, links, length, h), length) for h in range(links)]
    for h in range(links):
        for d in range(3):
            coord = received[at + d : at + d + 1, place[h]]
            rows[d, :, h * length : (h + 1) * length] = jnp.broadcast_to(coord, (8, length))
    for n in range(1, links + 1):
        own = own_place(right, blocks, links, length, n)
        lower = jnp.where(right, blocks - 1 - links + n, 0)
        flags = []
        for h in range(n):
            k = links - n + h
            ours = jnp.full((1, 128), pair[k, lower].astype(F32), F32)
            theirs = received[at + 3 + k : at + 4 + k, place[h]][:, 0:128]
            flags += [jnp.broadcast_to(jnp.where(right, ours, theirs), (8, 128))] * (length // 128)
        lanes = list(range(0, n * length, 128))
        strip = 32 if n > 2 else 64

        def store_to(row, lane):
            def store(top, rest):
                k_high[pl.ds(row, strip), lane : lane + 128] = top
                k_low[pl.ds(row, strip), lane : lane + 128] = rest

            return store

        def body(s, _):
            step = pl.multiple_of(s * strip, strip)
            stores = [store_to((n - 1) * length + step, lane) for lane in lanes]
            fill_strip(columns, pl.multiple_of(own + step, strip), strip, rows, lanes, flags, stores)
            return 0

        lax.fori_loop(0, length // strip, body, 0)


def halo_product(right, load, k_high, k_low, out, halves, blocks):
    span = k_high.shape[0]
    length = out.shape[1] // blocks
    links = span // length
    for h in range(links):
        store_halves(halves, h * length, load(pl.ds(halo_place(right, links, length, h), length)))
    for n in range(1, links + 1):
        deep, at = slice(0, n * length), slice((n - 1) * length, n * length)
        own = pl.ds(own_place(right, blocks, links, length, n), length)
        out[:, own] = out[:, own] + multiply(halves[:, deep], k_high[at, deep], k_low[at, deep], turned=True)


def own_product(right, vector, k_high, k_low, out, halves, blocks):
    span = out.shape[1]
    length = vector.shape[1] // blocks
    links = span // length
    for n in range(1, links + 1):
        own = pl.ds(own_place(right, blocks, links, length, n), length)
        store_halves(halves, (n - 1) * length, vector[:, own])
    for h in range(links):
        deep, at = slice(h * length, span), slice(h * length, (h + 1) * length)
        place = pl.ds(halo_place(right, links, length, h), length)
        out[:, place] = multiply(halves[:, deep], k_high[deep, at], k_low[deep, at])


def store_send(right, vector, send):
    here, span = vector.shape[1], send.shape[1]
    send[...] = vector[:, pl.ds(send_place(right, here, span), span)]


def mate_first_kernel(pair, partial, received, columns, k_high, k_low, out, to_next, halves, rows):
    probe_count = out.shape[0]
    right = is_right(True)
    fill_halo(right, pair, received, columns, k_high, k_low, rows)
    out[...] = partial[...]
    halo_product(right, lambda at: received[0:probe_count, at], k_high, k_low, out, halves, pair.shape[1])
    store_send(is_right(False), out, to_next)


def next_first_kernel(
    pair, partial, first, received, columns, k_high, k_low, out, given, to_mate, halves, rows
):
    probe_count = out.shape[0]
    right = is_right(False)
    fill_halo(right, pair, received, columns, k_high, k_low, rows)
    out[...] = partial[...]
    halo_product(right, lambda at: received[0:probe_count, at], k_high, k_low, out, halves, pair.shape[1])
    store_send(is_right(True), out, to_mate)
    own_product(right, first, k_high, k_low, given, halves, pair.shape[1])


def add_sums(table, terms):
    lane = lax.broadcasted_iota(jnp.int32, table.shape, 1)
    for power, left, right in terms:
        part = None
        for at in range(0, left.shape[1], 128):
            term = left[:, at : at + 128] * right[:, at : at + 128]
            part = term if part is None else part + term
        table = jnp.where(lane == power, jnp.sum(part, axis=1, keepdims=True), table)
    return table


def local_second_kernel(noise, first, second, k_high, k_low, out, table, halves):
    local_product(noise, second, k_high, k_low, out, halves)
    table[...] = add_sums(jnp.zeros(table.shape, F32), ((0, first, first), (1, first, second), (2, second, second)))


def local_third_kernel(noise, second, third, table_in, k_high, k_low, out, table, halves):
    local_product(noise, third, k_high, k_low, out, halves)
    table[...] = add_sums(table_in[...], ((3, second, third), (4, third, third)))


def halo_second_kernel(
    partial, beyond, given, mate, mate_high, mate_low, next_high, next_low, out, to_next, to_mate, halves, *, blocks
):
    out[...] = partial[...]
    halo_product(is_right(True), lambda at: mate[:, at], mate_high, mate_low, out, halves, blocks)
    halo_product(is_right(False), lambda at: beyond[:, at] + given[:, at], next_high, next_low, out, halves, blocks)
    store_send(is_right(False), out, to_next)
    store_send(is_right(True), out, to_mate)


def halo_third_kernel(
    partial, beyond, mate, mate_high, mate_low, next_high, next_low, third, table, out, sums, halves, *, blocks
):
    out[...] = partial[...]
    halo_product(is_right(True), lambda at: mate[:, at], mate_high, mate_low, out, halves, blocks)
    halo_product(is_right(False), lambda at: beyond[:, at], next_high, next_low, out, halves, blocks)
    full = add_sums(table[...], ((5, third, out), (6, out, out)))
    turned = jnp.transpose(full)[0:8, :]
    compact = jnp.concatenate([turned[0:4], turned[4:8]], axis=1)
    sums[...] = jnp.broadcast_to(compact[None], sums.shape)


def polynomials(moment):
    def dot(p, q):
        total, size = 0.0, 0.0
        for i, x in enumerate(p):
            for j, y in enumerate(q):
                term = x * y * moment[i + j]
                total, size = total + term, size + jnp.abs(term)
        return total, size

    def add(p, q, factor):
        count = max(len(p), len(q))
        p, q = p + [0.0] * (count - len(p)), q + [0.0] * (count - len(q))
        return [x + factor * y for x, y in zip(p, q)]

    one = jnp.ones_like(moment[0])
    solution, residual, direction = [jnp.zeros_like(one)], [one], [one]
    norm = moment[0]
    good = norm > 0.0
    for step in range(ITERS):
        image = add([0.0 * one] + direction, direction, SHIFT)
        curvature, size = dot(direction, image)
        good = good & (size <= MAX_AMP * curvature)
        step_size = norm / curvature
        solution = add(solution, direction, step_size)
        residual = add(residual, image, -step_size)
        new, size = dot(residual, residual)
        if step < ITERS - 1:
            good = good & (size <= MAX_AMP * new)
            direction = add(residual, direction, new / norm)
        norm = new
    size = sum(jnp.abs(x) * jnp.sqrt(moment[2 * i]) for i, x in enumerate(residual))
    good = good & (size * size <= MAX_NORM * MAX_NORM * norm)
    return solution, residual, good


def finish_kernel(sums, first, second, third, fourth, solution, residual, good):
    total = jnp.sum(sums[...], axis=0)
    rows = first.shape[0]
    moment = [total[k : k + 1, 0:rows] for k in range(4)] + [total[k : k + 1, rows : 2 * rows] for k in range(3)]
    mix_solution, mix_residual, fine = polynomials(moment)
    table = jnp.concatenate(mix_solution + mix_residual + [jnp.zeros_like(moment[0])], axis=0)
    table = jnp.concatenate([table, jnp.zeros_like(table)], axis=1)
    table = jnp.transpose(jnp.concatenate([table, jnp.zeros((120, 128), F32)], axis=0))[0:rows]
    basis = (first[...], second[...], third[...], fourth[...])

    def mix(at, count):
        total = table[:, at : at + 1] * basis[0]
        for k in range(1, count):
            total = total + table[:, at + k : at + k + 1] * basis[k]
        return total

    solution[...] = mix(0, ITERS)
    residual[...] = mix(ITERS, ITERS + 1)
    good[0, 0] = jnp.min(jnp.where(fine, 1.0, 0.0))


VMEM = pl.BlockSpec(memory_space=pltpu.VMEM)
SMEM = pl.BlockSpec(memory_space=pltpu.SMEM)
ANY = pl.BlockSpec(memory_space=pl.ANY)


def call(kernel, name, out_shape, in_specs, scratch_shapes=(), out_specs=None):
    kwargs = {} if out_specs is None else {"out_specs": out_specs}
    return pl.pallas_call(
        kernel,
        out_shape=out_shape,
        in_specs=in_specs,
        scratch_shapes=scratch_shapes,
        compiler_params=pltpu.CompilerParams(vmem_limit_bytes=VMEM_LIMIT),
        name=name,
        **kwargs,
    )


def swap_mate(array):
    return lax.ppermute(array, AXES, [(i, i ^ 1) for i in range(lax.axis_size(AXES))])


def swap_next(array):
    return lax.ppermute(array, AXES, [(i, i + 1 if i % 2 else i - 1) for i in range(1, lax.axis_size(AXES) - 1)])


def per_device(coords, noise_var, pair_list, probes):
    rows, here = probes.shape
    links, blocks = pair_list.shape
    length = here // blocks
    span = links * length
    noise = noise_var.reshape(1, here)

    whole = jax.ShapeDtypeStruct((rows, here), F32)
    part = jax.ShapeDtypeStruct((rows, span), F32)
    packed = jax.ShapeDtypeStruct((rows + 8, span), F32)
    sums_table = jax.ShapeDtypeStruct((rows, 128), F32)
    local_table = jax.ShapeDtypeStruct((blocks, here, length), BF16)
    halo_table = jax.ShapeDtypeStruct((span, span), BF16)
    local_halves = pltpu.VMEM((2 * rows, here), BF16)
    halo_halves = pltpu.VMEM((2 * rows, span), BF16)

    to_mate, to_next = call(
        pack_kernel,
        "pack",
        (packed, packed),
        [ANY, ANY, ANY],
        [pltpu.VMEM((3, here), F32), pltpu.SMEM((links, blocks), jnp.int32), pltpu.SemaphoreType.DMA((4,))],
    )(coords, pair_list, probes)
    mate, beyond = swap_mate(to_mate), swap_next(to_next)
    k_high, k_low, partial, first, columns = call(
        local_first_kernel,
        "local_first",
        (local_table, local_table, whole, whole, jax.ShapeDtypeStruct((3, here, 128), F32)),
        [VMEM, VMEM, SMEM, ANY],
        [
            local_halves,
            pltpu.VMEM((3, 8, here), F32),
            pltpu.VMEM((blocks, 8, here), F32),
            pltpu.SemaphoreType.DMA((1,)),
        ],
    )(coords, noise, pair_list, probes)
    halo_scratch = [halo_halves, pltpu.VMEM((3, 8, span), F32)]
    mate_high, mate_low, partial, to_next = call(
        mate_first_kernel, "mate_first", (halo_table, halo_table, whole, part), [SMEM, VMEM, VMEM, VMEM], halo_scratch
    )(pair_list, partial, mate, columns)
    ahead = swap_next(to_next)
    next_high, next_low, second, given, to_mate = call(
        next_first_kernel,
        "next_first",
        (halo_table, halo_table, whole, part, part),
        [SMEM, VMEM, VMEM, VMEM, VMEM],
        halo_scratch,
    )(pair_list, partial, first, beyond, columns)

    mate = swap_mate(to_mate)
    partial, table = call(local_second_kernel, "local_second", (whole, sums_table), [VMEM] * 5, [local_halves])(
        noise, first, second, k_high, k_low
    )
    third, to_next, to_mate = call(
        functools.partial(halo_second_kernel, blocks=blocks), "halo_second", (whole, part, part), [VMEM] * 8, [halo_halves]
    )(partial, ahead, given, mate, mate_high, mate_low, next_high, next_low)

    beyond, mate = swap_next(to_next), swap_mate(to_mate)
    partial, table = call(local_third_kernel, "local_third", (whole, sums_table), [VMEM] * 6, [local_halves])(
        noise, second, third, table, k_high, k_low
    )
    regions, subs = lax.axis_size("region"), lax.axis_size("sub")
    fourth, sums = call(
        functools.partial(halo_third_kernel, blocks=blocks),
        "halo_third",
        (whole, jax.ShapeDtypeStruct((regions, 4, 128), F32)),
        [VMEM] * 9,
        [halo_halves],
    )(partial, beyond, mate, mate_high, mate_low, next_high, next_low, third, table)

    sums = jnp.sum(lax.all_to_all(sums, "region", 0, 0), axis=0)
    sums = lax.all_to_all(jnp.broadcast_to(sums[None], (subs, 4, 128)), "sub", 0, 0)
    solution, residual, good = call(
        finish_kernel,
        "finish",
        (whole, whole, jax.ShapeDtypeStruct((1, 1), F32)),
        [VMEM] * 5,
        out_specs=(VMEM, VMEM, SMEM),
    )(sums, first, second, third, fourth)

    def again(state):
        solution, residual = plain(coords, noise_var, pair_list, probes)
        return jnp.ones_like(state[0]), solution, residual

    _, solution, residual = lax.while_loop(lambda state: state[0][0, 0] < 0.5, again, (good, solution, residual))
    return solution, residual


def solution(mesh):
    in_specs = (P(None, AXES), P(AXES), P(None, AXES), P(None, AXES))
    out_specs = (P(None, AXES), P(None, AXES))
    return jax.shard_map(per_device, mesh=mesh, in_specs=in_specs, out_specs=out_specs, check_vma=False)
```

```python
import functools

import jax
import jax.numpy as jnp
from jax import lax
from jax.experimental import pallas as pl
from jax.experimental.pallas import tpu as pltpu
from jax.sharding import PartitionSpec as P

ITERS = 3
AXES = ("region", "sub")
SHIFT = 6.0
SCALE = 1.0 / 256.0
FAR = 65536.0
MAX_AMP = 100.0
MAX_NORM = 30.0
F32 = jnp.float32
BF16 = jnp.bfloat16
VMEM_LIMIT = 40 * 1024 * 1024


def shifted(array, by):
    count = lax.axis_size(AXES)
    pairs = [(i, i + by) for i in range(count) if 0 <= i + by < count]
    return lax.ppermute(array, AXES, pairs)


def wendland(left, right):
    squared = (left[0][..., :, None] - right[0][..., None, :]) ** 2
    squared = squared + (left[1][..., :, None] - right[1][..., None, :]) ** 2
    squared = squared + (left[2][..., :, None] - right[2][..., None, :]) ** 2
    distance = jnp.sqrt(squared)
    support = jnp.maximum(1.0 - distance, 0.0)
    return support**4 * (4.0 * distance + 1.0)


def squares(residual):
    return lax.psum(jnp.sum(residual * residual, axis=1), AXES)


def plain(coords, noise_var, pair_list, probes):
    probe_count, points_here = probes.shape
    links = pair_list.shape[0]
    blocks_here = pair_list.shape[1]
    block_len = points_here // blocks_here
    span_cols = links * block_len
    local_c = coords.reshape(3, blocks_here, block_len)
    weights = pair_list.astype(F32)
    ahead_c = shifted(coords[:, :span_cols], -1)
    ext_c = jnp.concatenate([local_c, ahead_c.reshape(3, links, block_len)], axis=1)

    def step(_, state):
        solution, residual, direction, res_norm = state
        ahead_v = shifted(direction[:, :span_cols], -1)
        ext_v = jnp.concatenate([direction, ahead_v], axis=1).reshape(probe_count, blocks_here + links, block_len)
        local_v = ext_v[:, :blocks_here]
        result = (noise_var[None, :] * direction).reshape(probe_count, blocks_here, block_len)
        spill = jnp.zeros((probe_count, blocks_here + links, block_len), F32)
        for offset in range(links + 1):
            kernel_block = wendland(local_c, ext_c[:, offset : offset + blocks_here])
            if offset > 0:
                kernel_block = kernel_block * weights[offset - 1][:, None, None]
            result = result + jnp.einsum(
                "pbj,bij->pbi", ext_v[:, offset : offset + blocks_here], kernel_block, precision=lax.Precision.HIGHEST
            )
            if offset > 0:
                spill = spill.at[:, offset : offset + blocks_here].add(
                    jnp.einsum("pbi,bij->pbj", local_v, kernel_block, precision=lax.Precision.HIGHEST)
                )
        result = result + spill[:, :blocks_here]
        result = result.at[:, :links].add(shifted(spill[:, blocks_here:], 1))
        product = result.reshape(probe_count, points_here)
        step_size = res_norm / lax.psum(jnp.sum(direction * product, axis=1), AXES)
        solution = solution + step_size[:, None] * direction
        residual = residual - step_size[:, None] * product
        next_norm = squares(residual)
        direction = residual + (next_norm / res_norm)[:, None] * direction
        return solution, residual, direction, next_norm

    state = (jnp.zeros_like(probes), probes, probes, squares(probes))
    solution, residual, _, _ = lax.fori_loop(0, ITERS, step, state)
    return solution, residual


def is_right(mate):
    return lax.axis_index("sub") % 2 == (0 if mate else 1)


def own_place(right, blocks, links, length, n):
    return pl.multiple_of(jnp.where(right, blocks - 1 - links + n, links - n) * length, 128)


def halo_place(right, links, length, h):
    return pl.multiple_of(jnp.where(right, h, links - 1 - h) * length, 128)


def send_place(right, here, span):
    return pl.multiple_of(jnp.where(right, here - span, 0), 128)


def split(value):
    high = value.astype(BF16)
    return high, (value - high.astype(F32)).astype(BF16)


def start_all(copies):
    for copy in copies:
        copy.start()
    return copies


def pack_kernel(coords, pair, probes, to_mate, to_next, own, points, flags, sem):
    links, blocks = pair.shape
    here = coords.shape[1]
    length = here // blocks
    rows, span = probes.shape[0], links * length
    place = [send_place(is_right(mate), here, span) for mate in (True, False)]
    copies = start_all(
        [
            pltpu.make_async_copy(pair, flags, sem.at[0]),
            pltpu.make_async_copy(coords, points, sem.at[1]),
            pltpu.make_async_copy(probes.at[:, pl.ds(place[0], span)], to_mate.at[0:rows], sem.at[2]),
            pltpu.make_async_copy(probes.at[:, pl.ds(place[1], span)], to_next.at[0:rows], sem.at[3]),
        ]
    )
    copies[0].wait()
    copies[1].wait()
    right = is_right(True)
    extra = [points[...]]
    for k in range(links):
        flag = [flags[k, b].astype(F32) for b in range(blocks)]
        extra.append(jnp.concatenate([jnp.full((1, length), f, F32) for f in flag], axis=1))
    extra = jnp.concatenate(extra + [jnp.zeros((8 - 3 - links, here), F32)], axis=0)
    own[...] = extra
    low, high = extra[:, 0:span], extra[:, here - span :]
    to_mate[rows : rows + 8, :] = jnp.where(right, high, low)
    to_next[rows : rows + 8, :] = jnp.where(right, low, high)
    copies[2].wait()
    copies[3].wait()


def fill_columns(columns, at, block):
    turned = jnp.transpose(block)
    for d in range(3):
        columns[d, at : at + turned.shape[0], :] = jnp.broadcast_to(turned[:, d : d + 1], (turned.shape[0], 128))


def fill_tiles(k_high, k_low, to_row, columns, from_row, count, rows, at, first):
    strip = 64 if at.stop - at.start <= 4 * 128 else 32

    def body(s, _):
        step = pl.multiple_of(s * strip, strip)
        column = [columns[d, pl.ds(from_row + step, strip), :].reshape(strip // 8, 8, 128) for d in range(3)]
        for lane in range(at.start, at.stop, 128):
            squared = None
            for d in range(3):
                away = column[d] - rows[d, :, lane : lane + 128][None]
                squared = away * away if squared is None else squared + away * away
            squared = jnp.maximum(squared, 1e-30)
            distance = squared * lax.rsqrt(squared)
            support = jnp.maximum(4.0 - distance, 0.0)
            support = support * support
            value = support * support * (distance + 1.0)
            top, rest = split(value.reshape(strip, 128))
            to = slice(first + lane - at.start, first + lane - at.start + 128)
            k_high[pl.ds(to_row + step, strip), to] = top
            k_low[pl.ds(to_row + step, strip), to] = rest
        return 0

    lax.fori_loop(0, count // strip, body, 0)


def store_halves(halves, at, vector):
    rows, size = vector.shape
    top, rest = split(vector * SCALE)
    halves[0:rows, at : at + size] = top
    halves[rows : 2 * rows, at : at + size] = rest


def multiply(both, k_high, k_low, turned=False):
    rows = both.shape[0] // 2
    dims = (((1,), (1 if turned else 0,)), ((), ()))
    most = lax.dot_general(both, k_high, dims, preferred_element_type=F32)
    rest = lax.dot_general(both[0:rows], k_low, dims, preferred_element_type=F32)
    return most[0:rows] + (most[rows : 2 * rows] + rest)


def local_product(noise, vector, k_high, k_low, out, halves, length):
    here = vector.shape[1]
    store_halves(halves, 0, vector[...])
    for start in range(0, here, length):
        stop = start + length
        at, before, after = slice(start, stop), slice(0, stop), slice(stop, here)
        value = multiply(halves[:, before], k_high[before, at], k_low[before, at])
        if stop < here:
            value = value + multiply(halves[:, after], k_high[at, after], k_low[at, after], turned=True)
        out[:, at] = value + (noise[:, at] - SHIFT) * vector[:, at]


def local_first_kernel(own, noise, probes, k_high, k_low, out, first, columns, halves, rows, sem, *, links):
    here = own.shape[1]
    blocks = links + 1
    length = here // blocks
    copy = pltpu.make_async_copy(probes, first, sem.at[0])
    copy.start()
    for j in range(blocks):
        fill_columns(columns, j * length, 4.0 * own[:, j * length : (j + 1) * length])
    for d in range(1, 3):
        rows[d] = jnp.broadcast_to(4.0 * own[d : d + 1, :], rows.shape[1:])
    for i in range(blocks):
        for j in range(i, blocks):
            at = slice(j * length, (j + 1) * length)
            moved = 4.0 * own[0:1, at]
            if j > i:
                flag = own[2 + j - i : 3 + j - i, i * length : (i + 1) * length]
                moved = jnp.where(flag == 1.0, moved, moved + FAR)
            rows[0, :, at] = jnp.broadcast_to(moved, (8, length))
        fill_tiles(k_high, k_low, i * length, columns, i * length, length, rows, slice(i * length, here), i * length)
    copy.wait()
    local_product(noise, first, k_high, k_low, out, halves, length)


def fill_halo(right, own, received, columns, tables, rows, links):
    length = received.shape[1] // links
    blocks = own.shape[1] // length
    at = received.shape[0] - 8
    place = [pl.ds(halo_place(right, links, length, h), length) for h in range(links)]
    for h in range(max(tables)):
        for d in range(1, 3):
            coord = 4.0 * received[at + d : at + d + 1, place[h]]
            rows[d, :, h * length : (h + 1) * length] = jnp.broadcast_to(coord, (8, length))
    for n, (k_high, k_low) in tables.items():
        mine = own_place(right, blocks, links, length, n)
        for h in range(n):
            k = links - n + h
            ours = own[3 + k : 4 + k, pl.ds(mine, length)]
            theirs = received[at + 3 + k : at + 4 + k, place[h]]
            coord = 4.0 * received[at : at + 1, place[h]]
            coord = jnp.where(jnp.where(right, ours, theirs) == 1.0, coord, coord + FAR)
            rows[0, :, h * length : (h + 1) * length] = jnp.broadcast_to(coord, (8, length))
        fill_tiles(k_high, k_low, 0, columns, mine, length, rows, slice(0, n * length), 0)


def table_rows(k_high, k_low, ns, length):
    parts = {n: (pl.ds((n - ns[0]) * length, length), slice(0, n * length)) for n in ns}
    return {n: (k_high.at[part], k_low.at[part]) for n, part in parts.items()}


def halo_product(right, load, tables, out, halves, links):
    length = halves.shape[1] // links
    blocks = out.shape[1] // length
    for h in range(max(tables)):
        store_halves(halves, h * length, load(pl.ds(halo_place(right, links, length, h), length)))
    for n, (k_high, k_low) in tables.items():
        own = pl.ds(own_place(right, blocks, links, length, n), length)
        out[:, own] = out[:, own] + multiply(halves[:, 0 : n * length], k_high[...], k_low[...], turned=True)


def own_product(right, vector, k_high, k_low, out, halves, blocks):
    span = out.shape[1]
    length = vector.shape[1] // blocks
    links = span // length
    for n in range(1, links + 1):
        own = pl.ds(own_place(right, blocks, links, length, n), length)
        store_halves(halves, (n - 1) * length, vector[:, own])
    for h in range(links):
        deep, at = slice(h * length, span), slice(h * length, (h + 1) * length)
        place = pl.ds(halo_place(right, links, length, h), length)
        out[:, place] = multiply(halves[:, deep], k_high[deep, at], k_low[deep, at])


def store_send(right, vector, send):
    here, span = vector.shape[1], send.shape[1]
    send[...] = vector[:, pl.ds(send_place(right, here, span), span)]


def mate_first_kernel(own, partial, received, columns, k_high, k_low, out, to_next, halves, rows, *, links):
    probe_count = out.shape[0]
    right = is_right(True)
    length = halves.shape[1] // links
    tables = table_rows(k_high, k_low, range(1, links), length)
    fill_halo(right, own, received, columns, tables, rows, links)
    out[...] = partial[...]
    halo_product(right, lambda at: received[0:probe_count, at], tables, out, halves, links)
    store_send(is_right(False), out, to_next)


def next_first_kernel(
    own, partial, first, mate, received, columns, mate_high, mate_low, k_high, k_low, out, given, to_mate, halves, rows, *, links
):
    probe_count = out.shape[0]
    length = halves.shape[1] // links
    out[...] = partial[...]
    right = is_right(True)
    tables = table_rows(mate_high, mate_low, range(links, links + 1), length)
    fill_halo(right, own, mate, columns, tables, rows, links)
    halo_product(right, lambda at: mate[0:probe_count, at], tables, out, halves, links)
    right = is_right(False)
    tables = table_rows(k_high, k_low, range(1, links + 1), length)
    fill_halo(right, own, received, columns, tables, rows, links)
    halo_product(right, lambda at: received[0:probe_count, at], tables, out, halves, links)
    store_send(is_right(True), out, to_mate)
    own_product(right, first, k_high, k_low, given, halves, links + 1)


def add_sums(table, terms):
    lane = lax.broadcasted_iota(jnp.int32, table.shape, 1)
    for power, left, right in terms:
        part = None
        for at in range(0, left.shape[1], 128):
            term = left[:, at : at + 128] * right[:, at : at + 128]
            part = term if part is None else part + term
        table = jnp.where(lane == power, jnp.sum(part, axis=1, keepdims=True), table)
    return table


def local_second_kernel(noise, first, second, k_high, k_low, out, table, halves, *, length):
    local_product(noise, second, k_high, k_low, out, halves, length)
    table[...] = add_sums(jnp.zeros(table.shape, F32), ((0, first, first), (1, first, second), (2, second, second)))


def local_third_kernel(noise, second, third, table_in, k_high, k_low, out, table, halves, *, length):
    local_product(noise, third, k_high, k_low, out, halves, length)
    table[...] = add_sums(table_in[...], ((3, second, third), (4, third, third)))


def both_products(partial, beyond, mate, tables, out, halves, links):
    length = halves.shape[1] // links
    out[...] = partial[...]
    mate_tables = table_rows(*tables[0:2], range(1, links), length)
    mate_tables.update(table_rows(*tables[2:4], range(links, links + 1), length))
    halo_product(is_right(True), lambda at: mate[:, at], mate_tables, out, halves, links)
    halo_product(is_right(False), beyond, table_rows(*tables[4:6], range(1, links + 1), length), out, halves, links)


def halo_second_kernel(partial, beyond, given, mate, *rest, links):
    tables, (out, to_next, to_mate, halves) = rest[0:6], rest[6:]
    both_products(partial, lambda at: beyond[:, at] + given[:, at], mate, tables, out, halves, links)
    store_send(is_right(False), out, to_next)
    store_send(is_right(True), out, to_mate)


def halo_third_kernel(partial, beyond, mate, *rest, links):
    tables, (third, table, out, sums, halves) = rest[0:6], rest[6:]
    both_products(partial, lambda at: beyond[:, at], mate, tables, out, halves, links)
    full = add_sums(table[...], ((5, third, out), (6, out, out)))
    turned = jnp.transpose(full)[0:8, :]
    compact = jnp.concatenate([turned[0:4], turned[4:8]], axis=1)
    sums[...] = jnp.broadcast_to(compact[None], sums.shape)


def polynomials(moment):
    def dot(p, q):
        total, size = 0.0, 0.0
        for i, x in enumerate(p):
            for j, y in enumerate(q):
                term = x * y * moment[i + j]
                total, size = total + term, size + jnp.abs(term)
        return total, size

    def add(p, q, factor):
        count = max(len(p), len(q))
        p, q = p + [0.0] * (count - len(p)), q + [0.0] * (count - len(q))
        return [x + factor * y for x, y in zip(p, q)]

    one = jnp.ones_like(moment[0])
    solution, residual, direction = [jnp.zeros_like(one)], [one], [one]
    norm = moment[0]
    good = norm > 0.0
    for step in range(ITERS):
        image = add([0.0 * one] + direction, direction, SHIFT)
        curvature, size = dot(direction, image)
        good = good & (size <= MAX_AMP * curvature)
        step_size = norm / curvature
        solution = add(solution, direction, step_size)
        residual = add(residual, image, -step_size)
        new, size = dot(residual, residual)
        if step < ITERS - 1:
            good = good & (size <= MAX_AMP * new)
            direction = add(residual, direction, new / norm)
        norm = new
    size = sum(jnp.abs(x) * jnp.sqrt(moment[2 * i]) for i, x in enumerate(residual))
    good = good & (size * size <= MAX_NORM * MAX_NORM * norm)
    return solution, residual, good


def finish_kernel(sums, first, second, third, fourth, solution, residual, good):
    total = jnp.sum(sums[...], axis=0)
    rows = first.shape[0]
    moment = [total[k : k + 1, 0:rows] for k in range(4)] + [total[k : k + 1, rows : 2 * rows] for k in range(3)]
    mix_solution, mix_residual, fine = polynomials(moment)
    table = jnp.concatenate(mix_solution + mix_residual + [jnp.zeros_like(moment[0])], axis=0)
    table = jnp.concatenate([table, jnp.zeros_like(table)], axis=1)
    table = jnp.transpose(jnp.concatenate([table, jnp.zeros((120, 128), F32)], axis=0))[0:rows]
    basis = (first[...], second[...], third[...], fourth[...])

    def mix(at, count):
        total = table[:, at : at + 1] * basis[0]
        for k in range(1, count):
            total = total + table[:, at + k : at + k + 1] * basis[k]
        return total

    solution[...] = mix(0, ITERS)
    residual[...] = mix(ITERS, ITERS + 1)
    good[0, 0] = jnp.min(jnp.where(fine, 1.0, 0.0))


VMEM = pl.BlockSpec(memory_space=pltpu.VMEM)
SMEM = pl.BlockSpec(memory_space=pltpu.SMEM)
ANY = pl.BlockSpec(memory_space=pl.ANY)


def call(kernel, name, out_shape, in_specs, scratch_shapes=(), out_specs=None):
    kwargs = {} if out_specs is None else {"out_specs": out_specs}
    return pl.pallas_call(
        kernel,
        out_shape=out_shape,
        in_specs=in_specs,
        scratch_shapes=scratch_shapes,
        compiler_params=pltpu.CompilerParams(vmem_limit_bytes=VMEM_LIMIT),
        name=name,
        **kwargs,
    )


def swap_mate(array):
    return lax.ppermute(array, AXES, [(i, i ^ 1) for i in range(lax.axis_size(AXES))])


def swap_next(array):
    return lax.ppermute(array, AXES, [(i, i + 1 if i % 2 else i - 1) for i in range(1, lax.axis_size(AXES) - 1)])


def per_device(coords, noise_var, pair_list, probes):
    rows, here = probes.shape
    links, blocks = pair_list.shape
    length = here // blocks
    span = links * length
    noise = noise_var.reshape(1, here)

    whole = jax.ShapeDtypeStruct((rows, here), F32)
    part = jax.ShapeDtypeStruct((rows, span), F32)
    packed = jax.ShapeDtypeStruct((rows + 8, span), F32)
    sums_table = jax.ShapeDtypeStruct((rows, 128), F32)
    local_table = jax.ShapeDtypeStruct((here, here), BF16)
    halo_table = jax.ShapeDtypeStruct((span, span), BF16)
    local_halves = pltpu.VMEM((2 * rows, here), BF16)
    halo_halves = pltpu.VMEM((2 * rows, span), BF16)

    to_mate, to_next, own = call(
        pack_kernel,
        "pack",
        (packed, packed, jax.ShapeDtypeStruct((8, here), F32)),
        [ANY, ANY, ANY],
        [pltpu.VMEM((3, here), F32), pltpu.SMEM((links, blocks), jnp.int32), pltpu.SemaphoreType.DMA((4,))],
    )(coords, pair_list, probes)
    mate, beyond = swap_mate(to_mate), swap_next(to_next)
    k_high, k_low, partial, first, columns = call(
        functools.partial(local_first_kernel, links=links),
        "local_first",
        (local_table, local_table, whole, whole, jax.ShapeDtypeStruct((3, here, 128), F32)),
        [VMEM, VMEM, ANY],
        [
            local_halves,
            pltpu.VMEM((3, 8, here), F32),
            pltpu.SemaphoreType.DMA((1,)),
        ],
    )(own, noise, probes)
    halo_scratch = [halo_halves, pltpu.VMEM((3, 8, span), F32)]
    early_table = jax.ShapeDtypeStruct((span - length, span - length), BF16)
    late_table = jax.ShapeDtypeStruct((length, span), BF16)
    early_high, early_low, partial, to_next = call(
        functools.partial(mate_first_kernel, links=links),
        "mate_first",
        (early_table, early_table, whole, part),
        [VMEM] * 4,
        halo_scratch,
    )(own, partial, mate, columns)
    ahead = swap_next(to_next)
    late_high, late_low, next_high, next_low, second, given, to_mate = call(
        functools.partial(next_first_kernel, links=links),
        "next_first",
        (late_table, late_table, halo_table, halo_table, whole, part, part),
        [VMEM] * 6,
        halo_scratch,
    )(own, partial, first, mate, beyond, columns)
    tables = (early_high, early_low, late_high, late_low, next_high, next_low)

    mate = swap_mate(to_mate)
    partial, table = call(
        functools.partial(local_second_kernel, length=length), "local_second", (whole, sums_table), [VMEM] * 5, [local_halves]
    )(noise, first, second, k_high, k_low)
    third, to_next, to_mate = call(
        functools.partial(halo_second_kernel, links=links), "halo_second", (whole, part, part), [VMEM] * 10, [halo_halves]
    )(partial, ahead, given, mate, *tables)

    beyond, mate = swap_next(to_next), swap_mate(to_mate)
    partial, table = call(
        functools.partial(local_third_kernel, length=length), "local_third", (whole, sums_table), [VMEM] * 6, [local_halves]
    )(noise, second, third, table, k_high, k_low)
    regions, subs = lax.axis_size("region"), lax.axis_size("sub")
    fourth, sums = call(
        functools.partial(halo_third_kernel, links=links),
        "halo_third",
        (whole, jax.ShapeDtypeStruct((regions, 4, 128), F32)),
        [VMEM] * 11,
        [halo_halves],
    )(partial, beyond, mate, *tables, third, table)

    sums = jnp.sum(lax.all_to_all(sums, "region", 0, 0), axis=0)
    sums = lax.all_to_all(jnp.broadcast_to(sums[None], (subs, 4, 128)), "sub", 0, 0)
    solution, residual, good = call(
        finish_kernel,
        "finish",
        (whole, whole, jax.ShapeDtypeStruct((1, 1), F32)),
        [VMEM] * 5,
        out_specs=(VMEM, VMEM, SMEM),
    )(sums, first, second, third, fourth)

    def again(state):
        solution, residual = plain(coords, noise_var, pair_list, probes)
        return jnp.ones_like(state[0]), solution, residual

    _, solution, residual = lax.while_loop(lambda state: state[0][0, 0] < 0.5, again, (good, solution, residual))
    return solution, residual


def solution(mesh):
    in_specs = (P(None, AXES), P(AXES), P(None, AXES), P(None, AXES))
    out_specs = (P(None, AXES), P(None, AXES))
    return jax.shard_map(per_device, mesh=mesh, in_specs=in_specs, out_specs=out_specs, check_vma=False)
```

```python
import functools

import jax
import jax.numpy as jnp
from jax import lax
from jax.experimental import pallas as pl
from jax.experimental.pallas import tpu as pltpu
from jax.sharding import PartitionSpec as P

ITERS = 3
AXES = ("region", "sub")
SHIFT = 6.0
SCALE = 1.0 / 256.0
FAR = 65536.0
MAX_AMP = 100.0
MAX_NORM = 30.0
F32 = jnp.float32
BF16 = jnp.bfloat16
VMEM_LIMIT = 40 * 1024 * 1024


def shifted(array, by):
    count = lax.axis_size(AXES)
    pairs = [(i, i + by) for i in range(count) if 0 <= i + by < count]
    return lax.ppermute(array, AXES, pairs)


def wendland(left, right):
    squared = (left[0][..., :, None] - right[0][..., None, :]) ** 2
    squared = squared + (left[1][..., :, None] - right[1][..., None, :]) ** 2
    squared = squared + (left[2][..., :, None] - right[2][..., None, :]) ** 2
    distance = jnp.sqrt(squared)
    support = jnp.maximum(1.0 - distance, 0.0)
    return support**4 * (4.0 * distance + 1.0)


def squares(residual):
    return lax.psum(jnp.sum(residual * residual, axis=1), AXES)


def plain(coords, noise_var, pair_list, probes):
    probe_count, points_here = probes.shape
    links = pair_list.shape[0]
    blocks_here = pair_list.shape[1]
    block_len = points_here // blocks_here
    span_cols = links * block_len
    local_c = coords.reshape(3, blocks_here, block_len)
    weights = pair_list.astype(F32)
    ahead_c = shifted(coords[:, :span_cols], -1)
    ext_c = jnp.concatenate([local_c, ahead_c.reshape(3, links, block_len)], axis=1)

    def step(_, state):
        solution, residual, direction, res_norm = state
        ahead_v = shifted(direction[:, :span_cols], -1)
        ext_v = jnp.concatenate([direction, ahead_v], axis=1).reshape(probe_count, blocks_here + links, block_len)
        local_v = ext_v[:, :blocks_here]
        result = (noise_var[None, :] * direction).reshape(probe_count, blocks_here, block_len)
        spill = jnp.zeros((probe_count, blocks_here + links, block_len), F32)
        for offset in range(links + 1):
            kernel_block = wendland(local_c, ext_c[:, offset : offset + blocks_here])
            if offset > 0:
                kernel_block = kernel_block * weights[offset - 1][:, None, None]
            result = result + jnp.einsum(
                "pbj,bij->pbi", ext_v[:, offset : offset + blocks_here], kernel_block, precision=lax.Precision.HIGHEST
            )
            if offset > 0:
                spill = spill.at[:, offset : offset + blocks_here].add(
                    jnp.einsum("pbi,bij->pbj", local_v, kernel_block, precision=lax.Precision.HIGHEST)
                )
        result = result + spill[:, :blocks_here]
        result = result.at[:, :links].add(shifted(spill[:, blocks_here:], 1))
        product = result.reshape(probe_count, points_here)
        step_size = res_norm / lax.psum(jnp.sum(direction * product, axis=1), AXES)
        solution = solution + step_size[:, None] * direction
        residual = residual - step_size[:, None] * product
        next_norm = squares(residual)
        direction = residual + (next_norm / res_norm)[:, None] * direction
        return solution, residual, direction, next_norm

    state = (jnp.zeros_like(probes), probes, probes, squares(probes))
    solution, residual, _, _ = lax.fori_loop(0, ITERS, step, state)
    return solution, residual


def is_right(mate):
    return lax.axis_index("sub") % 2 == (0 if mate else 1)


def own_place(right, blocks, links, length, n):
    return pl.multiple_of(jnp.where(right, blocks - 1 - links + n, links - n) * length, 128)


def halo_place(right, links, length, h):
    return pl.multiple_of(jnp.where(right, h, links - 1 - h) * length, 128)


def send_place(right, here, span):
    return pl.multiple_of(jnp.where(right, here - span, 0), 128)


def split(value):
    high = value.astype(BF16)
    return high, (value - high.astype(F32)).astype(BF16)


def start_all(copies):
    for copy in copies:
        copy.start()
    return copies


def pack_kernel(coords, pair, probes, to_mate, to_next, own, points, flags, sem):
    links, blocks = pair.shape
    here = coords.shape[1]
    length = here // blocks
    rows, span = probes.shape[0], links * length
    place = [send_place(is_right(mate), here, span) for mate in (True, False)]
    copies = start_all(
        [
            pltpu.make_async_copy(pair, flags, sem.at[0]),
            pltpu.make_async_copy(coords, points, sem.at[1]),
            pltpu.make_async_copy(probes.at[:, pl.ds(place[0], span)], to_mate.at[0:rows], sem.at[2]),
            pltpu.make_async_copy(probes.at[:, pl.ds(place[1], span)], to_next.at[0:rows], sem.at[3]),
        ]
    )
    copies[0].wait()
    copies[1].wait()
    right = is_right(True)
    extra = [points[...]]
    for k in range(links):
        flag = [flags[k, b].astype(F32) for b in range(blocks)]
        extra.append(jnp.concatenate([jnp.full((1, length), f, F32) for f in flag], axis=1))
    extra = jnp.concatenate(extra + [jnp.zeros((8 - 3 - links, here), F32)], axis=0)
    own[...] = extra
    low, high = extra[:, 0:span], extra[:, here - span :]
    to_mate[rows : rows + 8, :] = jnp.where(right, high, low)
    to_next[rows : rows + 8, :] = jnp.where(right, low, high)
    copies[2].wait()
    copies[3].wait()


def fill_columns(columns, at, block):
    turned = jnp.transpose(block)
    for d in range(3):
        columns[d, at : at + turned.shape[0], :] = jnp.broadcast_to(turned[:, d : d + 1], (turned.shape[0], 128))


def fill_tiles(k_high, k_low, to_row, columns, from_row, count, rows, at, first):
    strip = 64 if at.stop - at.start <= 4 * 128 else 32

    def body(s, _):
        step = pl.multiple_of(s * strip, strip)
        column = [columns[d, pl.ds(from_row + step, strip), :].reshape(strip // 8, 8, 128) for d in range(3)]
        for lane in range(at.start, at.stop, 128):
            squared = None
            for d in range(3):
                away = column[d] - rows[d, :, lane : lane + 128][None]
                squared = away * away if squared is None else squared + away * away
            squared = jnp.maximum(squared, 1e-30)
            distance = squared * lax.rsqrt(squared)
            support = jnp.maximum(4.0 - distance, 0.0)
            support = support * support
            value = support * support * (distance + 1.0)
            top, rest = split(value.reshape(strip, 128))
            to = slice(first + lane - at.start, first + lane - at.start + 128)
            k_high[pl.ds(to_row + step, strip), to] = top
            k_low[pl.ds(to_row + step, strip), to] = rest
        return 0

    lax.fori_loop(0, count // strip, body, 0)


def store_halves(halves, at, vector):
    rows, size = vector.shape
    top, rest = split(vector * SCALE)
    halves[0:rows, at : at + size] = top
    halves[rows : 2 * rows, at : at + size] = rest


def multiply(both, k_high, k_low, turned=False):
    rows = both.shape[0] // 2
    dims = (((1,), (1 if turned else 0,)), ((), ()))
    most = lax.dot_general(both, k_high, dims, preferred_element_type=F32)
    rest = lax.dot_general(both[0:rows], k_low, dims, preferred_element_type=F32)
    return most[0:rows] + (most[rows : 2 * rows] + rest)


def local_product(noise, vector, k_high, k_low, out, halves, length):
    here = vector.shape[1]
    store_halves(halves, 0, vector[...])
    for start in range(0, here, length):
        stop = start + length
        at, before, after = slice(start, stop), slice(0, stop), slice(stop, here)
        value = multiply(halves[:, before], k_high[before, at], k_low[before, at])
        if stop < here:
            value = value + multiply(halves[:, after], k_high[at, after], k_low[at, after], turned=True)
        out[:, at] = value + (noise[:, at] - SHIFT) * vector[:, at]


def local_first_kernel(own, noise, probes, k_high, k_low, out, first, columns, halves, rows, sem, *, links):
    here = own.shape[1]
    blocks = links + 1
    length = here // blocks
    copy = pltpu.make_async_copy(probes, first, sem.at[0])
    copy.start()
    for j in range(blocks):
        fill_columns(columns, j * length, 4.0 * own[:, j * length : (j + 1) * length])
    for d in range(1, 3):
        rows[d] = jnp.broadcast_to(4.0 * own[d : d + 1, :], rows.shape[1:])
    for i in range(blocks):
        for j in range(i, blocks):
            at = slice(j * length, (j + 1) * length)
            moved = 4.0 * own[0:1, at]
            if j > i:
                flag = own[2 + j - i : 3 + j - i, i * length : (i + 1) * length]
                moved = jnp.where(flag == 1.0, moved, moved + FAR)
            rows[0, :, at] = jnp.broadcast_to(moved, (8, length))
        fill_tiles(k_high, k_low, i * length, columns, i * length, length, rows, slice(i * length, here), i * length)
    copy.wait()
    local_product(noise, first, k_high, k_low, out, halves, length)


def fill_halo(right, own, received, columns, tables, rows, links):
    length = received.shape[1] // links
    blocks = own.shape[1] // length
    at = received.shape[0] - 8
    place = [pl.ds(halo_place(right, links, length, h), length) for h in range(links)]
    for h in range(max(tables)):
        for d in range(1, 3):
            coord = 4.0 * received[at + d : at + d + 1, place[h]]
            rows[d, :, h * length : (h + 1) * length] = jnp.broadcast_to(coord, (8, length))
    for n, (k_high, k_low) in tables.items():
        mine = own_place(right, blocks, links, length, n)
        for h in range(n):
            k = links - n + h
            ours = own[3 + k : 4 + k, pl.ds(mine, length)]
            theirs = received[at + 3 + k : at + 4 + k, place[h]]
            coord = 4.0 * received[at : at + 1, place[h]]
            coord = jnp.where(jnp.where(right, ours, theirs) == 1.0, coord, coord + FAR)
            rows[0, :, h * length : (h + 1) * length] = jnp.broadcast_to(coord, (8, length))
        fill_tiles(k_high, k_low, 0, columns, mine, length, rows, slice(0, n * length), 0)


def table_rows(k_high, k_low, ns, length):
    parts = {n: (pl.ds((n - ns[0]) * length, length), slice(0, n * length)) for n in ns}
    return {n: (k_high.at[part], k_low.at[part]) for n, part in parts.items()}


def halo_product(right, load, tables, out, halves, links):
    length = halves.shape[1] // links
    blocks = out.shape[1] // length
    for h in range(max(tables)):
        store_halves(halves, h * length, load(pl.ds(halo_place(right, links, length, h), length)))
    for n, (k_high, k_low) in tables.items():
        own = pl.ds(own_place(right, blocks, links, length, n), length)
        out[:, own] = out[:, own] + multiply(halves[:, 0 : n * length], k_high[...], k_low[...], turned=True)


def own_product(right, vector, k_high, k_low, out, halves, blocks):
    span = out.shape[1]
    length = vector.shape[1] // blocks
    links = span // length
    for n in range(1, links + 1):
        own = pl.ds(own_place(right, blocks, links, length, n), length)
        store_halves(halves, (n - 1) * length, vector[:, own])
    for h in range(links):
        deep, at = slice(h * length, span), slice(h * length, (h + 1) * length)
        place = pl.ds(halo_place(right, links, length, h), length)
        out[:, place] = multiply(halves[:, deep], k_high[deep, at], k_low[deep, at])


def store_send(right, vector, send):
    here, span = vector.shape[1], send.shape[1]
    rows = vector.shape[0]
    send[0:rows, :] = vector[:, pl.ds(send_place(right, here, span), span)]
    if send.shape[0] > rows:
        send[rows:, :] = jnp.zeros((send.shape[0] - rows, span), F32)


def mate_first_kernel(own, partial, received, columns, k_high, k_low, out, to_next, halves, rows, *, links):
    probe_count = out.shape[0]
    right = is_right(True)
    length = halves.shape[1] // links
    tables = table_rows(k_high, k_low, range(1, links), length)
    fill_halo(right, own, received, columns, tables, rows, links)
    out[...] = partial[...]
    halo_product(right, lambda at: received[0:probe_count, at], tables, out, halves, links)
    store_send(is_right(False), out, to_next)


def next_first_kernel(
    own, partial, mate, received, columns, mate_high, mate_low, k_high, k_low, out, to_mate, halves, rows, *, links
):
    probe_count = out.shape[0]
    length = halves.shape[1] // links
    out[...] = partial[...]
    right = is_right(True)
    tables = table_rows(mate_high, mate_low, range(links, links + 1), length)
    fill_halo(right, own, mate, columns, tables, rows, links)
    halo_product(right, lambda at: mate[0:probe_count, at], tables, out, halves, links)
    right = is_right(False)
    tables = table_rows(k_high, k_low, range(1, links + 1), length)
    fill_halo(right, own, received, columns, tables, rows, links)
    halo_product(right, lambda at: received[0:probe_count, at], tables, out, halves, links)
    store_send(is_right(True), out, to_mate)


def add_sums(table, terms):
    lane = lax.broadcasted_iota(jnp.int32, table.shape, 1)
    for power, left, right in terms:
        part = None
        for at in range(0, left.shape[1], 128):
            term = left[:, at : at + 128] * right[:, at : at + 128]
            part = term if part is None else part + term
        table = jnp.where(lane == power, jnp.sum(part, axis=1, keepdims=True), table)
    return table


def local_second_kernel(noise, second, k_high, k_low, out, halves, *, length):
    local_product(noise, second, k_high, k_low, out, halves, length)


def local_third_kernel(noise, first, second, third, k_high, k_low, out, table, halves, *, length):
    local_product(noise, third, k_high, k_low, out, halves, length)
    terms = ((0, first, first), (1, first, second), (2, second, second), (3, second, third), (4, third, third))
    table[...] = add_sums(jnp.zeros(table.shape, F32), terms)


def mate_second_kernel(partial, mate, k_high, k_low, out, to_next, halves, *, links):
    length = halves.shape[1] // links
    out[...] = partial[...]
    tables = table_rows(k_high, k_low, range(1, links), length)
    halo_product(is_right(True), lambda at: mate[:, at], tables, out, halves, links)
    store_send(is_right(False), out, to_next)


def next_second_kernel(
    partial, first, second, mate, ahead, mate_high, mate_low, k_high, k_low, out, given, to_mate, halves, *, links
):
    length = halves.shape[1] // links
    right = is_right(False)
    out[...] = partial[...]
    tables = table_rows(mate_high, mate_low, range(links, links + 1), length)
    halo_product(is_right(True), lambda at: mate[:, at], tables, out, halves, links)
    own_product(right, first, k_high, k_low, given, halves, links + 1)
    tables = table_rows(k_high, k_low, range(1, links + 1), length)
    halo_product(right, received_share(ahead, given), tables, out, halves, links)
    store_send(is_right(True), out, to_mate)
    own_product(right, second, k_high, k_low, given, halves, links + 1)


def received_share(received, given):
    return lambda at: received[0 : given.shape[0], at] + given[:, at]


def mate_third_kernel(partial, mate, early_high, early_low, late_high, late_low, out, halves, *, links):
    length = halves.shape[1] // links
    out[...] = partial[...]
    tables = table_rows(early_high, early_low, range(1, links), length)
    tables.update(table_rows(late_high, late_low, range(links, links + 1), length))
    halo_product(is_right(True), lambda at: mate[:, at], tables, out, halves, links)


def next_third_kernel(partial, after, given, k_high, k_low, third, table, out, sums, halves, *, links):
    length = halves.shape[1] // links
    out[...] = partial[...]
    tables = table_rows(k_high, k_low, range(1, links + 1), length)
    halo_product(is_right(False), received_share(after, given), tables, out, halves, links)
    full = add_sums(table[...], ((5, third, out), (6, out, out)))
    turned = jnp.transpose(full)[0:8, :]
    compact = jnp.concatenate([turned[0:4], turned[4:8]], axis=1)
    sums[...] = jnp.broadcast_to(compact[None], sums.shape)


def polynomials(moment):
    def dot(p, q):
        total, size = 0.0, 0.0
        for i, x in enumerate(p):
            for j, y in enumerate(q):
                term = x * y * moment[i + j]
                total, size = total + term, size + jnp.abs(term)
        return total, size

    def add(p, q, factor):
        count = max(len(p), len(q))
        p, q = p + [0.0] * (count - len(p)), q + [0.0] * (count - len(q))
        return [x + factor * y for x, y in zip(p, q)]

    one = jnp.ones_like(moment[0])
    solution, residual, direction = [jnp.zeros_like(one)], [one], [one]
    norm = moment[0]
    good = norm > 0.0
    for step in range(ITERS):
        image = add([0.0 * one] + direction, direction, SHIFT)
        curvature, size = dot(direction, image)
        good = good & (size <= MAX_AMP * curvature)
        step_size = norm / curvature
        solution = add(solution, direction, step_size)
        residual = add(residual, image, -step_size)
        new, size = dot(residual, residual)
        if step < ITERS - 1:
            good = good & (size <= MAX_AMP * new)
            direction = add(residual, direction, new / norm)
        norm = new
    size = sum(jnp.abs(x) * jnp.sqrt(moment[2 * i]) for i, x in enumerate(residual))
    good = good & (size * size <= MAX_NORM * MAX_NORM * norm)
    return solution, residual, good


def finish_kernel(sums, first, second, third, fourth, solution, residual, good):
    total = jnp.sum(sums[...], axis=0)
    rows = first.shape[0]
    moment = [total[k : k + 1, 0:rows] for k in range(4)] + [total[k : k + 1, rows : 2 * rows] for k in range(3)]
    mix_solution, mix_residual, fine = polynomials(moment)
    table = jnp.concatenate(mix_solution + mix_residual + [jnp.zeros_like(moment[0])], axis=0)
    table = jnp.concatenate([table, jnp.zeros_like(table)], axis=1)
    table = jnp.transpose(jnp.concatenate([table, jnp.zeros((120, 128), F32)], axis=0))[0:rows]
    basis = (first[...], second[...], third[...], fourth[...])

    def mix(at, count):
        total = table[:, at : at + 1] * basis[0]
        for k in range(1, count):
            total = total + table[:, at + k : at + k + 1] * basis[k]
        return total

    solution[...] = mix(0, ITERS)
    residual[...] = mix(ITERS, ITERS + 1)
    good[0, 0] = jnp.min(jnp.where(fine, 1.0, 0.0))


VMEM = pl.BlockSpec(memory_space=pltpu.VMEM)
SMEM = pl.BlockSpec(memory_space=pltpu.SMEM)
ANY = pl.BlockSpec(memory_space=pl.ANY)


def call(kernel, name, out_shape, in_specs, scratch_shapes=(), out_specs=None):
    kwargs = {} if out_specs is None else {"out_specs": out_specs}
    return pl.pallas_call(
        kernel,
        out_shape=out_shape,
        in_specs=in_specs,
        scratch_shapes=scratch_shapes,
        compiler_params=pltpu.CompilerParams(vmem_limit_bytes=VMEM_LIMIT),
        name=name,
        **kwargs,
    )


def swap_mate(array):
    return lax.ppermute(array, AXES, [(i, i ^ 1) for i in range(lax.axis_size(AXES))])


def swap_next(array):
    return lax.ppermute(array, AXES, [(i, i + 1 if i % 2 else i - 1) for i in range(1, lax.axis_size(AXES) - 1)])


def per_device(coords, noise_var, pair_list, probes):
    rows, here = probes.shape
    links, blocks = pair_list.shape
    length = here // blocks
    span = links * length
    noise = noise_var.reshape(1, here)

    whole = jax.ShapeDtypeStruct((rows, here), F32)
    part = jax.ShapeDtypeStruct((rows, span), F32)
    packed = jax.ShapeDtypeStruct((rows + 8, span), F32)
    wide_part = jax.ShapeDtypeStruct((rows + 8, span), F32)
    sums_table = jax.ShapeDtypeStruct((rows, 128), F32)
    local_table = jax.ShapeDtypeStruct((here, here), BF16)
    halo_table = jax.ShapeDtypeStruct((span, span), BF16)
    local_halves = pltpu.VMEM((2 * rows, here), BF16)
    halo_halves = pltpu.VMEM((2 * rows, span), BF16)

    to_mate, to_next, own = call(
        pack_kernel,
        "pack",
        (packed, packed, jax.ShapeDtypeStruct((8, here), F32)),
        [ANY, ANY, ANY],
        [pltpu.VMEM((3, here), F32), pltpu.SMEM((links, blocks), jnp.int32), pltpu.SemaphoreType.DMA((4,))],
    )(coords, pair_list, probes)
    mate, beyond = swap_mate(to_mate), swap_next(to_next)
    k_high, k_low, partial, first, columns = call(
        functools.partial(local_first_kernel, links=links),
        "local_first",
        (local_table, local_table, whole, whole, jax.ShapeDtypeStruct((3, here, 128), F32)),
        [VMEM, VMEM, ANY],
        [
            local_halves,
            pltpu.VMEM((3, 8, here), F32),
            pltpu.SemaphoreType.DMA((1,)),
        ],
    )(own, noise, probes)
    halo_scratch = [halo_halves, pltpu.VMEM((3, 8, span), F32)]
    early_table = jax.ShapeDtypeStruct((span - length, span - length), BF16)
    late_table = jax.ShapeDtypeStruct((length, span), BF16)
    early_high, early_low, partial, to_next = call(
        functools.partial(mate_first_kernel, links=links),
        "mate_first",
        (early_table, early_table, whole, wide_part),
        [VMEM] * 4,
        halo_scratch,
    )(own, partial, mate, columns)
    ahead = swap_next(to_next)
    late_high, late_low, next_high, next_low, second, to_mate = call(
        functools.partial(next_first_kernel, links=links),
        "next_first",
        (late_table, late_table, halo_table, halo_table, whole, part),
        [VMEM] * 5,
        halo_scratch,
    )(own, partial, mate, beyond, columns)

    mate = swap_mate(to_mate)
    partial = call(
        functools.partial(local_second_kernel, length=length), "local_second", whole, [VMEM] * 4, [local_halves]
    )(noise, second, k_high, k_low)
    partial, to_next = call(
        functools.partial(mate_second_kernel, links=links), "mate_second", (whole, wide_part), [VMEM] * 4, [halo_halves]
    )(partial, mate, early_high, early_low)
    after = swap_next(to_next)
    third, given, to_mate = call(
        functools.partial(next_second_kernel, links=links),
        "next_second",
        (whole, part, part),
        [VMEM] * 9,
        [halo_halves],
    )(partial, first, second, mate, ahead, late_high, late_low, next_high, next_low)

    mate = swap_mate(to_mate)
    partial, table = call(
        functools.partial(local_third_kernel, length=length), "local_third", (whole, sums_table), [VMEM] * 6, [local_halves]
    )(noise, first, second, third, k_high, k_low)
    regions, subs = lax.axis_size("region"), lax.axis_size("sub")
    partial = call(
        functools.partial(mate_third_kernel, links=links), "mate_third", whole, [VMEM] * 6, [halo_halves]
    )(partial, mate, early_high, early_low, late_high, late_low)
    fourth, sums = call(
        functools.partial(next_third_kernel, links=links),
        "next_third",
        (whole, jax.ShapeDtypeStruct((regions, 4, 128), F32)),
        [VMEM] * 7,
        [halo_halves],
    )(partial, after, given, next_high, next_low, third, table)

    sums = jnp.sum(lax.all_to_all(sums, "region", 0, 0), axis=0)
    sums = lax.all_to_all(jnp.broadcast_to(sums[None], (subs, 4, 128)), "sub", 0, 0)
    solution, residual, good = call(
        finish_kernel,
        "finish",
        (whole, whole, jax.ShapeDtypeStruct((1, 1), F32)),
        [VMEM] * 5,
        out_specs=(VMEM, VMEM, SMEM),
    )(sums, first, second, third, fourth)

    def again(state):
        solution, residual = plain(coords, noise_var, pair_list, probes)
        return jnp.ones_like(state[0]), solution, residual

    _, solution, residual = lax.while_loop(lambda state: state[0][0, 0] < 0.5, again, (good, solution, residual))
    return solution, residual


def solution(mesh):
    in_specs = (P(None, AXES), P(AXES), P(None, AXES), P(None, AXES))
    out_specs = (P(None, AXES), P(None, AXES))
    return jax.shard_map(per_device, mesh=mesh, in_specs=in_specs, out_specs=out_specs, check_vma=False)
```

```python
import functools

import jax
import jax.numpy as jnp
from jax import lax
from jax.experimental import pallas as pl
from jax.experimental.pallas import tpu as pltpu
from jax.sharding import PartitionSpec as P

ITERS = 3
AXES = ("region", "sub")
SHIFT = 6.0
SCALE = 1.0 / 256.0
FAR = 65536.0
MAX_AMP = 100.0
MAX_NORM = 30.0
F32 = jnp.float32
BF16 = jnp.bfloat16
VMEM_LIMIT = 40 * 1024 * 1024


def shifted(array, by):
    count = lax.axis_size(AXES)
    pairs = [(i, i + by) for i in range(count) if 0 <= i + by < count]
    return lax.ppermute(array, AXES, pairs)


def wendland(left, right):
    squared = (left[0][..., :, None] - right[0][..., None, :]) ** 2
    squared = squared + (left[1][..., :, None] - right[1][..., None, :]) ** 2
    squared = squared + (left[2][..., :, None] - right[2][..., None, :]) ** 2
    distance = jnp.sqrt(squared)
    support = jnp.maximum(1.0 - distance, 0.0)
    return support**4 * (4.0 * distance + 1.0)


def squares(residual):
    return lax.psum(jnp.sum(residual * residual, axis=1), AXES)


def plain(coords, noise_var, pair_list, probes):
    probe_count, points_here = probes.shape
    links = pair_list.shape[0]
    blocks_here = pair_list.shape[1]
    block_len = points_here // blocks_here
    span_cols = links * block_len
    local_c = coords.reshape(3, blocks_here, block_len)
    weights = pair_list.astype(F32)
    ahead_c = shifted(coords[:, :span_cols], -1)
    ext_c = jnp.concatenate([local_c, ahead_c.reshape(3, links, block_len)], axis=1)

    def step(_, state):
        solution, residual, direction, res_norm = state
        ahead_v = shifted(direction[:, :span_cols], -1)
        ext_v = jnp.concatenate([direction, ahead_v], axis=1).reshape(probe_count, blocks_here + links, block_len)
        local_v = ext_v[:, :blocks_here]
        result = (noise_var[None, :] * direction).reshape(probe_count, blocks_here, block_len)
        spill = jnp.zeros((probe_count, blocks_here + links, block_len), F32)
        for offset in range(links + 1):
            kernel_block = wendland(local_c, ext_c[:, offset : offset + blocks_here])
            if offset > 0:
                kernel_block = kernel_block * weights[offset - 1][:, None, None]
            result = result + jnp.einsum(
                "pbj,bij->pbi", ext_v[:, offset : offset + blocks_here], kernel_block, precision=lax.Precision.HIGHEST
            )
            if offset > 0:
                spill = spill.at[:, offset : offset + blocks_here].add(
                    jnp.einsum("pbi,bij->pbj", local_v, kernel_block, precision=lax.Precision.HIGHEST)
                )
        result = result + spill[:, :blocks_here]
        result = result.at[:, :links].add(shifted(spill[:, blocks_here:], 1))
        product = result.reshape(probe_count, points_here)
        step_size = res_norm / lax.psum(jnp.sum(direction * product, axis=1), AXES)
        solution = solution + step_size[:, None] * direction
        residual = residual - step_size[:, None] * product
        next_norm = squares(residual)
        direction = residual + (next_norm / res_norm)[:, None] * direction
        return solution, residual, direction, next_norm

    state = (jnp.zeros_like(probes), probes, probes, squares(probes))
    solution, residual, _, _ = lax.fori_loop(0, ITERS, step, state)
    return solution, residual


def is_right(mate):
    return lax.axis_index("sub") % 2 == (0 if mate else 1)


def own_place(right, blocks, links, length, n):
    return pl.multiple_of(jnp.where(right, blocks - 1 - links + n, links - n) * length, 128)


def halo_place(right, links, length, h):
    return pl.multiple_of(jnp.where(right, h, links - 1 - h) * length, 128)


def send_place(right, here, span):
    return pl.multiple_of(jnp.where(right, here - span, 0), 128)


def split(value):
    high = value.astype(BF16)
    return high, (value - high.astype(F32)).astype(BF16)


def start_all(copies):
    for copy in copies:
        copy.start()
    return copies


def pack_kernel(coords, pair, probes, to_mate, to_next, own, points, flags, sem):
    links, blocks = pair.shape
    here = coords.shape[1]
    length = here // blocks
    rows, span = probes.shape[0], links * length
    place = [send_place(is_right(mate), here, span) for mate in (True, False)]
    copies = start_all(
        [
            pltpu.make_async_copy(pair, flags, sem.at[0]),
            pltpu.make_async_copy(coords, points, sem.at[1]),
            pltpu.make_async_copy(probes.at[:, pl.ds(place[0], span)], to_mate.at[0:rows], sem.at[2]),
            pltpu.make_async_copy(probes.at[:, pl.ds(place[1], span)], to_next.at[0:rows], sem.at[3]),
        ]
    )
    copies[0].wait()
    copies[1].wait()
    right = is_right(True)
    extra = [points[...]]
    for k in range(links):
        flag = [flags[k, b].astype(F32) for b in range(blocks)]
        extra.append(jnp.concatenate([jnp.full((1, length), f, F32) for f in flag], axis=1))
    extra = jnp.concatenate(extra + [jnp.zeros((8 - 3 - links, here), F32)], axis=0)
    own[...] = extra
    low, high = extra[:, 0:span], extra[:, here - span :]
    to_mate[rows : rows + 8, :] = jnp.where(right, high, low)
    to_next[rows : rows + 8, :] = jnp.where(right, low, high)
    copies[2].wait()
    copies[3].wait()


def column_steps(columns, at, block):
    def fill(d, turned):
        size = turned.shape[0]
        columns[d, at : at + size, :] = jnp.broadcast_to(turned[:, d : d + 1], (size, 128))

    def step():
        turned = jnp.transpose(block)
        for d in range(3):
            fill(d, turned)

    return [step]


def fill_strip(k_high, k_low, to_row, columns, from_row, strip, rows, x, at, first):
    column = [columns[d, pl.ds(from_row, strip), :].reshape(strip // 8, 8, 128) for d in range(3)]
    for lane in range(at.start, at.stop, 128):
        squared = None
        for d in range(3):
            away = column[d] - rows[d if d else x, :, lane : lane + 128][None]
            squared = away * away if squared is None else squared + away * away
        squared = jnp.maximum(squared, 1e-30)
        distance = squared * lax.rsqrt(squared)
        support = jnp.maximum(4.0 - distance, 0.0)
        support = support * support
        value = support * support * (distance + 1.0)
        top, rest = split(value.reshape(strip, 128))
        to = slice(first + lane - at.start, first + lane - at.start + 128)
        k_high[pl.ds(to_row, strip), to] = top
        k_low[pl.ds(to_row, strip), to] = rest


def fill_tiles(k_high, k_low, to_row, columns, from_row, count, rows, x, at, first, beside=()):
    strip = 64 if at.stop - at.start <= 4 * 128 else 32
    if not beside:

        def body(s, _):
            step = pl.multiple_of(s * strip, strip)
            fill_strip(k_high, k_low, to_row + step, columns, from_row + step, strip, rows, x, at, first)
            return 0

        lax.fori_loop(0, count // strip, body, 0)
        return
    done = 0
    for s in range(count // strip):
        step = s * strip
        fill_strip(k_high, k_low, to_row + step, columns, from_row + step, strip, rows, x, at, first)
        while done < len(beside) * (s + 1) * strip // count:
            beside[done]()
            done += 1


def store_halves(halves, at, vector):
    rows, size = vector.shape
    top, rest = split(vector * SCALE)
    halves[0:rows, at : at + size] = top
    halves[rows : 2 * rows, at : at + size] = rest


def multiply(both, k_high, k_low, turned=False):
    rows = both.shape[0] // 2
    dims = (((1,), (1 if turned else 0,)), ((), ()))
    most = lax.dot_general(both, k_high, dims, preferred_element_type=F32)
    rest = lax.dot_general(both[0:rows], k_low, dims, preferred_element_type=F32)
    return most[0:rows] + (most[rows : 2 * rows] + rest)


def local_product(noise, vector, k_high, k_low, out, halves, length):
    here = vector.shape[1]
    store_halves(halves, 0, vector[...])
    for start in range(0, here, length):
        stop = start + length
        at, before, after = slice(start, stop), slice(0, stop), slice(stop, here)
        value = multiply(halves[:, before], k_high[before, at], k_low[before, at])
        if stop < here:
            value = value + multiply(halves[:, after], k_high[at, after], k_low[at, after], turned=True)
        out[:, at] = value + (noise[:, at] - SHIFT) * vector[:, at]


def row_steps(halves, k_high, k_low, out, start, length):
    stop, here = start + length, out.shape[1]
    steps = []

    def natural(at):
        def step():
            out[:, at] = out[:, at] + multiply(halves[:, start:stop], k_high[start:stop, at], k_low[start:stop, at])

        return step

    def mirrored(at):
        def step():
            value = multiply(halves[:, at], k_high[start:stop, at], k_low[start:stop, at], turned=True)
            out[:, start:stop] = out[:, start:stop] + value

        return step

    for at in range(start, here, length):
        steps.append(natural(slice(at, at + length)))
    for at in range(stop, here, length):
        steps.append(mirrored(slice(at, at + length)))
    return steps


def local_first_kernel(own, noise, probes, k_high, k_low, out, first, columns, halves, rows, sem, *, links):
    here = own.shape[1]
    blocks = links + 1
    length = here // blocks
    copy = pltpu.make_async_copy(probes, first, sem.at[0])
    copy.start()
    for d in range(1, 3):
        rows[d] = jnp.broadcast_to(4.0 * own[d : d + 1, :], rows.shape[1:])
    steps = []
    for j in range(blocks):
        half = length // 2
        for at in (j * length, j * length + half):
            steps += column_steps(columns, at, 4.0 * own[:, at : at + half])
    for step in steps[0:2]:
        step()
    steps = steps[2:]
    for i in range(blocks):
        for j in range(i, blocks):
            at = slice(j * length, (j + 1) * length)
            moved = 4.0 * own[0:1, at]
            if j > i:
                flag = own[2 + j - i : 3 + j - i, i * length : (i + 1) * length]
                moved = jnp.where(flag == 1.0, moved, moved + FAR)
            rows[3 + i, :, at] = jnp.broadcast_to(moved, (8, length))
        start = i * length
        fill_tiles(k_high, k_low, start, columns, start, length, rows, 3 + i, slice(start, here), start, steps)
        if i == 0:
            copy.wait()
            store_halves(halves, 0, first[...])
            out[...] = (noise[...] - SHIFT) * first[...]
        steps = row_steps(halves, k_high, k_low, out, start, length)
    for step in steps:
        step()


def halo_rows(right, own, received, rows, links, ns):
    length = received.shape[1] // links
    blocks = own.shape[1] // length
    at = received.shape[0] - 8
    place = [pl.ds(halo_place(right, links, length, h), length) for h in range(links)]
    for h in range(max(ns)):
        for d in range(1, 3):
            coord = 4.0 * received[at + d : at + d + 1, place[h]]
            rows[d, :, h * length : (h + 1) * length] = jnp.broadcast_to(coord, (8, length))
    for n in ns:
        mine = own_place(right, blocks, links, length, n)
        for h in range(n):
            k = links - n + h
            ours = own[3 + k : 4 + k, pl.ds(mine, length)]
            theirs = received[at + 3 + k : at + 4 + k, place[h]]
            coord = 4.0 * received[at : at + 1, place[h]]
            coord = jnp.where(jnp.where(right, ours, theirs) == 1.0, coord, coord + FAR)
            rows[2 + n, :, h * length : (h + 1) * length] = jnp.broadcast_to(coord, (8, length))


def fill_halo(right, received, columns, tables, out, halves, rows, links, beside):
    probe_count = out.shape[0]
    length = received.shape[1] // links
    blocks = out.shape[1] // length
    for h in range(max(tables)):
        place = pl.ds(halo_place(right, links, length, h), length)
        store_halves(halves, h * length, received[0:probe_count, place])

    def product(n, h):
        own = pl.ds(own_place(right, blocks, links, length, n), length)
        at = slice(h * length, (h + 1) * length)
        k_high, k_low = tables[n]

        def step():
            out[:, own] = out[:, own] + multiply(halves[:, at], k_high[:, at], k_low[:, at], turned=True)

        return step

    for n in sorted(tables, reverse=True):
        mine = own_place(right, blocks, links, length, n)
        k_high, k_low = tables[n]
        fill_tiles(k_high, k_low, 0, columns, mine, length, rows, 2 + n, slice(0, n * length), 0, beside)
        beside = [product(n, h) for h in range(n)]
    return beside


def table_rows(k_high, k_low, ns, length):
    parts = {n: (pl.ds((n - ns[0]) * length, length), slice(0, n * length)) for n in ns}
    return {n: (k_high.at[part], k_low.at[part]) for n, part in parts.items()}


def halo_product(right, load, tables, out, halves, links):
    length = halves.shape[1] // links
    blocks = out.shape[1] // length
    for h in range(max(tables)):
        store_halves(halves, h * length, load(pl.ds(halo_place(right, links, length, h), length)))
    for n, (k_high, k_low) in tables.items():
        own = pl.ds(own_place(right, blocks, links, length, n), length)
        out[:, own] = out[:, own] + multiply(halves[:, 0 : n * length], k_high[...], k_low[...], turned=True)


def own_product(right, vector, k_high, k_low, out, halves, blocks):
    span = out.shape[1]
    length = vector.shape[1] // blocks
    links = span // length
    for n in range(1, links + 1):
        own = pl.ds(own_place(right, blocks, links, length, n), length)
        store_halves(halves, (n - 1) * length, vector[:, own])
    for h in range(links):
        deep, at = slice(h * length, span), slice(h * length, (h + 1) * length)
        place = pl.ds(halo_place(right, links, length, h), length)
        out[:, place] = multiply(halves[:, deep], k_high[deep, at], k_low[deep, at])


def store_send(right, vector, send):
    here, span = vector.shape[1], send.shape[1]
    rows = vector.shape[0]
    send[0:rows, :] = vector[:, pl.ds(send_place(right, here, span), span)]
    if send.shape[0] > rows:
        send[rows:, :] = jnp.zeros((send.shape[0] - rows, span), F32)


def mate_first_kernel(own, partial, received, columns, k_high, k_low, out, to_next, halves, rows, *, links):
    right = is_right(True)
    length = halves.shape[1] // links
    ns = range(1, links)
    halo_rows(right, own, received, rows, links, ns)
    out[...] = partial[...]
    tables = table_rows(k_high, k_low, ns, length)
    for step in fill_halo(right, received, columns, tables, out, halves, rows, links, []):
        step()
    store_send(is_right(False), out, to_next)


def next_first_kernel(
    own,
    partial,
    mate,
    received,
    columns,
    mate_high,
    mate_low,
    k_high,
    k_low,
    out,
    to_mate,
    mate_halves,
    mate_rows,
    halves,
    rows,
    *,
    links,
):
    length = halves.shape[1] // links
    out[...] = partial[...]
    left, right = is_right(True), is_right(False)
    late, ns = range(links, links + 1), range(1, links + 1)
    halo_rows(left, own, mate, mate_rows, links, late)
    halo_rows(right, own, received, rows, links, ns)
    tables = table_rows(mate_high, mate_low, late, length)
    steps = fill_halo(left, mate, columns, tables, out, mate_halves, mate_rows, links, [])
    tables = table_rows(k_high, k_low, ns, length)
    for step in fill_halo(right, received, columns, tables, out, halves, rows, links, steps):
        step()
    store_send(is_right(True), out, to_mate)


def add_sums(table, terms):
    lane = lax.broadcasted_iota(jnp.int32, table.shape, 1)
    for power, left, right in terms:
        part = None
        for at in range(0, left.shape[1], 128):
            term = left[:, at : at + 128] * right[:, at : at + 128]
            part = term if part is None else part + term
        table = jnp.where(lane == power, jnp.sum(part, axis=1, keepdims=True), table)
    return table


def local_second_kernel(noise, second, k_high, k_low, out, halves, *, length):
    local_product(noise, second, k_high, k_low, out, halves, length)


def local_third_kernel(noise, first, second, third, k_high, k_low, out, table, halves, *, length):
    local_product(noise, third, k_high, k_low, out, halves, length)
    terms = ((0, first, first), (1, first, second), (2, second, second), (3, second, third), (4, third, third))
    table[...] = add_sums(jnp.zeros(table.shape, F32), terms)


def mate_second_kernel(partial, mate, k_high, k_low, out, to_next, halves, *, links):
    length = halves.shape[1] // links
    out[...] = partial[...]
    tables = table_rows(k_high, k_low, range(1, links), length)
    halo_product(is_right(True), lambda at: mate[:, at], tables, out, halves, links)
    store_send(is_right(False), out, to_next)


def next_second_kernel(
    partial, first, second, mate, ahead, mate_high, mate_low, k_high, k_low, out, given, to_mate, halves, *, links
):
    length = halves.shape[1] // links
    right = is_right(False)
    out[...] = partial[...]
    tables = table_rows(mate_high, mate_low, range(links, links + 1), length)
    halo_product(is_right(True), lambda at: mate[:, at], tables, out, halves, links)
    own_product(right, first, k_high, k_low, given, halves, links + 1)
    tables = table_rows(k_high, k_low, range(1, links + 1), length)
    halo_product(right, received_share(ahead, given), tables, out, halves, links)
    store_send(is_right(True), out, to_mate)
    own_product(right, second, k_high, k_low, given, halves, links + 1)


def received_share(received, given):
    return lambda at: received[0 : given.shape[0], at] + given[:, at]


def mate_third_kernel(partial, mate, early_high, early_low, late_high, late_low, out, halves, *, links):
    length = halves.shape[1] // links
    out[...] = partial[...]
    tables = table_rows(early_high, early_low, range(1, links), length)
    tables.update(table_rows(late_high, late_low, range(links, links + 1), length))
    halo_product(is_right(True), lambda at: mate[:, at], tables, out, halves, links)


def next_third_kernel(partial, after, given, k_high, k_low, third, table, out, sums, halves, *, links):
    length = halves.shape[1] // links
    out[...] = partial[...]
    tables = table_rows(k_high, k_low, range(1, links + 1), length)
    halo_product(is_right(False), received_share(after, given), tables, out, halves, links)
    full = add_sums(table[...], ((5, third, out), (6, out, out)))
    turned = jnp.transpose(full)[0:8, :]
    compact = jnp.concatenate([turned[0:4], turned[4:8]], axis=1)
    sums[...] = jnp.broadcast_to(compact[None], sums.shape)


def polynomials(moment):
    def dot(p, q):
        total, size = 0.0, 0.0
        for i, x in enumerate(p):
            for j, y in enumerate(q):
                term = x * y * moment[i + j]
                total, size = total + term, size + jnp.abs(term)
        return total, size

    def add(p, q, factor):
        count = max(len(p), len(q))
        p, q = p + [0.0] * (count - len(p)), q + [0.0] * (count - len(q))
        return [x + factor * y for x, y in zip(p, q)]

    one = jnp.ones_like(moment[0])
    solution, residual, direction = [jnp.zeros_like(one)], [one], [one]
    norm = moment[0]
    good = norm > 0.0
    for step in range(ITERS):
        image = add([0.0 * one] + direction, direction, SHIFT)
        curvature, size = dot(direction, image)
        good = good & (size <= MAX_AMP * curvature)
        step_size = norm / curvature
        solution = add(solution, direction, step_size)
        residual = add(residual, image, -step_size)
        new, size = dot(residual, residual)
        if step < ITERS - 1:
            good = good & (size <= MAX_AMP * new)
            direction = add(residual, direction, new / norm)
        norm = new
    size = sum(jnp.abs(x) * jnp.sqrt(moment[2 * i]) for i, x in enumerate(residual))
    good = good & (size * size <= MAX_NORM * MAX_NORM * norm)
    return solution, residual, good


def finish_kernel(sums, first, second, third, fourth, solution, residual, good):
    total = jnp.sum(sums[...], axis=0)
    rows = first.shape[0]
    moment = [total[k : k + 1, 0:rows] for k in range(4)] + [total[k : k + 1, rows : 2 * rows] for k in range(3)]
    mix_solution, mix_residual, fine = polynomials(moment)
    table = jnp.concatenate(mix_solution + mix_residual + [jnp.zeros_like(moment[0])], axis=0)
    table = jnp.concatenate([table, jnp.zeros_like(table)], axis=1)
    table = jnp.transpose(jnp.concatenate([table, jnp.zeros((120, 128), F32)], axis=0))[0:rows]
    basis = (first[...], second[...], third[...], fourth[...])

    def mix(at, count):
        total = table[:, at : at + 1] * basis[0]
        for k in range(1, count):
            total = total + table[:, at + k : at + k + 1] * basis[k]
        return total

    solution[...] = mix(0, ITERS)
    residual[...] = mix(ITERS, ITERS + 1)
    good[0, 0] = jnp.min(jnp.where(fine, 1.0, 0.0))


VMEM = pl.BlockSpec(memory_space=pltpu.VMEM)
SMEM = pl.BlockSpec(memory_space=pltpu.SMEM)
ANY = pl.BlockSpec(memory_space=pl.ANY)


def call(kernel, name, out_shape, in_specs, scratch_shapes=(), out_specs=None):
    kwargs = {} if out_specs is None else {"out_specs": out_specs}
    return pl.pallas_call(
        kernel,
        out_shape=out_shape,
        in_specs=in_specs,
        scratch_shapes=scratch_shapes,
        compiler_params=pltpu.CompilerParams(vmem_limit_bytes=VMEM_LIMIT),
        name=name,
        **kwargs,
    )


def swap_mate(array):
    return lax.ppermute(array, AXES, [(i, i ^ 1) for i in range(lax.axis_size(AXES))])


def swap_next(array):
    return lax.ppermute(array, AXES, [(i, i + 1 if i % 2 else i - 1) for i in range(1, lax.axis_size(AXES) - 1)])


def per_device(coords, noise_var, pair_list, probes):
    rows, here = probes.shape
    links, blocks = pair_list.shape
    length = here // blocks
    span = links * length
    noise = noise_var.reshape(1, here)

    whole = jax.ShapeDtypeStruct((rows, here), F32)
    part = jax.ShapeDtypeStruct((rows, span), F32)
    packed = jax.ShapeDtypeStruct((rows + 8, span), F32)
    wide_part = jax.ShapeDtypeStruct((rows + 8, span), F32)
    sums_table = jax.ShapeDtypeStruct((rows, 128), F32)
    local_table = jax.ShapeDtypeStruct((here, here), BF16)
    halo_table = jax.ShapeDtypeStruct((span, span), BF16)
    local_halves = pltpu.VMEM((2 * rows, here), BF16)
    halo_halves = pltpu.VMEM((2 * rows, span), BF16)

    to_mate, to_next, own = call(
        pack_kernel,
        "pack",
        (packed, packed, jax.ShapeDtypeStruct((8, here), F32)),
        [ANY, ANY, ANY],
        [pltpu.VMEM((3, here), F32), pltpu.SMEM((links, blocks), jnp.int32), pltpu.SemaphoreType.DMA((4,))],
    )(coords, pair_list, probes)
    mate, beyond = swap_mate(to_mate), swap_next(to_next)
    k_high, k_low, partial, first, columns = call(
        functools.partial(local_first_kernel, links=links),
        "local_first",
        (local_table, local_table, whole, whole, jax.ShapeDtypeStruct((3, here, 128), F32)),
        [VMEM, VMEM, ANY],
        [
            local_halves,
            pltpu.VMEM((3 + blocks, 8, here), F32),
            pltpu.SemaphoreType.DMA((1,)),
        ],
    )(own, noise, probes)
    halo_scratch = [halo_halves, pltpu.VMEM((3 + links, 8, span), F32)]
    early_table = jax.ShapeDtypeStruct((span - length, span - length), BF16)
    late_table = jax.ShapeDtypeStruct((length, span), BF16)
    early_high, early_low, partial, to_next = call(
        functools.partial(mate_first_kernel, links=links),
        "mate_first",
        (early_table, early_table, whole, wide_part),
        [VMEM] * 4,
        halo_scratch,
    )(own, partial, mate, columns)
    ahead = swap_next(to_next)
    late_high, late_low, next_high, next_low, second, to_mate = call(
        functools.partial(next_first_kernel, links=links),
        "next_first",
        (late_table, late_table, halo_table, halo_table, whole, part),
        [VMEM] * 5,
        halo_scratch + halo_scratch,
    )(own, partial, mate, beyond, columns)

    mate = swap_mate(to_mate)
    partial = call(
        functools.partial(local_second_kernel, length=length), "local_second", whole, [VMEM] * 4, [local_halves]
    )(noise, second, k_high, k_low)
    partial, to_next = call(
        functools.partial(mate_second_kernel, links=links), "mate_second", (whole, wide_part), [VMEM] * 4, [halo_halves]
    )(partial, mate, early_high, early_low)
    after = swap_next(to_next)
    third, given, to_mate = call(
        functools.partial(next_second_kernel, links=links),
        "next_second",
        (whole, part, part),
        [VMEM] * 9,
        [halo_halves],
    )(partial, first, second, mate, ahead, late_high, late_low, next_high, next_low)

    mate = swap_mate(to_mate)
    partial, table = call(
        functools.partial(local_third_kernel, length=length), "local_third", (whole, sums_table), [VMEM] * 6, [local_halves]
    )(noise, first, second, third, k_high, k_low)
    regions, subs = lax.axis_size("region"), lax.axis_size("sub")
    partial = call(
        functools.partial(mate_third_kernel, links=links), "mate_third", whole, [VMEM] * 6, [halo_halves]
    )(partial, mate, early_high, early_low, late_high, late_low)
    fourth, sums = call(
        functools.partial(next_third_kernel, links=links),
        "next_third",
        (whole, jax.ShapeDtypeStruct((regions, 4, 128), F32)),
        [VMEM] * 7,
        [halo_halves],
    )(partial, after, given, next_high, next_low, third, table)

    sums = jnp.sum(lax.all_to_all(sums, "region", 0, 0), axis=0)
    sums = lax.all_to_all(jnp.broadcast_to(sums[None], (subs, 4, 128)), "sub", 0, 0)
    solution, residual, good = call(
        finish_kernel,
        "finish",
        (whole, whole, jax.ShapeDtypeStruct((1, 1), F32)),
        [VMEM] * 5,
        out_specs=(VMEM, VMEM, SMEM),
    )(sums, first, second, third, fourth)

    def again(state):
        solution, residual = plain(coords, noise_var, pair_list, probes)
        return jnp.ones_like(state[0]), solution, residual

    _, solution, residual = lax.while_loop(lambda state: state[0][0, 0] < 0.5, again, (good, solution, residual))
    return solution, residual


def solution(mesh):
    in_specs = (P(None, AXES), P(AXES), P(None, AXES), P(None, AXES))
    out_specs = (P(None, AXES), P(None, AXES))
    return jax.shard_map(per_device, mesh=mesh, in_specs=in_specs, out_specs=out_specs, check_vma=False)
```

```python
import functools

import jax
import jax.numpy as jnp
from jax import lax
from jax.experimental import pallas as pl
from jax.experimental.pallas import tpu as pltpu
from jax.sharding import PartitionSpec as P

ITERS = 3
AXES = ("region", "sub")
SHIFT = 6.0
SCALE = 1.0 / 256.0
FAR = 65536.0
MAX_AMP = 100.0
MAX_NORM = 30.0
F32 = jnp.float32
BF16 = jnp.bfloat16
VMEM_LIMIT = 40 * 1024 * 1024


def shifted(array, by):
    count = lax.axis_size(AXES)
    pairs = [(i, i + by) for i in range(count) if 0 <= i + by < count]
    return lax.ppermute(array, AXES, pairs)


def wendland(left, right):
    squared = (left[0][..., :, None] - right[0][..., None, :]) ** 2
    squared = squared + (left[1][..., :, None] - right[1][..., None, :]) ** 2
    squared = squared + (left[2][..., :, None] - right[2][..., None, :]) ** 2
    distance = jnp.sqrt(squared)
    support = jnp.maximum(1.0 - distance, 0.0)
    return support**4 * (4.0 * distance + 1.0)


def squares(residual):
    return lax.psum(jnp.sum(residual * residual, axis=1), AXES)


def plain(coords, noise_var, pair_list, probes):
    probe_count, points_here = probes.shape
    links = pair_list.shape[0]
    blocks_here = pair_list.shape[1]
    block_len = points_here // blocks_here
    span_cols = links * block_len
    local_c = coords.reshape(3, blocks_here, block_len)
    weights = pair_list.astype(F32)
    ahead_c = shifted(coords[:, :span_cols], -1)
    ext_c = jnp.concatenate([local_c, ahead_c.reshape(3, links, block_len)], axis=1)

    def step(_, state):
        solution, residual, direction, res_norm = state
        ahead_v = shifted(direction[:, :span_cols], -1)
        ext_v = jnp.concatenate([direction, ahead_v], axis=1).reshape(probe_count, blocks_here + links, block_len)
        local_v = ext_v[:, :blocks_here]
        result = (noise_var[None, :] * direction).reshape(probe_count, blocks_here, block_len)
        spill = jnp.zeros((probe_count, blocks_here + links, block_len), F32)
        for offset in range(links + 1):
            kernel_block = wendland(local_c, ext_c[:, offset : offset + blocks_here])
            if offset > 0:
                kernel_block = kernel_block * weights[offset - 1][:, None, None]
            result = result + jnp.einsum(
                "pbj,bij->pbi", ext_v[:, offset : offset + blocks_here], kernel_block, precision=lax.Precision.HIGHEST
            )
            if offset > 0:
                spill = spill.at[:, offset : offset + blocks_here].add(
                    jnp.einsum("pbi,bij->pbj", local_v, kernel_block, precision=lax.Precision.HIGHEST)
                )
        result = result + spill[:, :blocks_here]
        result = result.at[:, :links].add(shifted(spill[:, blocks_here:], 1))
        product = result.reshape(probe_count, points_here)
        step_size = res_norm / lax.psum(jnp.sum(direction * product, axis=1), AXES)
        solution = solution + step_size[:, None] * direction
        residual = residual - step_size[:, None] * product
        next_norm = squares(residual)
        direction = residual + (next_norm / res_norm)[:, None] * direction
        return solution, residual, direction, next_norm

    state = (jnp.zeros_like(probes), probes, probes, squares(probes))
    solution, residual, _, _ = lax.fori_loop(0, ITERS, step, state)
    return solution, residual


def is_right(mate):
    return lax.axis_index("sub") % 2 == (0 if mate else 1)


def own_place(right, blocks, links, length, n):
    return pl.multiple_of(jnp.where(right, blocks - 1 - links + n, links - n) * length, 128)


def halo_place(right, links, length, h):
    return pl.multiple_of(jnp.where(right, h, links - 1 - h) * length, 128)


def send_place(right, here, span):
    return pl.multiple_of(jnp.where(right, here - span, 0), 128)


def split(value):
    high = value.astype(BF16)
    return high, (value - high.astype(F32)).astype(BF16)


def start_all(copies):
    for copy in copies:
        copy.start()
    return copies


def pack_kernel(coords, pair, probes, to_mate, to_next, own, points, flags, sem):
    links, blocks = pair.shape
    here = coords.shape[1]
    length = here // blocks
    rows, span = probes.shape[0], links * length
    place = [send_place(is_right(mate), here, span) for mate in (True, False)]
    copies = start_all(
        [
            pltpu.make_async_copy(pair, flags, sem.at[0]),
            pltpu.make_async_copy(coords, points, sem.at[1]),
            pltpu.make_async_copy(probes.at[:, pl.ds(place[0], span)], to_mate.at[0:rows], sem.at[2]),
            pltpu.make_async_copy(probes.at[:, pl.ds(place[1], span)], to_next.at[0:rows], sem.at[3]),
        ]
    )
    copies[0].wait()
    copies[1].wait()
    right = is_right(True)
    extra = [points[...]]
    for k in range(links):
        flag = [flags[k, b].astype(F32) for b in range(blocks)]
        extra.append(jnp.concatenate([jnp.full((1, length), f, F32) for f in flag], axis=1))
    extra = jnp.concatenate(extra + [jnp.zeros((8 - 3 - links, here), F32)], axis=0)
    own[...] = extra
    low, high = extra[:, 0:span], extra[:, here - span :]
    to_mate[rows : rows + 8, :] = jnp.where(right, high, low)
    to_next[rows : rows + 8, :] = jnp.where(right, low, high)
    to_next[rows + 8 :, :] = jnp.zeros((to_next.shape[0] - rows - 8, span), F32)
    copies[2].wait()
    copies[3].wait()


def column_steps(columns, at, block):
    def fill(d, turned):
        size = turned.shape[0]
        columns[d, at : at + size, :] = jnp.broadcast_to(turned[:, d : d + 1], (size, 128))

    def step():
        turned = jnp.transpose(block)
        for d in range(3):
            fill(d, turned)

    return [step]


def fill_strip(k_high, k_low, to_row, columns, from_row, strip, rows, x, at, first):
    column = [columns[d, pl.ds(from_row, strip), :].reshape(strip // 8, 8, 128) for d in range(3)]
    for lane in range(at.start, at.stop, 128):
        squared = None
        for d in range(3):
            away = column[d] - rows[d if d else x, :, lane : lane + 128][None]
            squared = away * away if squared is None else squared + away * away
        squared = jnp.maximum(squared, 1e-30)
        distance = squared * lax.rsqrt(squared)
        support = jnp.maximum(4.0 - distance, 0.0)
        support = support * support
        value = support * support * (distance + 1.0)
        top, rest = split(value.reshape(strip, 128))
        to = slice(first + lane - at.start, first + lane - at.start + 128)
        k_high[pl.ds(to_row, strip), to] = top
        k_low[pl.ds(to_row, strip), to] = rest


def fill_tiles(k_high, k_low, to_row, columns, from_row, count, rows, x, at, first, beside=()):
    strip = 64 if at.stop - at.start <= 4 * 128 else 32
    if not beside:

        def body(s, _):
            step = pl.multiple_of(s * strip, strip)
            fill_strip(k_high, k_low, to_row + step, columns, from_row + step, strip, rows, x, at, first)
            return 0

        lax.fori_loop(0, count // strip, body, 0)
        return
    done = 0
    for s in range(count // strip):
        step = s * strip
        fill_strip(k_high, k_low, to_row + step, columns, from_row + step, strip, rows, x, at, first)
        while done < len(beside) * (s + 1) * strip // count:
            beside[done]()
            done += 1


def store_halves(halves, at, vector):
    rows, size = vector.shape
    top, rest = split(vector * SCALE)
    halves[0:rows, at : at + size] = top
    halves[rows : 2 * rows, at : at + size] = rest


def multiply(both, k_high, k_low, turned=False):
    rows = both.shape[0] // 2
    dims = (((1,), (1 if turned else 0,)), ((), ()))
    most = lax.dot_general(both, k_high, dims, preferred_element_type=F32)
    rest = lax.dot_general(both[0:rows], k_low, dims, preferred_element_type=F32)
    return most[0:rows] + (most[rows : 2 * rows] + rest)


def local_product(noise, vector, k_high, k_low, out, halves, length):
    here = vector.shape[1]
    store_halves(halves, 0, vector[...])
    for start in range(0, here, length):
        stop = start + length
        at, before, after = slice(start, stop), slice(0, stop), slice(stop, here)
        value = multiply(halves[:, before], k_high[before, at], k_low[before, at])
        if stop < here:
            value = value + multiply(halves[:, after], k_high[at, after], k_low[at, after], turned=True)
        out[:, at] = value + (noise[:, at] - SHIFT) * vector[:, at]


def row_steps(halves, k_high, k_low, out, start, length):
    stop, here = start + length, out.shape[1]
    steps = []

    def natural(at):
        def step():
            out[:, at] = out[:, at] + multiply(halves[:, start:stop], k_high[start:stop, at], k_low[start:stop, at])

        return step

    def mirrored(at):
        def step():
            value = multiply(halves[:, at], k_high[start:stop, at], k_low[start:stop, at], turned=True)
            out[:, start:stop] = out[:, start:stop] + value

        return step

    for at in range(start, here, length):
        steps.append(natural(slice(at, at + length)))
    for at in range(stop, here, length):
        steps.append(mirrored(slice(at, at + length)))
    return steps


def local_first_kernel(own, noise, probes, k_high, k_low, out, first, columns, halves, rows, sem, *, links):
    here = own.shape[1]
    blocks = links + 1
    length = here // blocks
    copy = pltpu.make_async_copy(probes, first, sem.at[0])
    copy.start()
    for d in range(1, 3):
        rows[d] = jnp.broadcast_to(4.0 * own[d : d + 1, :], rows.shape[1:])
    steps = []
    for j in range(blocks):
        half = length // 2
        for at in (j * length, j * length + half):
            steps += column_steps(columns, at, 4.0 * own[:, at : at + half])
    for step in steps[0:2]:
        step()
    steps = steps[2:]
    for i in range(blocks):
        for j in range(i, blocks):
            at = slice(j * length, (j + 1) * length)
            moved = 4.0 * own[0:1, at]
            if j > i:
                flag = own[2 + j - i : 3 + j - i, i * length : (i + 1) * length]
                moved = jnp.where(flag == 1.0, moved, moved + FAR)
            rows[3 + i, :, at] = jnp.broadcast_to(moved, (8, length))
        start = i * length
        fill_tiles(k_high, k_low, start, columns, start, length, rows, 3 + i, slice(start, here), start, steps)
        if i == 0:
            copy.wait()
            store_halves(halves, 0, first[...])
            out[...] = (noise[...] - SHIFT) * first[...]
        steps = row_steps(halves, k_high, k_low, out, start, length)
    for step in steps:
        step()


def halo_rows(right, own, received, at, rows, links, ns):
    length = received.shape[1] // links
    blocks = own.shape[1] // length
    place = [pl.ds(halo_place(right, links, length, h), length) for h in range(links)]
    for h in range(max(ns)):
        for d in range(1, 3):
            coord = 4.0 * received[at + d : at + d + 1, place[h]]
            rows[d, :, h * length : (h + 1) * length] = jnp.broadcast_to(coord, (8, length))
    for n in ns:
        mine = own_place(right, blocks, links, length, n)
        for h in range(n):
            k = links - n + h
            ours = own[3 + k : 4 + k, pl.ds(mine, length)]
            theirs = received[at + 3 + k : at + 4 + k, place[h]]
            coord = 4.0 * received[at : at + 1, place[h]]
            coord = jnp.where(jnp.where(right, ours, theirs) == 1.0, coord, coord + FAR)
            rows[2 + n, :, h * length : (h + 1) * length] = jnp.broadcast_to(coord, (8, length))


def fill_halo(right, received, columns, tables, out, halves, rows, links, beside):
    probe_count = out.shape[0]
    length = received.shape[1] // links
    blocks = out.shape[1] // length
    for h in range(max(tables)):
        place = pl.ds(halo_place(right, links, length, h), length)
        store_halves(halves, h * length, received[0:probe_count, place])

    def product(n, h):
        own = pl.ds(own_place(right, blocks, links, length, n), length)
        at = slice(h * length, (h + 1) * length)
        k_high, k_low = tables[n]

        def step():
            out[:, own] = out[:, own] + multiply(halves[:, at], k_high[:, at], k_low[:, at], turned=True)

        return step

    for n in sorted(tables, reverse=True):
        mine = own_place(right, blocks, links, length, n)
        k_high, k_low = tables[n]
        fill_tiles(k_high, k_low, 0, columns, mine, length, rows, 2 + n, slice(0, n * length), 0, beside)
        beside = [product(n, h) for h in range(n)]
    return beside


def table_rows(k_high, k_low, ns, length):
    parts = {n: (pl.ds((n - ns[0]) * length, length), slice(0, n * length)) for n in ns}
    return {n: (k_high.at[part], k_low.at[part]) for n, part in parts.items()}


def halo_product(right, load, tables, out, halves, links):
    length = halves.shape[1] // links
    blocks = out.shape[1] // length
    for h in range(max(tables)):
        store_halves(halves, h * length, load(pl.ds(halo_place(right, links, length, h), length)))
    for n, (k_high, k_low) in tables.items():
        own = pl.ds(own_place(right, blocks, links, length, n), length)
        out[:, own] = out[:, own] + multiply(halves[:, 0 : n * length], k_high[...], k_low[...], turned=True)


def own_product(right, vector, k_high, k_low, out, halves, blocks):
    span = out.shape[1]
    length = vector.shape[1] // blocks
    links = span // length
    for n in range(1, links + 1):
        own = pl.ds(own_place(right, blocks, links, length, n), length)
        store_halves(halves, (n - 1) * length, vector[:, own])
    for h in range(links):
        deep, at = slice(h * length, span), slice(h * length, (h + 1) * length)
        place = pl.ds(halo_place(right, links, length, h), length)
        out[:, place] = multiply(halves[:, deep], k_high[deep, at], k_low[deep, at])


def store_send(right, vector, send):
    here, span = vector.shape[1], send.shape[1]
    rows = vector.shape[0]
    send[0:rows, :] = vector[:, pl.ds(send_place(right, here, span), span)]
    if send.shape[0] > rows:
        send[rows:, :] = jnp.zeros((send.shape[0] - rows, span), F32)


def mate_first_kernel(own, partial, received, columns, k_high, k_low, out, to_next, halves, rows, *, links):
    right = is_right(True)
    length = halves.shape[1] // links
    ns = range(1, links)
    halo_rows(right, own, received, out.shape[0], rows, links, ns)
    out[...] = partial[...]
    tables = table_rows(k_high, k_low, ns, length)
    for step in fill_halo(right, received, columns, tables, out, halves, rows, links, []):
        step()
    store_send(is_right(False), out, to_next)


def next_first_kernel(
    own,
    partial,
    mate,
    received,
    columns,
    mate_high,
    mate_low,
    k_high,
    k_low,
    out,
    to_mate,
    mate_halves,
    mate_rows,
    halves,
    rows,
    *,
    links,
):
    length = halves.shape[1] // links
    out[...] = partial[...]
    left, right = is_right(True), is_right(False)
    late, ns = range(links, links + 1), range(1, links + 1)
    halo_rows(left, own, mate, out.shape[0], mate_rows, links, late)
    halo_rows(right, own, received, out.shape[0], rows, links, ns)
    tables = table_rows(mate_high, mate_low, late, length)
    steps = fill_halo(left, mate, columns, tables, out, mate_halves, mate_rows, links, [])
    tables = table_rows(k_high, k_low, ns, length)
    for step in fill_halo(right, received, columns, tables, out, halves, rows, links, steps):
        step()
    store_send(is_right(True), out, to_mate)


def add_sums(table, terms):
    lane = lax.broadcasted_iota(jnp.int32, table.shape, 1)
    for power, left, right in terms:
        part = None
        for at in range(0, left.shape[1], 128):
            term = left[:, at : at + 128] * right[:, at : at + 128]
            part = term if part is None else part + term
        table = jnp.where(lane == power, jnp.sum(part, axis=1, keepdims=True), table)
    return table


def local_second_kernel(noise, second, k_high, k_low, out, halves, *, length):
    local_product(noise, second, k_high, k_low, out, halves, length)


def local_third_kernel(noise, first, second, third, k_high, k_low, out, table, halves, *, length):
    local_product(noise, third, k_high, k_low, out, halves, length)
    terms = ((0, first, first), (1, first, second), (2, second, second), (3, second, third), (4, third, third))
    table[...] = add_sums(jnp.zeros(table.shape, F32), terms)


def mate_second_kernel(partial, mate, k_high, k_low, out, to_next, halves, *, links):
    length = halves.shape[1] // links
    out[...] = partial[...]
    tables = table_rows(k_high, k_low, range(1, links), length)
    halo_product(is_right(True), lambda at: mate[:, at], tables, out, halves, links)
    store_send(is_right(False), out, to_next)


def next_second_kernel(
    partial, first, second, mate, ahead, mate_high, mate_low, k_high, k_low, out, given, to_mate, halves, *, links
):
    length = halves.shape[1] // links
    right = is_right(False)
    out[...] = partial[...]
    tables = table_rows(mate_high, mate_low, range(links, links + 1), length)
    halo_product(is_right(True), lambda at: mate[:, at], tables, out, halves, links)
    own_product(right, first, k_high, k_low, given, halves, links + 1)
    tables = table_rows(k_high, k_low, range(1, links + 1), length)
    halo_product(right, received_share(ahead, given), tables, out, halves, links)
    store_send(is_right(True), out, to_mate)
    own_product(right, second, k_high, k_low, given, halves, links + 1)


def received_share(received, given):
    return lambda at: received[0 : given.shape[0], at] + given[:, at]


def mate_third_kernel(partial, mate, early_high, early_low, late_high, late_low, out, halves, *, links):
    length = halves.shape[1] // links
    out[...] = partial[...]
    tables = table_rows(early_high, early_low, range(1, links), length)
    tables.update(table_rows(late_high, late_low, range(links, links + 1), length))
    halo_product(is_right(True), lambda at: mate[:, at], tables, out, halves, links)


def next_third_kernel(partial, after, given, k_high, k_low, third, table, out, sums, halves, *, links):
    length = halves.shape[1] // links
    out[...] = partial[...]
    tables = table_rows(k_high, k_low, range(1, links + 1), length)
    halo_product(is_right(False), received_share(after, given), tables, out, halves, links)
    full = add_sums(table[...], ((5, third, out), (6, out, out)))
    turned = jnp.transpose(full)[0:8, :]
    compact = jnp.concatenate([turned[0:4], turned[4:8]], axis=1)
    sums[...] = jnp.broadcast_to(compact[None], sums.shape)


def polynomials(moment):
    def dot(p, q):
        total, size = 0.0, 0.0
        for i, x in enumerate(p):
            for j, y in enumerate(q):
                term = x * y * moment[i + j]
                total, size = total + term, size + jnp.abs(term)
        return total, size

    def add(p, q, factor):
        count = max(len(p), len(q))
        p, q = p + [0.0] * (count - len(p)), q + [0.0] * (count - len(q))
        return [x + factor * y for x, y in zip(p, q)]

    one = jnp.ones_like(moment[0])
    solution, residual, direction = [jnp.zeros_like(one)], [one], [one]
    norm = moment[0]
    good = norm > 0.0
    for step in range(ITERS):
        image = add([0.0 * one] + direction, direction, SHIFT)
        curvature, size = dot(direction, image)
        good = good & (size <= MAX_AMP * curvature)
        step_size = norm / curvature
        solution = add(solution, direction, step_size)
        residual = add(residual, image, -step_size)
        new, size = dot(residual, residual)
        if step < ITERS - 1:
            good = good & (size <= MAX_AMP * new)
            direction = add(residual, direction, new / norm)
        norm = new
    size = sum(jnp.abs(x) * jnp.sqrt(moment[2 * i]) for i, x in enumerate(residual))
    good = good & (size * size <= MAX_NORM * MAX_NORM * norm)
    return solution, residual, good


def finish_kernel(sums, first, second, third, fourth, solution, residual, good):
    total = jnp.sum(sums[...], axis=0)
    rows = first.shape[0]
    moment = [total[k : k + 1, 0:rows] for k in range(4)] + [total[k : k + 1, rows : 2 * rows] for k in range(3)]
    mix_solution, mix_residual, fine = polynomials(moment)
    table = jnp.concatenate(mix_solution + mix_residual + [jnp.zeros_like(moment[0])], axis=0)
    table = jnp.concatenate([table, jnp.zeros_like(table)], axis=1)
    table = jnp.transpose(jnp.concatenate([table, jnp.zeros((120, 128), F32)], axis=0))[0:rows]
    basis = (first[...], second[...], third[...], fourth[...])

    def mix(at, count):
        total = table[:, at : at + 1] * basis[0]
        for k in range(1, count):
            total = total + table[:, at + k : at + k + 1] * basis[k]
        return total

    solution[...] = mix(0, ITERS)
    residual[...] = mix(ITERS, ITERS + 1)
    good[0, 0] = jnp.min(jnp.where(fine, 1.0, 0.0))


VMEM = pl.BlockSpec(memory_space=pltpu.VMEM)
SMEM = pl.BlockSpec(memory_space=pltpu.SMEM)
ANY = pl.BlockSpec(memory_space=pl.ANY)


def call(kernel, name, out_shape, in_specs, scratch_shapes=(), out_specs=None):
    kwargs = {} if out_specs is None else {"out_specs": out_specs}
    return pl.pallas_call(
        kernel,
        out_shape=out_shape,
        in_specs=in_specs,
        scratch_shapes=scratch_shapes,
        compiler_params=pltpu.CompilerParams(vmem_limit_bytes=VMEM_LIMIT),
        name=name,
        **kwargs,
    )


def swap_mate(array):
    return lax.ppermute(array, AXES, [(i, i ^ 1) for i in range(lax.axis_size(AXES))])


def swap_next(array):
    return lax.ppermute(array, AXES, [(i, i + 1 if i % 2 else i - 1) for i in range(1, lax.axis_size(AXES) - 1)])


def per_device(coords, noise_var, pair_list, probes):
    rows, here = probes.shape
    links, blocks = pair_list.shape
    length = here // blocks
    span = links * length
    noise = noise_var.reshape(1, here)

    whole = jax.ShapeDtypeStruct((rows, here), F32)
    part = jax.ShapeDtypeStruct((rows, span), F32)
    packed = jax.ShapeDtypeStruct((rows + 8, span), F32)
    wide_packed = jax.ShapeDtypeStruct((rows + 16, span), F32)
    wide_part = jax.ShapeDtypeStruct((rows + 8, span), F32)
    sums_table = jax.ShapeDtypeStruct((rows, 128), F32)
    local_table = jax.ShapeDtypeStruct((here, here), BF16)
    halo_table = jax.ShapeDtypeStruct((span, span), BF16)
    local_halves = pltpu.VMEM((2 * rows, here), BF16)
    halo_halves = pltpu.VMEM((2 * rows, span), BF16)

    to_mate, to_next, own = call(
        pack_kernel,
        "pack",
        (packed, wide_packed, jax.ShapeDtypeStruct((8, here), F32)),
        [ANY, ANY, ANY],
        [pltpu.VMEM((3, here), F32), pltpu.SMEM((links, blocks), jnp.int32), pltpu.SemaphoreType.DMA((4,))],
    )(coords, pair_list, probes)
    mate, beyond = swap_mate(to_mate), swap_next(to_next)
    k_high, k_low, partial, first, columns = call(
        functools.partial(local_first_kernel, links=links),
        "local_first",
        (local_table, local_table, whole, whole, jax.ShapeDtypeStruct((3, here, 128), F32)),
        [VMEM, VMEM, ANY],
        [
            local_halves,
            pltpu.VMEM((3 + blocks, 8, here), F32),
            pltpu.SemaphoreType.DMA((1,)),
        ],
    )(own, noise, probes)
    halo_scratch = [halo_halves, pltpu.VMEM((3 + links, 8, span), F32)]
    early_table = jax.ShapeDtypeStruct((span - length, span - length), BF16)
    late_table = jax.ShapeDtypeStruct((length, span), BF16)
    early_high, early_low, partial, to_next = call(
        functools.partial(mate_first_kernel, links=links),
        "mate_first",
        (early_table, early_table, whole, wide_part),
        [VMEM] * 4,
        halo_scratch,
    )(own, partial, mate, columns)
    ahead = swap_next(to_next)
    late_high, late_low, next_high, next_low, second, to_mate = call(
        functools.partial(next_first_kernel, links=links),
        "next_first",
        (late_table, late_table, halo_table, halo_table, whole, part),
        [VMEM] * 5,
        halo_scratch + halo_scratch,
    )(own, partial, mate, beyond, columns)

    mate = swap_mate(to_mate)
    partial = call(
        functools.partial(local_second_kernel, length=length), "local_second", whole, [VMEM] * 4, [local_halves]
    )(noise, second, k_high, k_low)
    partial, to_next = call(
        functools.partial(mate_second_kernel, links=links), "mate_second", (whole, wide_part), [VMEM] * 4, [halo_halves]
    )(partial, mate, early_high, early_low)
    after = swap_next(to_next)
    third, given, to_mate = call(
        functools.partial(next_second_kernel, links=links),
        "next_second",
        (whole, part, part),
        [VMEM] * 9,
        [halo_halves],
    )(partial, first, second, mate, ahead, late_high, late_low, next_high, next_low)

    mate = swap_mate(to_mate)
    partial, table = call(
        functools.partial(local_third_kernel, length=length), "local_third", (whole, sums_table), [VMEM] * 6, [local_halves]
    )(noise, first, second, third, k_high, k_low)
    regions, subs = lax.axis_size("region"), lax.axis_size("sub")
    partial = call(
        functools.partial(mate_third_kernel, links=links), "mate_third", whole, [VMEM] * 6, [halo_halves]
    )(partial, mate, early_high, early_low, late_high, late_low)
    fourth, sums = call(
        functools.partial(next_third_kernel, links=links),
        "next_third",
        (whole, jax.ShapeDtypeStruct((regions, 4, 128), F32)),
        [VMEM] * 7,
        [halo_halves],
    )(partial, after, given, next_high, next_low, third, table)

    sums = jnp.sum(lax.all_to_all(sums, "region", 0, 0), axis=0)
    sums = lax.all_to_all(jnp.broadcast_to(sums[None], (subs, 4, 128)), "sub", 0, 0)
    solution, residual, good = call(
        finish_kernel,
        "finish",
        (whole, whole, jax.ShapeDtypeStruct((1, 1), F32)),
        [VMEM] * 5,
        out_specs=(VMEM, VMEM, SMEM),
    )(sums, first, second, third, fourth)

    def again(state):
        solution, residual = plain(coords, noise_var, pair_list, probes)
        return jnp.ones_like(state[0]), solution, residual

    _, solution, residual = lax.while_loop(lambda state: state[0][0, 0] < 0.5, again, (good, solution, residual))
    return solution, residual


def solution(mesh):
    in_specs = (P(None, AXES), P(AXES), P(None, AXES), P(None, AXES))
    out_specs = (P(None, AXES), P(None, AXES))
    return jax.shard_map(per_device, mesh=mesh, in_specs=in_specs, out_specs=out_specs, check_vma=False)
```

```python
import functools

import jax
import jax.numpy as jnp
from jax import lax
from jax.experimental import pallas as pl
from jax.experimental.pallas import tpu as pltpu
from jax.sharding import PartitionSpec as P

ITERS = 3
AXES = ("region", "sub")
SHIFT = 6.0
SCALE = 1.0 / 256.0
FAR = 65536.0
MAX_AMP = 100.0
MAX_NORM = 30.0
F32 = jnp.float32
BF16 = jnp.bfloat16
VMEM_LIMIT = 40 * 1024 * 1024


def shifted(array, by):
    count = lax.axis_size(AXES)
    pairs = [(i, i + by) for i in range(count) if 0 <= i + by < count]
    return lax.ppermute(array, AXES, pairs)


def wendland(left, right):
    squared = (left[0][..., :, None] - right[0][..., None, :]) ** 2
    squared = squared + (left[1][..., :, None] - right[1][..., None, :]) ** 2
    squared = squared + (left[2][..., :, None] - right[2][..., None, :]) ** 2
    distance = jnp.sqrt(squared)
    support = jnp.maximum(1.0 - distance, 0.0)
    return support**4 * (4.0 * distance + 1.0)


def squares(residual):
    return lax.psum(jnp.sum(residual * residual, axis=1), AXES)


def plain(coords, noise_var, pair_list, probes):
    probe_count, points_here = probes.shape
    links = pair_list.shape[0]
    blocks_here = pair_list.shape[1]
    block_len = points_here // blocks_here
    span_cols = links * block_len
    local_c = coords.reshape(3, blocks_here, block_len)
    weights = pair_list.astype(F32)
    ahead_c = shifted(coords[:, :span_cols], -1)
    ext_c = jnp.concatenate([local_c, ahead_c.reshape(3, links, block_len)], axis=1)

    def step(_, state):
        solution, residual, direction, res_norm = state
        ahead_v = shifted(direction[:, :span_cols], -1)
        ext_v = jnp.concatenate([direction, ahead_v], axis=1).reshape(probe_count, blocks_here + links, block_len)
        local_v = ext_v[:, :blocks_here]
        result = (noise_var[None, :] * direction).reshape(probe_count, blocks_here, block_len)
        spill = jnp.zeros((probe_count, blocks_here + links, block_len), F32)
        for offset in range(links + 1):
            kernel_block = wendland(local_c, ext_c[:, offset : offset + blocks_here])
            if offset > 0:
                kernel_block = kernel_block * weights[offset - 1][:, None, None]
            result = result + jnp.einsum(
                "pbj,bij->pbi", ext_v[:, offset : offset + blocks_here], kernel_block, precision=lax.Precision.HIGHEST
            )
            if offset > 0:
                spill = spill.at[:, offset : offset + blocks_here].add(
                    jnp.einsum("pbi,bij->pbj", local_v, kernel_block, precision=lax.Precision.HIGHEST)
                )
        result = result + spill[:, :blocks_here]
        result = result.at[:, :links].add(shifted(spill[:, blocks_here:], 1))
        product = result.reshape(probe_count, points_here)
        step_size = res_norm / lax.psum(jnp.sum(direction * product, axis=1), AXES)
        solution = solution + step_size[:, None] * direction
        residual = residual - step_size[:, None] * product
        next_norm = squares(residual)
        direction = residual + (next_norm / res_norm)[:, None] * direction
        return solution, residual, direction, next_norm

    state = (jnp.zeros_like(probes), probes, probes, squares(probes))
    solution, residual, _, _ = lax.fori_loop(0, ITERS, step, state)
    return solution, residual


def is_right(mate):
    return lax.axis_index("sub") % 2 == (0 if mate else 1)


def own_place(right, blocks, links, length, n):
    return pl.multiple_of(jnp.where(right, blocks - 1 - links + n, links - n) * length, 128)


def halo_place(right, links, length, h):
    return pl.multiple_of(jnp.where(right, h, links - 1 - h) * length, 128)


def send_place(right, here, span):
    return pl.multiple_of(jnp.where(right, here - span, 0), 128)


def split(value):
    high = value.astype(BF16)
    return high, (value - high.astype(F32)).astype(BF16)


def start_all(copies):
    for copy in copies:
        copy.start()
    return copies


def pack_kernel(coords, pair, probes, to_mate, to_next, own, points, flags, sem):
    links, blocks = pair.shape
    here = coords.shape[1]
    length = here // blocks
    rows, span = probes.shape[0], links * length
    place = [send_place(is_right(mate), here, span) for mate in (True, False)]
    copies = start_all(
        [
            pltpu.make_async_copy(pair, flags, sem.at[0]),
            pltpu.make_async_copy(coords, points, sem.at[1]),
            pltpu.make_async_copy(probes.at[:, pl.ds(place[0], span)], to_mate.at[0:rows], sem.at[2]),
            pltpu.make_async_copy(probes.at[:, pl.ds(place[1], span)], to_next.at[0:rows], sem.at[3]),
        ]
    )
    copies[0].wait()
    copies[1].wait()
    right = is_right(True)
    extra = [points[...]]
    for k in range(links):
        flag = [flags[k, b].astype(F32) for b in range(blocks)]
        extra.append(jnp.concatenate([jnp.full((1, length), f, F32) for f in flag], axis=1))
    extra = jnp.concatenate(extra + [jnp.zeros((8 - 3 - links, here), F32)], axis=0)
    own[...] = extra
    low, high = extra[:, 0:span], extra[:, here - span :]
    to_mate[rows : rows + 8, :] = jnp.where(right, high, low)
    to_next[rows : rows + 8, :] = jnp.where(right, low, high)
    to_next[rows + 8 :, :] = jnp.zeros((to_next.shape[0] - rows - 8, span), F32)
    copies[2].wait()
    copies[3].wait()


def column_steps(columns, at, load):
    def fill(d, turned):
        size = turned.shape[0]
        columns[d, at : at + size, :] = jnp.broadcast_to(turned[:, d : d + 1], (size, 128))

    def step():
        turned = jnp.transpose(load())
        for d in range(3):
            fill(d, turned)

    return [step]


def fill_strip(k_high, k_low, to_row, columns, from_row, strip, rows, x, at, first):
    column = [columns[d, pl.ds(from_row, strip), :].reshape(strip // 8, 8, 128) for d in range(3)]
    for lane in range(at.start, at.stop, 128):
        squared = None
        for d in range(3):
            away = column[d] - rows[d if d else x, :, lane : lane + 128][None]
            squared = away * away if squared is None else squared + away * away
        squared = jnp.maximum(squared, 1e-30)
        distance = squared * lax.rsqrt(squared)
        support = jnp.maximum(4.0 - distance, 0.0)
        support = support * support
        value = support * support * (distance + 1.0)
        top, rest = split(value.reshape(strip, 128))
        to = slice(first + lane - at.start, first + lane - at.start + 128)
        k_high[pl.ds(to_row, strip), to] = top
        k_low[pl.ds(to_row, strip), to] = rest


def fill_tiles(k_high, k_low, to_row, columns, from_row, count, rows, x, at, first, beside=()):
    strip = 64 if at.stop - at.start <= 4 * 128 else 32
    if not beside:

        def body(s, _):
            step = pl.multiple_of(s * strip, strip)
            fill_strip(k_high, k_low, to_row + step, columns, from_row + step, strip, rows, x, at, first)
            return 0

        lax.fori_loop(0, count // strip, body, 0)
        return
    done = 0
    for s in range(count // strip):
        step = s * strip
        fill_strip(k_high, k_low, to_row + step, columns, from_row + step, strip, rows, x, at, first)
        while done < len(beside) * (s + 1) * strip // count:
            beside[done]()
            done += 1


def store_halves(halves, at, vector):
    rows, size = vector.shape
    top, rest = split(vector * SCALE)
    halves[0:rows, at : at + size] = top
    halves[rows : 2 * rows, at : at + size] = rest


def multiply(both, k_high, k_low, turned=False):
    rows = both.shape[0] // 2
    dims = (((1,), (1 if turned else 0,)), ((), ()))
    most = lax.dot_general(both, k_high, dims, preferred_element_type=F32)
    rest = lax.dot_general(both[0:rows], k_low, dims, preferred_element_type=F32)
    return most[0:rows] + (most[rows : 2 * rows] + rest)


def local_product(noise, vector, k_high, k_low, out, halves, length):
    here = vector.shape[1]
    store_halves(halves, 0, vector[...])
    for start in range(0, here, length):
        stop = start + length
        at, before, after = slice(start, stop), slice(0, stop), slice(stop, here)
        value = multiply(halves[:, before], k_high[before, at], k_low[before, at])
        if stop < here:
            value = value + multiply(halves[:, after], k_high[at, after], k_low[at, after], turned=True)
        out[:, at] = value + (noise[:, at] - SHIFT) * vector[:, at]


def row_steps(halves, k_high, k_low, out, start, length):
    stop, here = start + length, out.shape[1]
    steps = []

    def natural(at):
        def step():
            out[:, at] = out[:, at] + multiply(halves[:, start:stop], k_high[start:stop, at], k_low[start:stop, at])

        return step

    def mirrored(at):
        def step():
            value = multiply(halves[:, at], k_high[start:stop, at], k_low[start:stop, at], turned=True)
            out[:, start:stop] = out[:, start:stop] + value

        return step

    for at in range(start, here, length):
        steps.append(natural(slice(at, at + length)))
    for at in range(stop, here, length):
        steps.append(mirrored(slice(at, at + length)))
    return steps


def local_first_kernel(own, noise, probes, k_high, k_low, out, first, halves, columns, rows, sem, *, links):
    here = own.shape[1]
    blocks = links + 1
    length = here // blocks
    copy = pltpu.make_async_copy(probes, first, sem.at[0])
    copy.start()
    for d in range(1, 3):
        rows[d] = jnp.broadcast_to(4.0 * own[d : d + 1, :], rows.shape[1:])
    steps = []
    for j in range(blocks):
        half = length // 2
        for at in (j * length, j * length + half):
            steps += column_steps(columns, at, lambda at=at: 4.0 * own[:, at : at + half])
    for step in steps[0:2]:
        step()
    steps = steps[2:]
    for i in range(blocks):
        for j in range(i, blocks):
            at = slice(j * length, (j + 1) * length)
            moved = 4.0 * own[0:1, at]
            if j > i:
                flag = own[2 + j - i : 3 + j - i, i * length : (i + 1) * length]
                moved = jnp.where(flag == 1.0, moved, moved + FAR)
            rows[3 + i, :, at] = jnp.broadcast_to(moved, (8, length))
        start = i * length
        fill_tiles(k_high, k_low, start, columns, start, length, rows, 3 + i, slice(start, here), start, steps)
        if i == 0:
            copy.wait()
            store_halves(halves, 0, first[...])
            out[...] = (noise[...] - SHIFT) * first[...]
        steps = row_steps(halves, k_high, k_low, out, start, length)
    for step in steps:
        step()


def halo_columns(right, received, at, columns, links, h):
    length = received.shape[1] // links
    half = length // 2
    steps = []
    for part in range(2):
        place = pl.ds(pl.multiple_of(halo_place(right, links, length, h) + part * half, 128), half)
        steps += column_steps(columns, h * length + part * half, lambda place=place: 4.0 * received[at : at + 8, place])
    return steps


def own_rows(right, own, received, at, rows, links, pieces):
    length = received.shape[1] // links
    blocks = own.shape[1] // length
    for n in sorted({n for _, ns in pieces for n in ns}):
        mine = pl.ds(own_place(right, blocks, links, length, n), length)
        lanes = slice((n - 1) * length, n * length)
        for d in range(1, 3):
            rows[d, :, lanes] = jnp.broadcast_to(4.0 * own[d : d + 1, mine], (8, length))
        for h, ns in pieces:
            if n not in ns:
                continue
            k = links - n + h
            ours = own[3 + k : 4 + k, mine]
            theirs = received[at + 3 + k : at + 4 + k, pl.ds(halo_place(right, links, length, h), length)]
            coord = 4.0 * own[0:1, mine]
            coord = jnp.where(jnp.where(right, ours, theirs) == 1.0, coord, coord + FAR)
            rows[3 + h, :, lanes] = jnp.broadcast_to(coord, (8, length))


def fill_halo(right, received, columns, pieces, out, halves, rows, links, beside):
    probe_count = out.shape[0]
    length = received.shape[1] // links
    blocks = out.shape[1] // length
    for h in range(max(h for h, _, _ in pieces) + 1):
        place = pl.ds(halo_place(right, links, length, h), length)
        store_halves(halves, h * length, received[0:probe_count, place])

    def product(h, n, k_high, k_low, lanes):
        own = pl.ds(own_place(right, blocks, links, length, n), length)
        at = slice(h * length, (h + 1) * length)

        def step():
            out[:, own] = out[:, own] + multiply(halves[:, at], k_high[:, lanes], k_low[:, lanes])

        return step

    for h, ns, (k_high, k_low) in pieces:
        lanes = slice((ns[0] - 1) * length, ns[-1] * length)
        fill_tiles(k_high, k_low, 0, columns, h * length, length, rows, 3 + h, lanes, 0, beside)
        beside = []
        for n in ns:
            beside.append(product(h, n, k_high, k_low, slice((n - ns[0]) * length, (n - ns[0] + 1) * length)))
    return beside


def part_of(tables, rows, lanes):
    return tuple(table.at[rows, lanes] for table in tables)


def early_tables(tables, links, length):
    return {n: part_of(tables, slice(0, n * length), slice((n - 1) * length, n * length)) for n in range(1, links)}


def halo_product(right, load, tables, out, halves, links):
    length = halves.shape[1] // links
    blocks = out.shape[1] // length
    for h in range(max(tables)):
        store_halves(halves, h * length, load(pl.ds(halo_place(right, links, length, h), length)))
    for n, (k_high, k_low) in tables.items():
        own = pl.ds(own_place(right, blocks, links, length, n), length)
        out[:, own] = out[:, own] + multiply(halves[:, 0 : n * length], k_high[...], k_low[...])


def own_product(right, vector, tables, out, halves, blocks):
    span = out.shape[1]
    length = vector.shape[1] // blocks
    links = span // length
    k_high, k_low = tables
    for n in range(1, links + 1):
        own = pl.ds(own_place(right, blocks, links, length, n), length)
        store_halves(halves, (n - 1) * length, vector[:, own])
    for h in range(links):
        deep, at = slice(h * length, span), slice(h * length, (h + 1) * length)
        place = pl.ds(halo_place(right, links, length, h), length)
        out[:, place] = multiply(halves[:, deep], k_high[at, deep], k_low[at, deep], turned=True)


def store_send(right, vector, send):
    here, span = vector.shape[1], send.shape[1]
    rows = vector.shape[0]
    send[0:rows, :] = vector[:, pl.ds(send_place(right, here, span), span)]
    if send.shape[0] > rows:
        send[rows:, :] = jnp.zeros((send.shape[0] - rows, span), F32)


def store_tiles(right, vector, send):
    here, count = vector.shape[1], vector.shape[0] // 8
    wide = (send.shape[0] - 1) // count
    start = send_place(right, here, wide * 128)
    for c in range(wide):
        lanes = pl.ds(pl.multiple_of(start + c * 128, 128), 128)
        send[c * count : (c + 1) * count] = vector[:, lanes].reshape(count, 8, 128)
    send[wide * count :] = jnp.zeros((1, 8, 128), F32)


def load_tiles(received, rows, at):
    count = rows // 8
    parts = []
    for c in range(at.size // 128):
        tile = (at.start // 128 + c) * count
        parts.append(received[pl.ds(tile, count)].reshape(rows, 128))
    return jnp.concatenate(parts, axis=1)


def mate_first_kernel(own, partial, received, k_high, k_low, out, to_next, columns, halves, rows, *, links):
    right = is_right(True)
    length = halves.shape[1] // links
    at = out.shape[0]
    pieces = [(h, range(h + 1, links)) for h in range(links - 1)]
    steps = []
    for h in range(links):
        steps += halo_columns(right, received, at, columns, links, h)
    for step in steps[0:2]:
        step()
    own_rows(right, own, received, at, rows, links, pieces)
    out[...] = partial[...]
    tables = (k_high, k_low)
    pieces = [
        (h, ns, part_of(tables, slice(h * length, (h + 1) * length), slice(h * length, (links - 1) * length)))
        for h, ns in pieces
    ]
    for step in fill_halo(right, received, columns, pieces, out, halves, rows, links, steps[2:]):
        step()
    store_send(is_right(False), out, to_next)


def next_first_kernel(
    own,
    partial,
    mate,
    mate_columns,
    received,
    mate_high,
    mate_low,
    k_high,
    k_low,
    out,
    to_mate,
    mate_halves,
    mate_rows,
    halves,
    rows,
    columns,
    *,
    links,
):
    length = halves.shape[1] // links
    at = out.shape[0]
    out[...] = partial[...]
    left, right = is_right(True), is_right(False)
    late = [(h, range(links, links + 1)) for h in range(links)]
    all_of = [(h, range(h + 1, links + 1)) for h in range(links)]
    own_rows(left, own, mate, at, mate_rows, links, late)
    own_rows(right, own, received, at, rows, links, all_of)
    steps = []
    for h in range(links):
        steps += halo_columns(right, received, at, columns, links, h)
    tables = (mate_high, mate_low)
    pieces = [(h, ns, part_of(tables, slice(h * length, (h + 1) * length), slice(0, length))) for h, ns in late]
    steps = fill_halo(left, mate, mate_columns, pieces, out, mate_halves, mate_rows, links, steps)
    tables = (k_high, k_low)
    pieces = [
        (h, ns, part_of(tables, slice(h * length, (h + 1) * length), slice(h * length, links * length)))
        for h, ns in all_of
    ]
    for step in fill_halo(right, received, columns, pieces, out, halves, rows, links, steps):
        step()
    store_send(is_right(True), out, to_mate)


def add_sums(table, terms):
    lane = lax.broadcasted_iota(jnp.int32, table.shape, 1)
    for power, left, right in terms:
        part = None
        for at in range(0, left.shape[1], 128):
            term = left[:, at : at + 128] * right[:, at : at + 128]
            part = term if part is None else part + term
        table = jnp.where(lane == power, jnp.sum(part, axis=1, keepdims=True), table)
    return table


def local_second_kernel(noise, second, k_high, k_low, out, halves, *, length):
    local_product(noise, second, k_high, k_low, out, halves, length)


def local_third_kernel(
    noise, first, second, third, k_high, k_low, next_high, next_low, out, given, table, halves, own_halves, *, length
):
    local_product(noise, third, k_high, k_low, out, halves, length)
    own_product(is_right(False), second, (next_high, next_low), given, own_halves, out.shape[1] // length)
    terms = ((0, first, first), (1, first, second), (2, second, second), (3, second, third), (4, third, third))
    table[...] = add_sums(jnp.zeros(table.shape, F32), terms)


def mate_second_kernel(partial, mate, k_high, k_low, out, to_next, halves, *, links):
    length = halves.shape[1] // links
    out[...] = partial[...]
    tables = early_tables((k_high, k_low), links, length)
    halo_product(is_right(True), lambda at: mate[:, at], tables, out, halves, links)
    store_tiles(is_right(False), out, to_next)


def next_tables(tables, links, length):
    return {n: part_of(tables, slice(0, n * length), slice((n - 1) * length, n * length)) for n in range(1, links + 1)}


def next_second_kernel(
    partial, first, mate, ahead, mate_high, mate_low, k_high, k_low, out, to_mate, halves, given, *, links
):
    length = halves.shape[1] // links
    right = is_right(False)
    out[...] = partial[...]
    halo_product(is_right(True), lambda at: mate[:, at], {links: (mate_high, mate_low)}, out, halves, links)
    own_product(right, first, (k_high, k_low), given, halves, links + 1)
    tables = next_tables((k_high, k_low), links, length)
    halo_product(right, received_share(ahead, given), tables, out, halves, links)
    store_send(is_right(True), out, to_mate)


def received_share(received, given):
    return lambda at: received[0 : given.shape[0], at] + given[:, at]


def mate_third_kernel(partial, mate, early_high, early_low, late_high, late_low, out, halves, *, links):
    length = halves.shape[1] // links
    out[...] = partial[...]
    tables = early_tables((early_high, early_low), links, length)
    tables[links] = (late_high, late_low)
    halo_product(is_right(True), lambda at: mate[:, at], tables, out, halves, links)


def next_third_kernel(partial, after, given, k_high, k_low, third, table, out, sums, halves, *, links):
    length = halves.shape[1] // links
    out[...] = partial[...]
    tables = next_tables((k_high, k_low), links, length)
    share = lambda at: load_tiles(after, out.shape[0], at) + given[:, at]
    halo_product(is_right(False), share, tables, out, halves, links)
    full = add_sums(table[...], ((5, third, out), (6, out, out)))
    turned = jnp.transpose(full)[0:8, :]
    compact = jnp.concatenate([turned[0:4], turned[4:8]], axis=1)
    sums[...] = jnp.broadcast_to(compact[None], sums.shape)


def polynomials(moment):
    def dot(p, q):
        total, size = 0.0, 0.0
        for i, x in enumerate(p):
            for j, y in enumerate(q):
                term = x * y * moment[i + j]
                total, size = total + term, size + jnp.abs(term)
        return total, size

    def add(p, q, factor):
        count = max(len(p), len(q))
        p, q = p + [0.0] * (count - len(p)), q + [0.0] * (count - len(q))
        return [x + factor * y for x, y in zip(p, q)]

    one = jnp.ones_like(moment[0])
    solution, residual, direction = [jnp.zeros_like(one)], [one], [one]
    norm = moment[0]
    good = norm > 0.0
    for step in range(ITERS):
        image = add([0.0 * one] + direction, direction, SHIFT)
        curvature, size = dot(direction, image)
        good = good & (size <= MAX_AMP * curvature)
        step_size = norm / curvature
        solution = add(solution, direction, step_size)
        residual = add(residual, image, -step_size)
        new, size = dot(residual, residual)
        if step < ITERS - 1:
            good = good & (size <= MAX_AMP * new)
            direction = add(residual, direction, new / norm)
        norm = new
    size = sum(jnp.abs(x) * jnp.sqrt(moment[2 * i]) for i, x in enumerate(residual))
    good = good & (size * size <= MAX_NORM * MAX_NORM * norm)
    return solution, residual, good


def finish_kernel(sums, first, second, third, fourth, solution, residual, good):
    total = jnp.sum(sums[...], axis=0)
    rows = first.shape[0]
    moment = [total[k : k + 1, 0:rows] for k in range(4)] + [total[k : k + 1, rows : 2 * rows] for k in range(3)]
    mix_solution, mix_residual, fine = polynomials(moment)
    table = jnp.concatenate(mix_solution + mix_residual + [jnp.zeros_like(moment[0])], axis=0)
    table = jnp.concatenate([table, jnp.zeros_like(table)], axis=1)
    table = jnp.transpose(jnp.concatenate([table, jnp.zeros((120, 128), F32)], axis=0))[0:rows]
    basis = (first[...], second[...], third[...], fourth[...])

    def mix(at, count):
        total = table[:, at : at + 1] * basis[0]
        for k in range(1, count):
            total = total + table[:, at + k : at + k + 1] * basis[k]
        return total

    solution[...] = mix(0, ITERS)
    residual[...] = mix(ITERS, ITERS + 1)
    good[0, 0] = jnp.min(jnp.where(fine, 1.0, 0.0))


VMEM = pl.BlockSpec(memory_space=pltpu.VMEM)
SMEM = pl.BlockSpec(memory_space=pltpu.SMEM)
ANY = pl.BlockSpec(memory_space=pl.ANY)


def call(kernel, name, out_shape, in_specs, scratch_shapes=(), out_specs=None):
    kwargs = {} if out_specs is None else {"out_specs": out_specs}
    return pl.pallas_call(
        kernel,
        out_shape=out_shape,
        in_specs=in_specs,
        scratch_shapes=scratch_shapes,
        compiler_params=pltpu.CompilerParams(vmem_limit_bytes=VMEM_LIMIT),
        name=name,
        **kwargs,
    )


def swap_mate(array):
    return lax.ppermute(array, AXES, [(i, i ^ 1) for i in range(lax.axis_size(AXES))])


def swap_next(array):
    return lax.ppermute(array, AXES, [(i, i + 1 if i % 2 else i - 1) for i in range(1, lax.axis_size(AXES) - 1)])


def per_device(coords, noise_var, pair_list, probes):
    rows, here = probes.shape
    links, blocks = pair_list.shape
    length = here // blocks
    span = links * length
    noise = noise_var.reshape(1, here)

    whole = jax.ShapeDtypeStruct((rows, here), F32)
    part = jax.ShapeDtypeStruct((rows, span), F32)
    packed = jax.ShapeDtypeStruct((rows + 8, span), F32)
    wide_packed = jax.ShapeDtypeStruct((rows + 16, span), F32)
    wide_part = jax.ShapeDtypeStruct((rows + 8, span), F32)
    tiled_part = jax.ShapeDtypeStruct((rows // 8 * (span // 128) + 1, 8, 128), F32)
    sums_table = jax.ShapeDtypeStruct((rows, 128), F32)
    local_table = jax.ShapeDtypeStruct((here, here), BF16)
    halo_table = jax.ShapeDtypeStruct((span, span), BF16)
    local_halves = pltpu.VMEM((2 * rows, here), BF16)
    halo_halves = pltpu.VMEM((2 * rows, span), BF16)

    to_mate, to_next, own = call(
        pack_kernel,
        "pack",
        (packed, wide_packed, jax.ShapeDtypeStruct((8, here), F32)),
        [ANY, ANY, ANY],
        [pltpu.VMEM((3, here), F32), pltpu.SMEM((links, blocks), jnp.int32), pltpu.SemaphoreType.DMA((4,))],
    )(coords, pair_list, probes)
    mate, beyond = swap_mate(to_mate), swap_next(to_next)
    k_high, k_low, partial, first = call(
        functools.partial(local_first_kernel, links=links),
        "local_first",
        (local_table, local_table, whole, whole),
        [VMEM, VMEM, ANY],
        [
            local_halves,
            pltpu.VMEM((3, here, 128), F32),
            pltpu.VMEM((3 + blocks, 8, here), F32),
            pltpu.SemaphoreType.DMA((1,)),
        ],
    )(own, noise, probes)
    halo_scratch = [halo_halves, pltpu.VMEM((3 + links, 8, span), F32)]
    early_table = jax.ShapeDtypeStruct((span - length, span - length), BF16)
    late_table = jax.ShapeDtypeStruct((span, length), BF16)
    halo_columns_of = jax.ShapeDtypeStruct((3, span, 128), F32)
    early_high, early_low, partial, to_next, mate_columns = call(
        functools.partial(mate_first_kernel, links=links),
        "mate_first",
        (early_table, early_table, whole, wide_part, halo_columns_of),
        [VMEM] * 3,
        halo_scratch,
    )(own, partial, mate)
    ahead = swap_next(to_next)
    late_high, late_low, next_high, next_low, second, to_mate = call(
        functools.partial(next_first_kernel, links=links),
        "next_first",
        (late_table, late_table, halo_table, halo_table, whole, part),
        [VMEM] * 5,
        halo_scratch + halo_scratch + [pltpu.VMEM((3, span, 128), F32)],
    )(own, partial, mate, mate_columns, beyond)

    mate = swap_mate(to_mate)
    partial = call(
        functools.partial(local_second_kernel, length=length), "local_second", whole, [VMEM] * 4, [local_halves]
    )(noise, second, k_high, k_low)
    partial, to_next = call(
        functools.partial(mate_second_kernel, links=links), "mate_second", (whole, tiled_part), [VMEM] * 4, [halo_halves]
    )(partial, mate, early_high, early_low)
    after = swap_next(to_next)
    third, to_mate = call(
        functools.partial(next_second_kernel, links=links),
        "next_second",
        (whole, part),
        [VMEM] * 8,
        [halo_halves, pltpu.VMEM((rows, span), F32)],
    )(partial, first, mate, ahead, late_high, late_low, next_high, next_low)

    mate = swap_mate(to_mate)
    partial, given, table = call(
        functools.partial(local_third_kernel, length=length),
        "local_third",
        (whole, part, sums_table),
        [VMEM] * 8,
        [local_halves, halo_halves],
    )(noise, first, second, third, k_high, k_low, next_high, next_low)
    regions, subs = lax.axis_size("region"), lax.axis_size("sub")
    partial = call(
        functools.partial(mate_third_kernel, links=links), "mate_third", whole, [VMEM] * 6, [halo_halves]
    )(partial, mate, early_high, early_low, late_high, late_low)
    fourth, sums = call(
        functools.partial(next_third_kernel, links=links),
        "next_third",
        (whole, jax.ShapeDtypeStruct((regions, 4, 128), F32)),
        [VMEM] * 7,
        [halo_halves],
    )(partial, after, given, next_high, next_low, third, table)

    sums = jnp.sum(lax.all_to_all(sums, "region", 0, 0), axis=0)
    sums = lax.all_to_all(jnp.broadcast_to(sums[None], (subs, 4, 128)), "sub", 0, 0)
    solution, residual, good = call(
        finish_kernel,
        "finish",
        (whole, whole, jax.ShapeDtypeStruct((1, 1), F32)),
        [VMEM] * 5,
        out_specs=(VMEM, VMEM, SMEM),
    )(sums, first, second, third, fourth)

    def again(state):
        solution, residual = plain(coords, noise_var, pair_list, probes)
        return jnp.ones_like(state[0]), solution, residual

    _, solution, residual = lax.while_loop(lambda state: state[0][0, 0] < 0.5, again, (good, solution, residual))
    return solution, residual


def solution(mesh):
    in_specs = (P(None, AXES), P(AXES), P(None, AXES), P(None, AXES))
    out_specs = (P(None, AXES), P(None, AXES))
    return jax.shard_map(per_device, mesh=mesh, in_specs=in_specs, out_specs=out_specs, check_vma=False)
```

```python
import functools

import jax
import jax.numpy as jnp
from jax import lax
from jax.experimental import pallas as pl
from jax.experimental.pallas import tpu as pltpu
from jax.sharding import PartitionSpec as P

ITERS = 3
AXES = ("region", "sub")
SHIFT = 6.0
SCALE = 1.0 / 256.0
FAR = 65536.0
MAX_AMP = 100.0
MAX_NORM = 30.0
F32 = jnp.float32
BF16 = jnp.bfloat16
VMEM_LIMIT = 40 * 1024 * 1024


def shifted(array, by):
    count = lax.axis_size(AXES)
    pairs = [(i, i + by) for i in range(count) if 0 <= i + by < count]
    return lax.ppermute(array, AXES, pairs)


def wendland(left, right):
    squared = (left[0][..., :, None] - right[0][..., None, :]) ** 2
    squared = squared + (left[1][..., :, None] - right[1][..., None, :]) ** 2
    squared = squared + (left[2][..., :, None] - right[2][..., None, :]) ** 2
    distance = jnp.sqrt(squared)
    support = jnp.maximum(1.0 - distance, 0.0)
    return support**4 * (4.0 * distance + 1.0)


def squares(residual):
    return lax.psum(jnp.sum(residual * residual, axis=1), AXES)


def plain(coords, noise_var, pair_list, probes):
    probe_count, points_here = probes.shape
    links = pair_list.shape[0]
    blocks_here = pair_list.shape[1]
    block_len = points_here // blocks_here
    span_cols = links * block_len
    local_c = coords.reshape(3, blocks_here, block_len)
    weights = pair_list.astype(F32)
    ahead_c = shifted(coords[:, :span_cols], -1)
    ext_c = jnp.concatenate([local_c, ahead_c.reshape(3, links, block_len)], axis=1)

    def step(_, state):
        solution, residual, direction, res_norm = state
        ahead_v = shifted(direction[:, :span_cols], -1)
        ext_v = jnp.concatenate([direction, ahead_v], axis=1).reshape(probe_count, blocks_here + links, block_len)
        local_v = ext_v[:, :blocks_here]
        result = (noise_var[None, :] * direction).reshape(probe_count, blocks_here, block_len)
        spill = jnp.zeros((probe_count, blocks_here + links, block_len), F32)
        for offset in range(links + 1):
            kernel_block = wendland(local_c, ext_c[:, offset : offset + blocks_here])
            if offset > 0:
                kernel_block = kernel_block * weights[offset - 1][:, None, None]
            result = result + jnp.einsum(
                "pbj,bij->pbi", ext_v[:, offset : offset + blocks_here], kernel_block, precision=lax.Precision.HIGHEST
            )
            if offset > 0:
                spill = spill.at[:, offset : offset + blocks_here].add(
                    jnp.einsum("pbi,bij->pbj", local_v, kernel_block, precision=lax.Precision.HIGHEST)
                )
        result = result + spill[:, :blocks_here]
        result = result.at[:, :links].add(shifted(spill[:, blocks_here:], 1))
        product = result.reshape(probe_count, points_here)
        step_size = res_norm / lax.psum(jnp.sum(direction * product, axis=1), AXES)
        solution = solution + step_size[:, None] * direction
        residual = residual - step_size[:, None] * product
        next_norm = squares(residual)
        direction = residual + (next_norm / res_norm)[:, None] * direction
        return solution, residual, direction, next_norm

    state = (jnp.zeros_like(probes), probes, probes, squares(probes))
    solution, residual, _, _ = lax.fori_loop(0, ITERS, step, state)
    return solution, residual


def is_right(mate):
    return lax.axis_index("sub") % 2 == (0 if mate else 1)


def own_place(right, blocks, links, length, n):
    return pl.multiple_of(jnp.where(right, blocks - 1 - links + n, links - n) * length, 128)


def halo_place(right, links, length, h):
    return pl.multiple_of(jnp.where(right, h, links - 1 - h) * length, 128)


def send_place(right, here, span):
    return pl.multiple_of(jnp.where(right, here - span, 0), 128)


def split(value):
    high = value.astype(BF16)
    return high, (value - high.astype(F32)).astype(BF16)


def start_all(copies):
    for copy in copies:
        copy.start()
    return copies


def pack_kernel(coords, pair, noise, probes, to_mate, to_next, own, points, flags, variance, sem):
    links, blocks = pair.shape
    here = coords.shape[1]
    length = here // blocks
    rows, span = probes.shape[0], links * length
    place = [send_place(is_right(mate), here, span) for mate in (True, False)]
    copies = start_all(
        [
            pltpu.make_async_copy(pair, flags, sem.at[0]),
            pltpu.make_async_copy(coords, points, sem.at[1]),
            pltpu.make_async_copy(noise, variance, sem.at[4]),
            pltpu.make_async_copy(probes.at[:, pl.ds(place[0], span)], to_mate.at[0:rows], sem.at[2]),
            pltpu.make_async_copy(probes.at[:, pl.ds(place[1], span)], to_next.at[0:rows], sem.at[3]),
        ]
    )
    for copy in copies[0:3]:
        copy.wait()
    right = is_right(True)
    extra = [points[...]]
    for k in range(links):
        flag = [flags[k, b].astype(F32) for b in range(blocks)]
        extra.append(jnp.concatenate([jnp.full((1, length), f, F32) for f in flag], axis=1))
    extra = jnp.concatenate(extra + [variance[...], jnp.zeros((8 - 4 - links, here), F32)], axis=0)
    own[...] = extra
    low, high = extra[:, 0:span], extra[:, here - span :]
    to_mate[rows : rows + 8, :] = jnp.where(right, high, low)
    to_next[rows : rows + 8, :] = jnp.where(right, low, high)
    to_next[rows + 8 :, :] = jnp.zeros((to_next.shape[0] - rows - 8, span), F32)
    copies[3].wait()
    copies[4].wait()


def column_steps(columns, at, load):
    def fill(d, turned):
        size = turned.shape[0]
        columns[d, at : at + size, :] = jnp.broadcast_to(turned[:, d : d + 1], (size, 128))

    def step():
        turned = jnp.transpose(load())
        for d in range(3):
            fill(d, turned)

    return [step]


def fill_strip(k_high, k_low, to_row, columns, from_row, strip, rows, x, at, first):
    column = [columns[d, pl.ds(from_row, strip), :].reshape(strip // 8, 8, 128) for d in range(3)]
    for lane in range(at.start, at.stop, 128):
        squared = None
        for d in range(3):
            away = column[d] - rows[d if d else x, :, lane : lane + 128][None]
            squared = away * away if squared is None else squared + away * away
        squared = jnp.maximum(squared, 1e-30)
        distance = squared * lax.rsqrt(squared)
        support = jnp.maximum(4.0 - distance, 0.0)
        support = support * support
        value = support * support * (distance + 1.0)
        top, rest = split(value.reshape(strip, 128))
        to = slice(first + lane - at.start, first + lane - at.start + 128)
        k_high[pl.ds(to_row, strip), to] = top
        k_low[pl.ds(to_row, strip), to] = rest


def fill_tiles(k_high, k_low, to_row, columns, from_row, count, rows, x, at, first, beside=()):
    strip = 64 if at.stop - at.start <= 4 * 128 else 32
    if not beside:

        def body(s, _):
            step = pl.multiple_of(s * strip, strip)
            fill_strip(k_high, k_low, to_row + step, columns, from_row + step, strip, rows, x, at, first)
            return 0

        lax.fori_loop(0, count // strip, body, 0)
        return
    done = 0
    for s in range(count // strip):
        step = s * strip
        fill_strip(k_high, k_low, to_row + step, columns, from_row + step, strip, rows, x, at, first)
        while done < len(beside) * (s + 1) * strip // count:
            beside[done]()
            done += 1


def store_halves(halves, at, vector):
    rows, size = vector.shape
    top, rest = split(vector * SCALE)
    halves[0:rows, at : at + size] = top
    halves[rows : 2 * rows, at : at + size] = rest


def multiply(both, k_high, k_low, turned=False):
    rows = both.shape[0] // 2
    dims = (((1,), (1 if turned else 0,)), ((), ()))
    most = lax.dot_general(both, k_high, dims, preferred_element_type=F32)
    rest = lax.dot_general(both[0:rows], k_low, dims, preferred_element_type=F32)
    return most[0:rows] + (most[rows : 2 * rows] + rest)


def local_product(own, vector, k_high, k_low, out, halves, length):
    here = vector.shape[1]
    noise = own[3 + here // length - 1 : 3 + here // length, :]
    store_halves(halves, 0, vector[...])
    for start in range(0, here, length):
        stop = start + length
        at, before, after = slice(start, stop), slice(0, stop), slice(stop, here)
        value = multiply(halves[:, before], k_high[before, at], k_low[before, at])
        if stop < here:
            value = value + multiply(halves[:, after], k_high[at, after], k_low[at, after], turned=True)
        out[:, at] = value + (noise[:, at] - SHIFT) * vector[:, at]


def row_steps(halves, k_high, k_low, out, start, length):
    stop, here = start + length, out.shape[1]
    steps = []

    def natural(at):
        def step():
            out[:, at] = out[:, at] + multiply(halves[:, start:stop], k_high[start:stop, at], k_low[start:stop, at])

        return step

    def mirrored(at):
        def step():
            value = multiply(halves[:, at], k_high[start:stop, at], k_low[start:stop, at], turned=True)
            out[:, start:stop] = out[:, start:stop] + value

        return step

    for at in range(start, here, length):
        steps.append(natural(slice(at, at + length)))
    for at in range(stop, here, length):
        steps.append(mirrored(slice(at, at + length)))
    return steps


def local_first_kernel(own, probes, k_high, k_low, out, first, halves, columns, rows, sem, *, links):
    noise = own[3 + links : 4 + links, :]
    here = own.shape[1]
    blocks = links + 1
    length = here // blocks
    copy = pltpu.make_async_copy(probes, first, sem.at[0])
    copy.start()
    for d in range(1, 3):
        rows[d] = jnp.broadcast_to(4.0 * own[d : d + 1, :], rows.shape[1:])
    steps = []
    for j in range(blocks):
        half = length // 2
        for at in (j * length, j * length + half):
            steps += column_steps(columns, at, lambda at=at: 4.0 * own[:, at : at + half])
    for step in steps[0:2]:
        step()
    steps = steps[2:]
    for i in range(blocks):
        for j in range(i, blocks):
            at = slice(j * length, (j + 1) * length)
            moved = 4.0 * own[0:1, at]
            if j > i:
                flag = own[2 + j - i : 3 + j - i, i * length : (i + 1) * length]
                moved = jnp.where(flag == 1.0, moved, moved + FAR)
            rows[3 + i, :, at] = jnp.broadcast_to(moved, (8, length))
        start = i * length
        fill_tiles(k_high, k_low, start, columns, start, length, rows, 3 + i, slice(start, here), start, steps)
        if i == 0:
            copy.wait()
            store_halves(halves, 0, first[...])
            out[...] = (noise - SHIFT) * first[...]
        steps = row_steps(halves, k_high, k_low, out, start, length)
    for step in steps:
        step()


def halo_columns(right, received, at, columns, links, h):
    length = received.shape[1] // links
    half = length // 2
    steps = []
    for part in range(2):
        place = pl.ds(pl.multiple_of(halo_place(right, links, length, h) + part * half, 128), half)
        steps += column_steps(columns, h * length + part * half, lambda place=place: 4.0 * received[at : at + 8, place])
    return steps


def own_rows(right, own, received, at, rows, links, pieces):
    length = received.shape[1] // links
    blocks = own.shape[1] // length
    for n in sorted({n for _, ns in pieces for n in ns}):
        mine = pl.ds(own_place(right, blocks, links, length, n), length)
        lanes = slice((n - 1) * length, n * length)
        for d in range(1, 3):
            rows[d, :, lanes] = jnp.broadcast_to(4.0 * own[d : d + 1, mine], (8, length))
        for h, ns in pieces:
            if n not in ns:
                continue
            k = links - n + h
            ours = own[3 + k : 4 + k, mine]
            theirs = received[at + 3 + k : at + 4 + k, pl.ds(halo_place(right, links, length, h), length)]
            coord = 4.0 * own[0:1, mine]
            coord = jnp.where(jnp.where(right, ours, theirs) == 1.0, coord, coord + FAR)
            rows[3 + h, :, lanes] = jnp.broadcast_to(coord, (8, length))


def fill_halo(right, received, columns, pieces, out, halves, rows, links, beside):
    probe_count = out.shape[0]
    length = received.shape[1] // links
    blocks = out.shape[1] // length
    for h in range(max(h for h, _, _ in pieces) + 1):
        place = pl.ds(halo_place(right, links, length, h), length)
        store_halves(halves, h * length, received[0:probe_count, place])

    def product(h, n, k_high, k_low, lanes):
        own = pl.ds(own_place(right, blocks, links, length, n), length)
        at = slice(h * length, (h + 1) * length)

        def step():
            out[:, own] = out[:, own] + multiply(halves[:, at], k_high[:, lanes], k_low[:, lanes])

        return step

    for h, ns, (k_high, k_low) in pieces:
        lanes = slice((ns[0] - 1) * length, ns[-1] * length)
        fill_tiles(k_high, k_low, 0, columns, h * length, length, rows, 3 + h, lanes, 0, beside)
        beside = []
        for n in ns:
            beside.append(product(h, n, k_high, k_low, slice((n - ns[0]) * length, (n - ns[0] + 1) * length)))
    return beside


def part_of(tables, rows, lanes):
    return tuple(table.at[rows, lanes] for table in tables)


def early_tables(tables, links, length):
    return {n: part_of(tables, slice(0, n * length), slice((n - 1) * length, n * length)) for n in range(1, links)}


def halo_product(right, load, tables, out, halves, links):
    length = halves.shape[1] // links
    blocks = out.shape[1] // length
    for h in range(max(tables)):
        store_halves(halves, h * length, load(pl.ds(halo_place(right, links, length, h), length)))
    for n, (k_high, k_low) in tables.items():
        own = pl.ds(own_place(right, blocks, links, length, n), length)
        out[:, own] = out[:, own] + multiply(halves[:, 0 : n * length], k_high[...], k_low[...])


def own_product(right, vector, tables, out, halves, blocks):
    span = out.shape[1]
    length = vector.shape[1] // blocks
    links = span // length
    k_high, k_low = tables
    for n in range(1, links + 1):
        own = pl.ds(own_place(right, blocks, links, length, n), length)
        store_halves(halves, (n - 1) * length, vector[:, own])
    for h in range(links):
        deep, at = slice(h * length, span), slice(h * length, (h + 1) * length)
        place = pl.ds(halo_place(right, links, length, h), length)
        out[:, place] = multiply(halves[:, deep], k_high[at, deep], k_low[at, deep], turned=True)


def store_send(right, vector, send):
    here, span = vector.shape[1], send.shape[1]
    rows = vector.shape[0]
    send[0:rows, :] = vector[:, pl.ds(send_place(right, here, span), span)]
    if send.shape[0] > rows:
        send[rows:, :] = jnp.zeros((send.shape[0] - rows, span), F32)


def store_tiles(right, vector, send):
    here, count = vector.shape[1], vector.shape[0] // 8
    wide = (send.shape[0] - 1) // count
    start = send_place(right, here, wide * 128)
    for c in range(wide):
        lanes = pl.ds(pl.multiple_of(start + c * 128, 128), 128)
        send[c * count : (c + 1) * count] = vector[:, lanes].reshape(count, 8, 128)
    send[wide * count :] = jnp.zeros((1, 8, 128), F32)


def load_tiles(received, rows, at):
    count = rows // 8
    parts = []
    for c in range(at.size // 128):
        tile = (at.start // 128 + c) * count
        parts.append(received[pl.ds(tile, count)].reshape(rows, 128))
    return jnp.concatenate(parts, axis=1)


def mate_first_kernel(own, partial, received, k_high, k_low, out, to_next, columns, halves, rows, *, links):
    right = is_right(True)
    length = halves.shape[1] // links
    at = out.shape[0]
    pieces = [(h, range(h + 1, links)) for h in range(links - 1)]
    steps = []
    for h in range(links):
        steps += halo_columns(right, received, at, columns, links, h)
    for step in steps[0:2]:
        step()
    own_rows(right, own, received, at, rows, links, pieces)
    out[...] = partial[...]
    tables = (k_high, k_low)
    pieces = [
        (h, ns, part_of(tables, slice(h * length, (h + 1) * length), slice(h * length, (links - 1) * length)))
        for h, ns in pieces
    ]
    for step in fill_halo(right, received, columns, pieces, out, halves, rows, links, steps[2:]):
        step()
    store_send(is_right(False), out, to_next)


def next_first_kernel(
    own,
    partial,
    mate,
    mate_columns,
    received,
    mate_high,
    mate_low,
    k_high,
    k_low,
    out,
    to_mate,
    mate_halves,
    mate_rows,
    halves,
    rows,
    columns,
    *,
    links,
):
    length = halves.shape[1] // links
    at = out.shape[0]
    out[...] = partial[...]
    left, right = is_right(True), is_right(False)
    late = [(h, range(links, links + 1)) for h in range(links)]
    all_of = [(h, range(h + 1, links + 1)) for h in range(links)]
    own_rows(left, own, mate, at, mate_rows, links, late)
    own_rows(right, own, received, at, rows, links, all_of)
    steps = []
    for h in range(links):
        steps += halo_columns(right, received, at, columns, links, h)
    tables = (mate_high, mate_low)
    pieces = [(h, ns, part_of(tables, slice(h * length, (h + 1) * length), slice(0, length))) for h, ns in late]
    steps = fill_halo(left, mate, mate_columns, pieces, out, mate_halves, mate_rows, links, steps)
    tables = (k_high, k_low)
    pieces = [
        (h, ns, part_of(tables, slice(h * length, (h + 1) * length), slice(h * length, links * length)))
        for h, ns in all_of
    ]
    for step in fill_halo(right, received, columns, pieces, out, halves, rows, links, steps):
        step()
    store_send(is_right(True), out, to_mate)


def add_sums(table, terms):
    lane = lax.broadcasted_iota(jnp.int32, table.shape, 1)
    for power, left, right in terms:
        part = None
        for at in range(0, left.shape[1], 128):
            term = left[:, at : at + 128] * right[:, at : at + 128]
            part = term if part is None else part + term
        table = jnp.where(lane == power, jnp.sum(part, axis=1, keepdims=True), table)
    return table


def local_second_kernel(own, second, k_high, k_low, out, halves, *, length):
    local_product(own, second, k_high, k_low, out, halves, length)


def local_third_kernel(
    own, first, second, third, k_high, k_low, next_high, next_low, out, given, table, halves, own_halves, *, length
):
    local_product(own, third, k_high, k_low, out, halves, length)
    own_product(is_right(False), second, (next_high, next_low), given, own_halves, out.shape[1] // length)
    terms = ((0, first, first), (1, first, second), (2, second, second), (3, second, third), (4, third, third))
    table[...] = add_sums(jnp.zeros(table.shape, F32), terms)


def mate_second_kernel(partial, mate, k_high, k_low, out, to_next, halves, *, links):
    length = halves.shape[1] // links
    out[...] = partial[...]
    tables = early_tables((k_high, k_low), links, length)
    halo_product(is_right(True), lambda at: mate[:, at], tables, out, halves, links)
    store_tiles(is_right(False), out, to_next)


def next_tables(tables, links, length):
    return {n: part_of(tables, slice(0, n * length), slice((n - 1) * length, n * length)) for n in range(1, links + 1)}


def next_second_kernel(
    partial, first, mate, ahead, mate_high, mate_low, k_high, k_low, out, to_mate, halves, given, *, links
):
    length = halves.shape[1] // links
    right = is_right(False)
    out[...] = partial[...]
    halo_product(is_right(True), lambda at: mate[:, at], {links: (mate_high, mate_low)}, out, halves, links)
    own_product(right, first, (k_high, k_low), given, halves, links + 1)
    tables = next_tables((k_high, k_low), links, length)
    halo_product(right, received_share(ahead, given), tables, out, halves, links)
    store_send(is_right(True), out, to_mate)


def received_share(received, given):
    return lambda at: received[0 : given.shape[0], at] + given[:, at]


def mate_third_kernel(partial, mate, early_high, early_low, late_high, late_low, out, halves, *, links):
    length = halves.shape[1] // links
    out[...] = partial[...]
    tables = early_tables((early_high, early_low), links, length)
    tables[links] = (late_high, late_low)
    halo_product(is_right(True), lambda at: mate[:, at], tables, out, halves, links)


def next_third_kernel(partial, after, given, k_high, k_low, third, table, out, sums, halves, *, links):
    length = halves.shape[1] // links
    out[...] = partial[...]
    tables = next_tables((k_high, k_low), links, length)
    share = lambda at: load_tiles(after, out.shape[0], at) + given[:, at]
    halo_product(is_right(False), share, tables, out, halves, links)
    full = add_sums(table[...], ((5, third, out), (6, out, out)))
    turned = jnp.transpose(full)[0:8, :]
    compact = jnp.concatenate([turned[0:4], turned[4:8]], axis=1)
    sums[...] = jnp.broadcast_to(compact[None], sums.shape)


def polynomials(moment):
    def dot(p, q):
        total, size = 0.0, 0.0
        for i, x in enumerate(p):
            for j, y in enumerate(q):
                term = x * y * moment[i + j]
                total, size = total + term, size + jnp.abs(term)
        return total, size

    def add(p, q, factor):
        count = max(len(p), len(q))
        p, q = p + [0.0] * (count - len(p)), q + [0.0] * (count - len(q))
        return [x + factor * y for x, y in zip(p, q)]

    one = jnp.ones_like(moment[0])
    solution, residual, direction = [jnp.zeros_like(one)], [one], [one]
    norm = moment[0]
    good = norm > 0.0
    for step in range(ITERS):
        image = add([0.0 * one] + direction, direction, SHIFT)
        curvature, size = dot(direction, image)
        good = good & (size <= MAX_AMP * curvature)
        step_size = norm / curvature
        solution = add(solution, direction, step_size)
        residual = add(residual, image, -step_size)
        new, size = dot(residual, residual)
        if step < ITERS - 1:
            good = good & (size <= MAX_AMP * new)
            direction = add(residual, direction, new / norm)
        norm = new
    size = sum(jnp.abs(x) * jnp.sqrt(moment[2 * i]) for i, x in enumerate(residual))
    good = good & (size * size <= MAX_NORM * MAX_NORM * norm)
    return solution, residual, good


def finish_kernel(sums, first, second, third, fourth, solution, residual, good):
    total = jnp.sum(sums[...], axis=0)
    rows = first.shape[0]
    moment = [total[k : k + 1, 0:rows] for k in range(4)] + [total[k : k + 1, rows : 2 * rows] for k in range(3)]
    mix_solution, mix_residual, fine = polynomials(moment)
    table = jnp.concatenate(mix_solution + mix_residual + [jnp.zeros_like(moment[0])], axis=0)
    table = jnp.concatenate([table, jnp.zeros_like(table)], axis=1)
    table = jnp.transpose(jnp.concatenate([table, jnp.zeros((120, 128), F32)], axis=0))[0:rows]
    basis = (first[...], second[...], third[...], fourth[...])

    def mix(at, count):
        total = table[:, at : at + 1] * basis[0]
        for k in range(1, count):
            total = total + table[:, at + k : at + k + 1] * basis[k]
        return total

    solution[...] = mix(0, ITERS)
    residual[...] = mix(ITERS, ITERS + 1)
    good[0, 0] = jnp.min(jnp.where(fine, 1.0, 0.0))


VMEM = pl.BlockSpec(memory_space=pltpu.VMEM)
SMEM = pl.BlockSpec(memory_space=pltpu.SMEM)
ANY = pl.BlockSpec(memory_space=pl.ANY)


def call(kernel, name, out_shape, in_specs, scratch_shapes=(), out_specs=None):
    kwargs = {} if out_specs is None else {"out_specs": out_specs}
    return pl.pallas_call(
        kernel,
        out_shape=out_shape,
        in_specs=in_specs,
        scratch_shapes=scratch_shapes,
        compiler_params=pltpu.CompilerParams(vmem_limit_bytes=VMEM_LIMIT),
        name=name,
        **kwargs,
    )


def swap_mate(array):
    return lax.ppermute(array, AXES, [(i, i ^ 1) for i in range(lax.axis_size(AXES))])


def swap_next(array):
    return lax.ppermute(array, AXES, [(i, i + 1 if i % 2 else i - 1) for i in range(1, lax.axis_size(AXES) - 1)])


def per_device(coords, noise_var, pair_list, probes):
    rows, here = probes.shape
    links, blocks = pair_list.shape
    length = here // blocks
    span = links * length
    noise = noise_var.reshape(1, here)

    whole = jax.ShapeDtypeStruct((rows, here), F32)
    part = jax.ShapeDtypeStruct((rows, span), F32)
    packed = jax.ShapeDtypeStruct((rows + 8, span), F32)
    wide_packed = jax.ShapeDtypeStruct((rows + 16, span), F32)
    wide_part = jax.ShapeDtypeStruct((rows + 8, span), F32)
    tiled_part = jax.ShapeDtypeStruct((rows // 8 * (span // 128) + 1, 8, 128), F32)
    sums_table = jax.ShapeDtypeStruct((rows, 128), F32)
    local_table = jax.ShapeDtypeStruct((here, here), BF16)
    halo_table = jax.ShapeDtypeStruct((span, span), BF16)
    local_halves = pltpu.VMEM((2 * rows, here), BF16)
    halo_halves = pltpu.VMEM((2 * rows, span), BF16)

    to_mate, to_next, own = call(
        pack_kernel,
        "pack",
        (packed, wide_packed, jax.ShapeDtypeStruct((8, here), F32)),
        [ANY] * 4,
        [
            pltpu.VMEM((3, here), F32),
            pltpu.SMEM((links, blocks), jnp.int32),
            pltpu.VMEM((1, here), F32),
            pltpu.SemaphoreType.DMA((5,)),
        ],
    )(coords, pair_list, noise, probes)
    mate, beyond = swap_mate(to_mate), swap_next(to_next)
    k_high, k_low, partial, first = call(
        functools.partial(local_first_kernel, links=links),
        "local_first",
        (local_table, local_table, whole, whole),
        [VMEM, ANY],
        [
            local_halves,
            pltpu.VMEM((3, here, 128), F32),
            pltpu.VMEM((3 + blocks, 8, here), F32),
            pltpu.SemaphoreType.DMA((1,)),
        ],
    )(own, probes)
    halo_scratch = [halo_halves, pltpu.VMEM((3 + links, 8, span), F32)]
    early_table = jax.ShapeDtypeStruct((span - length, span - length), BF16)
    late_table = jax.ShapeDtypeStruct((span, length), BF16)
    halo_columns_of = jax.ShapeDtypeStruct((3, span, 128), F32)
    early_high, early_low, partial, to_next, mate_columns = call(
        functools.partial(mate_first_kernel, links=links),
        "mate_first",
        (early_table, early_table, whole, wide_part, halo_columns_of),
        [VMEM] * 3,
        halo_scratch,
    )(own, partial, mate)
    ahead = swap_next(to_next)
    late_high, late_low, next_high, next_low, second, to_mate = call(
        functools.partial(next_first_kernel, links=links),
        "next_first",
        (late_table, late_table, halo_table, halo_table, whole, part),
        [VMEM] * 5,
        halo_scratch + halo_scratch + [pltpu.VMEM((3, span, 128), F32)],
    )(own, partial, mate, mate_columns, beyond)

    mate = swap_mate(to_mate)
    partial = call(
        functools.partial(local_second_kernel, length=length), "local_second", whole, [VMEM] * 4, [local_halves]
    )(own, second, k_high, k_low)
    partial, to_next = call(
        functools.partial(mate_second_kernel, links=links), "mate_second", (whole, tiled_part), [VMEM] * 4, [halo_halves]
    )(partial, mate, early_high, early_low)
    after = swap_next(to_next)
    third, to_mate = call(
        functools.partial(next_second_kernel, links=links),
        "next_second",
        (whole, part),
        [VMEM] * 8,
        [halo_halves, pltpu.VMEM((rows, span), F32)],
    )(partial, first, mate, ahead, late_high, late_low, next_high, next_low)

    mate = swap_mate(to_mate)
    partial, given, table = call(
        functools.partial(local_third_kernel, length=length),
        "local_third",
        (whole, part, sums_table),
        [VMEM] * 8,
        [local_halves, halo_halves],
    )(own, first, second, third, k_high, k_low, next_high, next_low)
    regions, subs = lax.axis_size("region"), lax.axis_size("sub")
    partial = call(
        functools.partial(mate_third_kernel, links=links), "mate_third", whole, [VMEM] * 6, [halo_halves]
    )(partial, mate, early_high, early_low, late_high, late_low)
    fourth, sums = call(
        functools.partial(next_third_kernel, links=links),
        "next_third",
        (whole, jax.ShapeDtypeStruct((regions, 4, 128), F32)),
        [VMEM] * 7,
        [halo_halves],
    )(partial, after, given, next_high, next_low, third, table)

    sums = jnp.sum(lax.all_to_all(sums, "region", 0, 0), axis=0)
    sums = lax.all_to_all(jnp.broadcast_to(sums[None], (subs, 4, 128)), "sub", 0, 0)
    solution, residual, good = call(
        finish_kernel,
        "finish",
        (whole, whole, jax.ShapeDtypeStruct((1, 1), F32)),
        [VMEM] * 5,
        out_specs=(VMEM, VMEM, SMEM),
    )(sums, first, second, third, fourth)

    def again(state):
        solution, residual = plain(coords, noise_var, pair_list, probes)
        return jnp.ones_like(state[0]), solution, residual

    _, solution, residual = lax.while_loop(lambda state: state[0][0, 0] < 0.5, again, (good, solution, residual))
    return solution, residual


def solution(mesh):
    in_specs = (P(None, AXES), P(AXES), P(None, AXES), P(None, AXES))
    out_specs = (P(None, AXES), P(None, AXES))
    return jax.shard_map(per_device, mesh=mesh, in_specs=in_specs, out_specs=out_specs, check_vma=False)
```

```python
import functools

import jax
import jax.numpy as jnp
from jax import lax
from jax.experimental import pallas as pl
from jax.experimental.pallas import tpu as pltpu
from jax.sharding import PartitionSpec as P

ITERS = 3
AXES = ("region", "sub")
SHIFT = 6.0
SCALE = 1.0 / 256.0
FAR = 65536.0
MAX_AMP = 100.0
MAX_NORM = 30.0
F32 = jnp.float32
BF16 = jnp.bfloat16
VMEM_LIMIT = 40 * 1024 * 1024


def shifted(array, by):
    count = lax.axis_size(AXES)
    pairs = [(i, i + by) for i in range(count) if 0 <= i + by < count]
    return lax.ppermute(array, AXES, pairs)


def wendland(left, right):
    squared = (left[0][..., :, None] - right[0][..., None, :]) ** 2
    squared = squared + (left[1][..., :, None] - right[1][..., None, :]) ** 2
    squared = squared + (left[2][..., :, None] - right[2][..., None, :]) ** 2
    distance = jnp.sqrt(squared)
    support = jnp.maximum(1.0 - distance, 0.0)
    return support**4 * (4.0 * distance + 1.0)


def squares(residual):
    return lax.psum(jnp.sum(residual * residual, axis=1), AXES)


def plain(coords, noise_var, pair_list, probes):
    probe_count, points_here = probes.shape
    links = pair_list.shape[0]
    blocks_here = pair_list.shape[1]
    block_len = points_here // blocks_here
    span_cols = links * block_len
    local_c = coords.reshape(3, blocks_here, block_len)
    weights = pair_list.astype(F32)
    ahead_c = shifted(coords[:, :span_cols], -1)
    ext_c = jnp.concatenate([local_c, ahead_c.reshape(3, links, block_len)], axis=1)

    def step(_, state):
        solution, residual, direction, res_norm = state
        ahead_v = shifted(direction[:, :span_cols], -1)
        ext_v = jnp.concatenate([direction, ahead_v], axis=1).reshape(probe_count, blocks_here + links, block_len)
        local_v = ext_v[:, :blocks_here]
        result = (noise_var[None, :] * direction).reshape(probe_count, blocks_here, block_len)
        spill = jnp.zeros((probe_count, blocks_here + links, block_len), F32)
        for offset in range(links + 1):
            kernel_block = wendland(local_c, ext_c[:, offset : offset + blocks_here])
            if offset > 0:
                kernel_block = kernel_block * weights[offset - 1][:, None, None]
            result = result + jnp.einsum(
                "pbj,bij->pbi", ext_v[:, offset : offset + blocks_here], kernel_block, precision=lax.Precision.HIGHEST
            )
            if offset > 0:
                spill = spill.at[:, offset : offset + blocks_here].add(
                    jnp.einsum("pbi,bij->pbj", local_v, kernel_block, precision=lax.Precision.HIGHEST)
                )
        result = result + spill[:, :blocks_here]
        result = result.at[:, :links].add(shifted(spill[:, blocks_here:], 1))
        product = result.reshape(probe_count, points_here)
        step_size = res_norm / lax.psum(jnp.sum(direction * product, axis=1), AXES)
        solution = solution + step_size[:, None] * direction
        residual = residual - step_size[:, None] * product
        next_norm = squares(residual)
        direction = residual + (next_norm / res_norm)[:, None] * direction
        return solution, residual, direction, next_norm

    state = (jnp.zeros_like(probes), probes, probes, squares(probes))
    solution, residual, _, _ = lax.fori_loop(0, ITERS, step, state)
    return solution, residual


def is_right(mate):
    return lax.axis_index("sub") % 2 == (0 if mate else 1)


def own_place(right, blocks, links, length, n):
    return pl.multiple_of(jnp.where(right, blocks - 1 - links + n, links - n) * length, 128)


def halo_place(right, links, length, h):
    return pl.multiple_of(jnp.where(right, h, links - 1 - h) * length, 128)


def send_place(right, here, span):
    return pl.multiple_of(jnp.where(right, here - span, 0), 128)


def split(value):
    high = value.astype(BF16)
    return high, (value - high.astype(F32)).astype(BF16)


def start_all(copies):
    for copy in copies:
        copy.start()
    return copies


def pack_kernel(coords, pair, noise, probes, to_mate, to_next, own, points, flags, variance, sem):
    links, blocks = pair.shape
    here = coords.shape[1]
    length = here // blocks
    rows, span = probes.shape[0], links * length
    place = [send_place(is_right(mate), here, span) for mate in (True, False)]
    copies = start_all(
        [
            pltpu.make_async_copy(pair, flags, sem.at[0]),
            pltpu.make_async_copy(coords, points, sem.at[1]),
            pltpu.make_async_copy(noise, variance, sem.at[4]),
            pltpu.make_async_copy(probes.at[:, pl.ds(place[0], span)], to_mate.at[0:rows], sem.at[2]),
            pltpu.make_async_copy(probes.at[:, pl.ds(place[1], span)], to_next.at[0:rows], sem.at[3]),
        ]
    )
    for copy in copies[0:3]:
        copy.wait()
    right = is_right(True)
    extra = [points[...]]
    for k in range(links):
        flag = [flags[k, b].astype(F32) for b in range(blocks)]
        extra.append(jnp.concatenate([jnp.full((1, length), f, F32) for f in flag], axis=1))
    extra = jnp.concatenate(extra + [variance[...], jnp.zeros((8 - 4 - links, here), F32)], axis=0)
    own[...] = extra
    low, high = extra[:, 0:span], extra[:, here - span :]
    to_mate[rows : rows + 8, :] = jnp.where(right, high, low)
    to_next[rows : rows + 8, :] = jnp.where(right, low, high)
    to_next[rows + 8 :, :] = jnp.zeros((to_next.shape[0] - rows - 8, span), F32)
    copies[3].wait()
    copies[4].wait()


def column_steps(columns, at, load):
    def fill(d, turned):
        size = turned.shape[0]
        columns[d, at : at + size, :] = jnp.broadcast_to(turned[:, d : d + 1], (size, 128))

    def step():
        turned = jnp.transpose(load())
        for d in range(3):
            fill(d, turned)

    return [step]


def fill_strip(k_high, k_low, to_row, columns, from_row, strip, rows, x, at, first):
    column = [columns[d, pl.ds(from_row, strip), :].reshape(strip // 8, 8, 128) for d in range(3)]
    for lane in range(at.start, at.stop, 128):
        squared = None
        for d in range(3):
            away = column[d] - rows[d if d else x, :, lane : lane + 128][None]
            squared = away * away if squared is None else squared + away * away
        squared = jnp.maximum(squared, 1e-30)
        distance = squared * lax.rsqrt(squared)
        support = jnp.maximum(4.0 - distance, 0.0)
        support = support * support
        value = support * support * (distance + 1.0)
        top, rest = split(value.reshape(strip, 128))
        to = slice(first + lane - at.start, first + lane - at.start + 128)
        k_high[pl.ds(to_row, strip), to] = top
        k_low[pl.ds(to_row, strip), to] = rest


def fill_tiles(k_high, k_low, to_row, columns, from_row, count, rows, x, at, first, beside=()):
    strip = 64 if at.stop - at.start <= 4 * 128 else 32
    if not beside:

        def body(s, _):
            step = pl.multiple_of(s * strip, strip)
            fill_strip(k_high, k_low, to_row + step, columns, from_row + step, strip, rows, x, at, first)
            return 0

        lax.fori_loop(0, count // strip, body, 0)
        return
    done = 0
    for s in range(count // strip):
        step = s * strip
        fill_strip(k_high, k_low, to_row + step, columns, from_row + step, strip, rows, x, at, first)
        while done < len(beside) * (s + 1) * strip // count:
            beside[done]()
            done += 1


def store_halves(halves, at, vector):
    rows, size = vector.shape
    top, rest = split(vector * SCALE)
    halves[0:rows, at : at + size] = top
    halves[rows : 2 * rows, at : at + size] = rest


def multiply(both, k_high, k_low, turned=False):
    rows = both.shape[0] // 2
    dims = (((1,), (1 if turned else 0,)), ((), ()))
    most = lax.dot_general(both, k_high, dims, preferred_element_type=F32)
    rest = lax.dot_general(both[0:rows], k_low, dims, preferred_element_type=F32)
    return most[0:rows] + (most[rows : 2 * rows] + rest)


def local_product(own, vector, k_high, k_low, out, halves, length):
    here = vector.shape[1]
    noise = own[3 + here // length - 1 : 3 + here // length, :]
    store_halves(halves, 0, vector[...])
    for start in range(0, here, length):
        stop = start + length
        at, before, after = slice(start, stop), slice(0, stop), slice(stop, here)
        value = multiply(halves[:, before], k_high[before, at], k_low[before, at])
        if stop < here:
            value = value + multiply(halves[:, after], k_high[at, after], k_low[at, after], turned=True)
        out[:, at] = value + (noise[:, at] - SHIFT) * vector[:, at]


def row_steps(halves, k_high, k_low, out, start, length):
    stop, here = start + length, out.shape[1]
    steps = []

    def natural(at):
        def step():
            out[:, at] = out[:, at] + multiply(halves[:, start:stop], k_high[start:stop, at], k_low[start:stop, at])

        return step

    def mirrored(at):
        def step():
            value = multiply(halves[:, at], k_high[start:stop, at], k_low[start:stop, at], turned=True)
            out[:, start:stop] = out[:, start:stop] + value

        return step

    for at in range(start, here, length):
        steps.append(natural(slice(at, at + length)))
    for at in range(stop, here, length):
        steps.append(mirrored(slice(at, at + length)))
    return steps


def local_first_kernel(own, probes, k_high, k_low, out, first, halves, columns, rows, sem, *, links):
    noise = own[3 + links : 4 + links, :]
    here = own.shape[1]
    blocks = links + 1
    length = here // blocks
    copy = pltpu.make_async_copy(probes, first, sem.at[0])
    copy.start()
    for d in range(1, 3):
        rows[d] = jnp.broadcast_to(4.0 * own[d : d + 1, :], rows.shape[1:])
    steps = []
    for j in range(blocks):
        half = length // 2
        for at in (j * length, j * length + half):
            steps += column_steps(columns, at, lambda at=at: 4.0 * own[:, at : at + half])
    for step in steps[0:2]:
        step()
    steps = steps[2:]
    for i in range(blocks):
        for j in range(i, blocks):
            at = slice(j * length, (j + 1) * length)
            moved = 4.0 * own[0:1, at]
            if j > i:
                flag = own[2 + j - i : 3 + j - i, i * length : (i + 1) * length]
                moved = jnp.where(flag == 1.0, moved, moved + FAR)
            rows[3 + i, :, at] = jnp.broadcast_to(moved, (8, length))
        start = i * length
        fill_tiles(k_high, k_low, start, columns, start, length, rows, 3 + i, slice(start, here), start, steps)
        if i == 0:
            copy.wait()
            store_halves(halves, 0, first[...])
            out[...] = (noise - SHIFT) * first[...]
        steps = row_steps(halves, k_high, k_low, out, start, length)
    for step in steps:
        step()


def halo_columns(right, received, at, columns, links, h):
    length = received.shape[1] // links
    half = length // 2
    steps = []
    for part in range(2):
        place = pl.ds(pl.multiple_of(halo_place(right, links, length, h) + part * half, 128), half)
        steps += column_steps(columns, h * length + part * half, lambda place=place: 4.0 * received[at : at + 8, place])
    return steps


def own_rows(right, own, received, at, rows, links, pieces):
    length = received.shape[1] // links
    blocks = own.shape[1] // length
    for n in sorted({n for _, ns in pieces for n in ns}):
        mine = pl.ds(own_place(right, blocks, links, length, n), length)
        lanes = slice((n - 1) * length, n * length)
        for d in range(1, 3):
            rows[d, :, lanes] = jnp.broadcast_to(4.0 * own[d : d + 1, mine], (8, length))
        for h, ns in pieces:
            if n not in ns:
                continue
            k = links - n + h
            ours = own[3 + k : 4 + k, mine]
            theirs = received[at + 3 + k : at + 4 + k, pl.ds(halo_place(right, links, length, h), length)]
            coord = 4.0 * own[0:1, mine]
            coord = jnp.where(jnp.where(right, ours, theirs) == 1.0, coord, coord + FAR)
            rows[3 + h, :, lanes] = jnp.broadcast_to(coord, (8, length))


def fill_halo(right, received, columns, pieces, out, halves, rows, links, beside):
    probe_count = out.shape[0]
    length = received.shape[1] // links
    blocks = out.shape[1] // length
    for h in range(max(h for h, _, _ in pieces) + 1):
        place = pl.ds(halo_place(right, links, length, h), length)
        store_halves(halves, h * length, received[0:probe_count, place])

    def product(h, n, k_high, k_low, lanes):
        own = pl.ds(own_place(right, blocks, links, length, n), length)
        at = slice(h * length, (h + 1) * length)

        def step():
            out[:, own] = out[:, own] + multiply(halves[:, at], k_high[:, lanes], k_low[:, lanes])

        return step

    for h, ns, (k_high, k_low) in pieces:
        lanes = slice((ns[0] - 1) * length, ns[-1] * length)
        fill_tiles(k_high, k_low, 0, columns, h * length, length, rows, 3 + h, lanes, 0, beside)
        beside = []
        for n in ns:
            beside.append(product(h, n, k_high, k_low, slice((n - ns[0]) * length, (n - ns[0] + 1) * length)))
    return beside


def part_of(tables, rows, lanes):
    return tuple(table.at[rows, lanes] for table in tables)


def early_tables(tables, links, length):
    return {n: part_of(tables, slice(0, n * length), slice((n - 1) * length, n * length)) for n in range(1, links)}


def halo_product(right, load, tables, out, halves, links):
    length = halves.shape[1] // links
    blocks = out.shape[1] // length
    for h in range(max(tables)):
        store_halves(halves, h * length, load(pl.ds(halo_place(right, links, length, h), length)))
    for n, (k_high, k_low) in tables.items():
        own = pl.ds(own_place(right, blocks, links, length, n), length)
        out[:, own] = out[:, own] + multiply(halves[:, 0 : n * length], k_high[...], k_low[...])


def own_product(right, vector, tables, out, halves, blocks):
    span = out.shape[1]
    length = vector.shape[1] // blocks
    links = span // length
    k_high, k_low = tables
    for n in range(1, links + 1):
        own = pl.ds(own_place(right, blocks, links, length, n), length)
        store_halves(halves, (n - 1) * length, vector[:, own])
    for h in range(links):
        deep, at = slice(h * length, span), slice(h * length, (h + 1) * length)
        place = pl.ds(halo_place(right, links, length, h), length)
        out[:, place] = multiply(halves[:, deep], k_high[at, deep], k_low[at, deep], turned=True)


def store_send(right, vector, send):
    here, span = vector.shape[1], send.shape[1]
    rows = vector.shape[0]
    send[0:rows, :] = vector[:, pl.ds(send_place(right, here, span), span)]
    if send.shape[0] > rows:
        send[rows:, :] = jnp.zeros((send.shape[0] - rows, span), F32)


def store_tiles(right, vector, send):
    here, count = vector.shape[1], vector.shape[0] // 8
    wide = (send.shape[0] - 1) // count
    start = send_place(right, here, wide * 128)
    for c in range(wide):
        lanes = pl.ds(pl.multiple_of(start + c * 128, 128), 128)
        send[c * count : (c + 1) * count] = vector[:, lanes].reshape(count, 8, 128)
    send[wide * count :] = jnp.zeros((1, 8, 128), F32)


def load_tiles(received, rows, at):
    count = rows // 8
    parts = []
    for c in range(at.size // 128):
        tile = (at.start // 128 + c) * count
        parts.append(received[pl.ds(tile, count)].reshape(rows, 128))
    return jnp.concatenate(parts, axis=1)


def mate_first_kernel(own, partial, received, k_high, k_low, out, to_next, columns, halves, rows, *, links):
    right = is_right(True)
    length = halves.shape[1] // links
    at = out.shape[0]
    pieces = [(h, range(h + 1, links)) for h in range(links - 1)]
    steps = []
    for h in range(links):
        steps += halo_columns(right, received, at, columns, links, h)
    for step in steps[0:2]:
        step()
    own_rows(right, own, received, at, rows, links, pieces)
    out[...] = partial[...]
    tables = (k_high, k_low)
    pieces = [
        (h, ns, part_of(tables, slice(h * length, (h + 1) * length), slice(h * length, (links - 1) * length)))
        for h, ns in pieces
    ]
    for step in fill_halo(right, received, columns, pieces, out, halves, rows, links, steps[2:]):
        step()
    store_send(is_right(False), out, to_next)


def next_first_kernel(
    own,
    partial,
    mate,
    mate_columns,
    received,
    mate_high,
    mate_low,
    k_high,
    k_low,
    out,
    to_mate,
    mate_halves,
    mate_rows,
    halves,
    rows,
    columns,
    *,
    links,
):
    length = halves.shape[1] // links
    at = out.shape[0]
    out[...] = partial[...]
    left, right = is_right(True), is_right(False)
    late = [(h, range(links, links + 1)) for h in range(links)]
    all_of = [(h, range(h + 1, links + 1)) for h in range(links)]
    own_rows(left, own, mate, at, mate_rows, links, late)
    own_rows(right, own, received, at, rows, links, all_of)
    steps = []
    for h in range(links):
        steps += halo_columns(right, received, at, columns, links, h)
    tables = (mate_high, mate_low)
    pieces = [(h, ns, part_of(tables, slice(h * length, (h + 1) * length), slice(0, length))) for h, ns in late]
    steps = fill_halo(left, mate, mate_columns, pieces, out, mate_halves, mate_rows, links, steps)
    tables = (k_high, k_low)
    pieces = [
        (h, ns, part_of(tables, slice(h * length, (h + 1) * length), slice(h * length, links * length)))
        for h, ns in all_of
    ]
    for step in fill_halo(right, received, columns, pieces, out, halves, rows, links, steps):
        step()
    store_send(is_right(True), out, to_mate)


def sum_rows(terms):
    rows = []
    for left, right in terms:
        part = None
        for at in range(0, left.shape[1], 128):
            term = left[:, at : at + 128] * right[:, at : at + 128]
            part = term if part is None else part + term
        rows.append(jnp.sum(jnp.transpose(part), axis=0, keepdims=True))
    return rows


def local_second_kernel(own, second, k_high, k_low, out, halves, *, length):
    local_product(own, second, k_high, k_low, out, halves, length)


def local_third_kernel(
    own, first, second, third, k_high, k_low, next_high, next_low, out, given, table, halves, own_halves, *, length
):
    local_product(own, third, k_high, k_low, out, halves, length)
    own_product(is_right(False), second, (next_high, next_low), given, own_halves, out.shape[1] // length)
    found = sum_rows(((first, first), (first, second), (second, second), (second, third), (third, third)))
    table[...] = jnp.concatenate(found + [jnp.zeros_like(found[0])] * 3, axis=0)


def mate_second_kernel(partial, mate, k_high, k_low, out, to_next, halves, *, links):
    length = halves.shape[1] // links
    out[...] = partial[...]
    tables = early_tables((k_high, k_low), links, length)
    halo_product(is_right(True), lambda at: mate[:, at], tables, out, halves, links)
    store_tiles(is_right(False), out, to_next)


def next_tables(tables, links, length):
    return {n: part_of(tables, slice(0, n * length), slice((n - 1) * length, n * length)) for n in range(1, links + 1)}


def next_second_kernel(
    partial, first, mate, ahead, mate_high, mate_low, k_high, k_low, out, to_mate, halves, given, *, links
):
    length = halves.shape[1] // links
    right = is_right(False)
    out[...] = partial[...]
    halo_product(is_right(True), lambda at: mate[:, at], {links: (mate_high, mate_low)}, out, halves, links)
    own_product(right, first, (k_high, k_low), given, halves, links + 1)
    tables = next_tables((k_high, k_low), links, length)
    halo_product(right, received_share(ahead, given), tables, out, halves, links)
    store_send(is_right(True), out, to_mate)


def received_share(received, given):
    return lambda at: received[0 : given.shape[0], at] + given[:, at]


def mate_third_kernel(partial, mate, early_high, early_low, late_high, late_low, out, halves, *, links):
    length = halves.shape[1] // links
    out[...] = partial[...]
    tables = early_tables((early_high, early_low), links, length)
    tables[links] = (late_high, late_low)
    halo_product(is_right(True), lambda at: mate[:, at], tables, out, halves, links)


def next_third_kernel(partial, after, given, k_high, k_low, third, table, out, sums, halves, *, links):
    length = halves.shape[1] // links
    out[...] = partial[...]
    tables = next_tables((k_high, k_low), links, length)
    share = lambda at: load_tiles(after, out.shape[0], at) + given[:, at]
    halo_product(is_right(False), share, tables, out, halves, links)
    late = sum_rows(((third, out), (out, out)))
    upper = jnp.concatenate([table[4:5, :]] + late + [jnp.zeros_like(late[0])], axis=0)
    compact = jnp.concatenate([table[0:4, :], upper], axis=1)
    sums[...] = jnp.broadcast_to(compact[None], sums.shape)


def polynomials(moment):
    def dot(p, q):
        total, size = 0.0, 0.0
        for i, x in enumerate(p):
            for j, y in enumerate(q):
                term = x * y * moment[i + j]
                total, size = total + term, size + jnp.abs(term)
        return total, size

    def add(p, q, factor):
        count = max(len(p), len(q))
        p, q = p + [0.0] * (count - len(p)), q + [0.0] * (count - len(q))
        return [x + factor * y for x, y in zip(p, q)]

    one = jnp.ones_like(moment[0])
    solution, residual, direction = [jnp.zeros_like(one)], [one], [one]
    norm = moment[0]
    good = norm > 0.0
    for step in range(ITERS):
        image = add([0.0 * one] + direction, direction, SHIFT)
        curvature, size = dot(direction, image)
        good = good & (size <= MAX_AMP * curvature)
        step_size = norm / curvature
        solution = add(solution, direction, step_size)
        residual = add(residual, image, -step_size)
        new, size = dot(residual, residual)
        if step < ITERS - 1:
            good = good & (size <= MAX_AMP * new)
            direction = add(residual, direction, new / norm)
        norm = new
    size = sum(jnp.abs(x) * jnp.sqrt(moment[2 * i]) for i, x in enumerate(residual))
    good = good & (size * size <= MAX_NORM * MAX_NORM * norm)
    return solution, residual, good


def finish_kernel(sums, first, second, third, fourth, solution, residual, good):
    total = jnp.sum(sums[...], axis=0)
    rows = first.shape[0]
    moment = [total[k : k + 1, 0:rows] for k in range(4)] + [total[k : k + 1, rows : 2 * rows] for k in range(3)]
    mix_solution, mix_residual, fine = polynomials(moment)
    table = jnp.concatenate(mix_solution + mix_residual + [jnp.zeros_like(moment[0])], axis=0)
    table = jnp.concatenate([table, jnp.zeros_like(table)], axis=1)
    table = jnp.transpose(jnp.concatenate([table, jnp.zeros((120, 128), F32)], axis=0))[0:rows]
    basis = (first[...], second[...], third[...], fourth[...])

    def mix(at, count):
        total = table[:, at : at + 1] * basis[0]
        for k in range(1, count):
            total = total + table[:, at + k : at + k + 1] * basis[k]
        return total

    solution[...] = mix(0, ITERS)
    residual[...] = mix(ITERS, ITERS + 1)
    good[0, 0] = jnp.min(jnp.where(fine, 1.0, 0.0))


VMEM = pl.BlockSpec(memory_space=pltpu.VMEM)
SMEM = pl.BlockSpec(memory_space=pltpu.SMEM)
ANY = pl.BlockSpec(memory_space=pl.ANY)


def call(kernel, name, out_shape, in_specs, scratch_shapes=(), out_specs=None):
    kwargs = {} if out_specs is None else {"out_specs": out_specs}
    return pl.pallas_call(
        kernel,
        out_shape=out_shape,
        in_specs=in_specs,
        scratch_shapes=scratch_shapes,
        compiler_params=pltpu.CompilerParams(vmem_limit_bytes=VMEM_LIMIT),
        name=name,
        **kwargs,
    )


def swap_mate(array):
    return lax.ppermute(array, AXES, [(i, i ^ 1) for i in range(lax.axis_size(AXES))])


def swap_next(array):
    return lax.ppermute(array, AXES, [(i, i + 1 if i % 2 else i - 1) for i in range(1, lax.axis_size(AXES) - 1)])


def per_device(coords, noise_var, pair_list, probes):
    rows, here = probes.shape
    links, blocks = pair_list.shape
    length = here // blocks
    span = links * length
    noise = noise_var.reshape(1, here)

    whole = jax.ShapeDtypeStruct((rows, here), F32)
    part = jax.ShapeDtypeStruct((rows, span), F32)
    packed = jax.ShapeDtypeStruct((rows + 8, span), F32)
    wide_packed = jax.ShapeDtypeStruct((rows + 16, span), F32)
    wide_part = jax.ShapeDtypeStruct((rows + 8, span), F32)
    tiled_part = jax.ShapeDtypeStruct((rows // 8 * (span // 128) + 1, 8, 128), F32)
    sums_table = jax.ShapeDtypeStruct((8, rows), F32)
    local_table = jax.ShapeDtypeStruct((here, here), BF16)
    halo_table = jax.ShapeDtypeStruct((span, span), BF16)
    local_halves = pltpu.VMEM((2 * rows, here), BF16)
    halo_halves = pltpu.VMEM((2 * rows, span), BF16)

    to_mate, to_next, own = call(
        pack_kernel,
        "pack",
        (packed, wide_packed, jax.ShapeDtypeStruct((8, here), F32)),
        [ANY] * 4,
        [
            pltpu.VMEM((3, here), F32),
            pltpu.SMEM((links, blocks), jnp.int32),
            pltpu.VMEM((1, here), F32),
            pltpu.SemaphoreType.DMA((5,)),
        ],
    )(coords, pair_list, noise, probes)
    mate, beyond = swap_mate(to_mate), swap_next(to_next)
    k_high, k_low, partial, first = call(
        functools.partial(local_first_kernel, links=links),
        "local_first",
        (local_table, local_table, whole, whole),
        [VMEM, ANY],
        [
            local_halves,
            pltpu.VMEM((3, here, 128), F32),
            pltpu.VMEM((3 + blocks, 8, here), F32),
            pltpu.SemaphoreType.DMA((1,)),
        ],
    )(own, probes)
    halo_scratch = [halo_halves, pltpu.VMEM((3 + links, 8, span), F32)]
    early_table = jax.ShapeDtypeStruct((span - length, span - length), BF16)
    late_table = jax.ShapeDtypeStruct((span, length), BF16)
    halo_columns_of = jax.ShapeDtypeStruct((3, span, 128), F32)
    early_high, early_low, partial, to_next, mate_columns = call(
        functools.partial(mate_first_kernel, links=links),
        "mate_first",
        (early_table, early_table, whole, wide_part, halo_columns_of),
        [VMEM] * 3,
        halo_scratch,
    )(own, partial, mate)
    ahead = swap_next(to_next)
    late_high, late_low, next_high, next_low, second, to_mate = call(
        functools.partial(next_first_kernel, links=links),
        "next_first",
        (late_table, late_table, halo_table, halo_table, whole, part),
        [VMEM] * 5,
        halo_scratch + halo_scratch + [pltpu.VMEM((3, span, 128), F32)],
    )(own, partial, mate, mate_columns, beyond)

    mate = swap_mate(to_mate)
    partial = call(
        functools.partial(local_second_kernel, length=length), "local_second", whole, [VMEM] * 4, [local_halves]
    )(own, second, k_high, k_low)
    partial, to_next = call(
        functools.partial(mate_second_kernel, links=links), "mate_second", (whole, tiled_part), [VMEM] * 4, [halo_halves]
    )(partial, mate, early_high, early_low)
    after = swap_next(to_next)
    third, to_mate = call(
        functools.partial(next_second_kernel, links=links),
        "next_second",
        (whole, part),
        [VMEM] * 8,
        [halo_halves, pltpu.VMEM((rows, span), F32)],
    )(partial, first, mate, ahead, late_high, late_low, next_high, next_low)

    mate = swap_mate(to_mate)
    partial, given, table = call(
        functools.partial(local_third_kernel, length=length),
        "local_third",
        (whole, part, sums_table),
        [VMEM] * 8,
        [local_halves, halo_halves],
    )(own, first, second, third, k_high, k_low, next_high, next_low)
    regions, subs = lax.axis_size("region"), lax.axis_size("sub")
    partial = call(
        functools.partial(mate_third_kernel, links=links), "mate_third", whole, [VMEM] * 6, [halo_halves]
    )(partial, mate, early_high, early_low, late_high, late_low)
    fourth, sums = call(
        functools.partial(next_third_kernel, links=links),
        "next_third",
        (whole, jax.ShapeDtypeStruct((regions, 4, 128), F32)),
        [VMEM] * 7,
        [halo_halves],
    )(partial, after, given, next_high, next_low, third, table)

    sums = jnp.sum(lax.all_to_all(sums, "region", 0, 0), axis=0)
    sums = lax.all_to_all(jnp.broadcast_to(sums[None], (subs, 4, 128)), "sub", 0, 0)
    solution, residual, good = call(
        finish_kernel,
        "finish",
        (whole, whole, jax.ShapeDtypeStruct((1, 1), F32)),
        [VMEM] * 5,
        out_specs=(VMEM, VMEM, SMEM),
    )(sums, first, second, third, fourth)

    def again(state):
        solution, residual = plain(coords, noise_var, pair_list, probes)
        return jnp.ones_like(state[0]), solution, residual

    _, solution, residual = lax.while_loop(lambda state: state[0][0, 0] < 0.5, again, (good, solution, residual))
    return solution, residual


def solution(mesh):
    in_specs = (P(None, AXES), P(AXES), P(None, AXES), P(None, AXES))
    out_specs = (P(None, AXES), P(None, AXES))
    return jax.shard_map(per_device, mesh=mesh, in_specs=in_specs, out_specs=out_specs, check_vma=False)
```

```python
import functools

import jax
import jax.numpy as jnp
from jax import lax
from jax.experimental import pallas as pl
from jax.experimental.pallas import tpu as pltpu
from jax.sharding import PartitionSpec as P

ITERS = 3
AXES = ("region", "sub")
SHIFT = 6.0
SCALE = 1.0 / 256.0
FAR = 65536.0
MAX_AMP = 100.0
MAX_NORM = 30.0
F32 = jnp.float32
BF16 = jnp.bfloat16
VMEM_LIMIT = 40 * 1024 * 1024


def shifted(array, by):
    count = lax.axis_size(AXES)
    pairs = [(i, i + by) for i in range(count) if 0 <= i + by < count]
    return lax.ppermute(array, AXES, pairs)


def wendland(left, right):
    squared = (left[0][..., :, None] - right[0][..., None, :]) ** 2
    squared = squared + (left[1][..., :, None] - right[1][..., None, :]) ** 2
    squared = squared + (left[2][..., :, None] - right[2][..., None, :]) ** 2
    distance = jnp.sqrt(squared)
    support = jnp.maximum(1.0 - distance, 0.0)
    return support**4 * (4.0 * distance + 1.0)


def squares(residual):
    return lax.psum(jnp.sum(residual * residual, axis=1), AXES)


def plain(coords, noise_var, pair_list, probes):
    probe_count, points_here = probes.shape
    links = pair_list.shape[0]
    blocks_here = pair_list.shape[1]
    block_len = points_here // blocks_here
    span_cols = links * block_len
    local_c = coords.reshape(3, blocks_here, block_len)
    weights = pair_list.astype(F32)
    ahead_c = shifted(coords[:, :span_cols], -1)
    ext_c = jnp.concatenate([local_c, ahead_c.reshape(3, links, block_len)], axis=1)

    def step(_, state):
        solution, residual, direction, res_norm = state
        ahead_v = shifted(direction[:, :span_cols], -1)
        ext_v = jnp.concatenate([direction, ahead_v], axis=1).reshape(probe_count, blocks_here + links, block_len)
        local_v = ext_v[:, :blocks_here]
        result = (noise_var[None, :] * direction).reshape(probe_count, blocks_here, block_len)
        spill = jnp.zeros((probe_count, blocks_here + links, block_len), F32)
        for offset in range(links + 1):
            kernel_block = wendland(local_c, ext_c[:, offset : offset + blocks_here])
            if offset > 0:
                kernel_block = kernel_block * weights[offset - 1][:, None, None]
            result = result + jnp.einsum(
                "pbj,bij->pbi", ext_v[:, offset : offset + blocks_here], kernel_block, precision=lax.Precision.HIGHEST
            )
            if offset > 0:
                spill = spill.at[:, offset : offset + blocks_here].add(
                    jnp.einsum("pbi,bij->pbj", local_v, kernel_block, precision=lax.Precision.HIGHEST)
                )
        result = result + spill[:, :blocks_here]
        result = result.at[:, :links].add(shifted(spill[:, blocks_here:], 1))
        product = result.reshape(probe_count, points_here)
        step_size = res_norm / lax.psum(jnp.sum(direction * product, axis=1), AXES)
        solution = solution + step_size[:, None] * direction
        residual = residual - step_size[:, None] * product
        next_norm = squares(residual)
        direction = residual + (next_norm / res_norm)[:, None] * direction
        return solution, residual, direction, next_norm

    state = (jnp.zeros_like(probes), probes, probes, squares(probes))
    solution, residual, _, _ = lax.fori_loop(0, ITERS, step, state)
    return solution, residual


def is_right(mate):
    return lax.axis_index("sub") % 2 == (0 if mate else 1)


def own_place(right, blocks, links, length, n):
    return pl.multiple_of(jnp.where(right, blocks - 1 - links + n, links - n) * length, 128)


def halo_place(right, links, length, h):
    return pl.multiple_of(jnp.where(right, h, links - 1 - h) * length, 128)


def send_place(right, here, span):
    return pl.multiple_of(jnp.where(right, here - span, 0), 128)


def split(value):
    high = value.astype(BF16)
    return high, (value - high.astype(F32)).astype(BF16)


def start_all(copies):
    for copy in copies:
        copy.start()
    return copies


def pack_kernel(coords, pair, noise, probes, to_mate, to_next, own, points, flags, variance, sem):
    links, blocks = pair.shape
    here = coords.shape[1]
    length = here // blocks
    rows, span = probes.shape[0], links * length
    place = [send_place(is_right(mate), here, span) for mate in (True, False)]
    copies = start_all(
        [
            pltpu.make_async_copy(pair, flags, sem.at[0]),
            pltpu.make_async_copy(coords, points, sem.at[1]),
            pltpu.make_async_copy(noise, variance, sem.at[4]),
            pltpu.make_async_copy(probes.at[:, pl.ds(place[0], span)], to_mate.at[0:rows], sem.at[2]),
            pltpu.make_async_copy(probes.at[:, pl.ds(place[1], span)], to_next.at[0:rows], sem.at[3]),
        ]
    )
    for copy in copies[0:3]:
        copy.wait()
    right = is_right(True)
    extra = [points[...]]
    for k in range(links):
        flag = [flags[k, b].astype(F32) for b in range(blocks)]
        extra.append(jnp.concatenate([jnp.full((1, length), f, F32) for f in flag], axis=1))
    extra = jnp.concatenate(extra + [variance[...], jnp.zeros((8 - 4 - links, here), F32)], axis=0)
    own[...] = extra
    low, high = extra[:, 0:span], extra[:, here - span :]
    to_mate[rows : rows + 8, :] = jnp.where(right, high, low)
    to_next[rows : rows + 8, :] = jnp.where(right, low, high)
    to_next[rows + 8 :, :] = jnp.zeros((to_next.shape[0] - rows - 8, span), F32)
    copies[3].wait()
    copies[4].wait()


def column_steps(columns, at, load):
    def fill(d, turned):
        size = turned.shape[0]
        columns[d, at : at + size, :] = jnp.broadcast_to(turned[:, d : d + 1], (size, 128))

    def step():
        turned = jnp.transpose(load())
        for d in range(3):
            fill(d, turned)

    return [step]


def fill_strip(k_high, k_low, to_row, columns, from_row, strip, rows, x, at, first):
    column = [columns[d, pl.ds(from_row, strip), :].reshape(strip // 8, 8, 128) for d in range(3)]
    for lane in range(at.start, at.stop, 128):
        squared = None
        for d in range(3):
            away = column[d] - rows[d if d else x, :, lane : lane + 128][None]
            squared = away * away if squared is None else squared + away * away
        squared = jnp.maximum(squared, 1e-30)
        distance = squared * lax.rsqrt(squared)
        support = jnp.maximum(4.0 - distance, 0.0)
        support = support * support
        value = support * support * (distance + 1.0)
        top, rest = split(value.reshape(strip, 128))
        to = slice(first + lane - at.start, first + lane - at.start + 128)
        k_high[pl.ds(to_row, strip), to] = top
        k_low[pl.ds(to_row, strip), to] = rest


def fill_tiles(k_high, k_low, to_row, columns, from_row, count, rows, x, at, first, beside=()):
    strip = 64 if at.stop - at.start <= 4 * 128 else 32
    if not beside:

        def body(s, _):
            step = pl.multiple_of(s * strip, strip)
            fill_strip(k_high, k_low, to_row + step, columns, from_row + step, strip, rows, x, at, first)
            return 0

        lax.fori_loop(0, count // strip, body, 0)
        return
    done = 0
    for s in range(count // strip):
        step = s * strip
        fill_strip(k_high, k_low, to_row + step, columns, from_row + step, strip, rows, x, at, first)
        while done < len(beside) * (s + 1) * strip // count:
            beside[done]()
            done += 1


def store_halves(halves, at, vector):
    rows, size = vector.shape
    top, rest = split(vector * SCALE)
    halves[0:rows, at : at + size] = top
    halves[rows : 2 * rows, at : at + size] = rest


def multiply(both, k_high, k_low, turned=False):
    rows = both.shape[0] // 2
    dims = (((1,), (1 if turned else 0,)), ((), ()))
    most = lax.dot_general(both, k_high, dims, preferred_element_type=F32)
    rest = lax.dot_general(both[0:rows], k_low, dims, preferred_element_type=F32)
    return most[0:rows] + (most[rows : 2 * rows] + rest)


def local_product(own, vector, k_high, k_low, out, halves, length):
    here = vector.shape[1]
    noise = own[3 + here // length - 1 : 3 + here // length, :]
    store_halves(halves, 0, vector[...])
    for start in range(0, here, length):
        stop = start + length
        at, before, after = slice(start, stop), slice(0, stop), slice(stop, here)
        value = multiply(halves[:, before], k_high[before, at], k_low[before, at])
        if stop < here:
            value = value + multiply(halves[:, after], k_high[at, after], k_low[at, after], turned=True)
        out[:, at] = value + (noise[:, at] - SHIFT) * vector[:, at]


def row_steps(halves, k_high, k_low, out, start, length):
    stop, here = start + length, out.shape[1]
    steps = []

    def natural(at):
        def step():
            out[:, at] = out[:, at] + multiply(halves[:, start:stop], k_high[start:stop, at], k_low[start:stop, at])

        return step

    def mirrored(at):
        def step():
            value = multiply(halves[:, at], k_high[start:stop, at], k_low[start:stop, at], turned=True)
            out[:, start:stop] = out[:, start:stop] + value

        return step

    for at in range(start, here, length):
        steps.append(natural(slice(at, at + length)))
    for at in range(stop, here, length):
        steps.append(mirrored(slice(at, at + length)))
    return steps


def local_first_kernel(own, probes, k_high, k_low, out, first, halves, columns, rows, sem, *, links):
    noise = own[3 + links : 4 + links, :]
    here = own.shape[1]
    blocks = links + 1
    length = here // blocks
    copy = pltpu.make_async_copy(probes, first, sem.at[0])
    copy.start()
    for d in range(1, 3):
        rows[d] = jnp.broadcast_to(4.0 * own[d : d + 1, :], rows.shape[1:])
    steps = []
    for j in range(blocks):
        half = length // 2
        for at in (j * length, j * length + half):
            steps += column_steps(columns, at, lambda at=at: 4.0 * own[:, at : at + half])
    for step in steps[0:2]:
        step()
    steps = steps[2:]
    for i in range(blocks):
        for j in range(i, blocks):
            at = slice(j * length, (j + 1) * length)
            moved = 4.0 * own[0:1, at]
            if j > i:
                flag = own[2 + j - i : 3 + j - i, i * length : (i + 1) * length]
                moved = jnp.where(flag == 1.0, moved, moved + FAR)
            rows[3 + i, :, at] = jnp.broadcast_to(moved, (8, length))
        start = i * length
        fill_tiles(k_high, k_low, start, columns, start, length, rows, 3 + i, slice(start, here), start, steps)
        if i == 0:
            copy.wait()
            store_halves(halves, 0, first[...])
            out[...] = (noise - SHIFT) * first[...]
        steps = row_steps(halves, k_high, k_low, out, start, length)
    for step in steps:
        step()


def halo_columns(right, received, at, columns, links, h):
    length = received.shape[1] // links
    half = length // 2
    steps = []
    for part in range(2):
        place = pl.ds(pl.multiple_of(halo_place(right, links, length, h) + part * half, 128), half)
        steps += column_steps(columns, h * length + part * half, lambda place=place: 4.0 * received[at : at + 8, place])
    return steps


def own_rows(right, own, received, at, rows, links, pieces):
    length = received.shape[1] // links
    blocks = own.shape[1] // length
    for n in sorted({n for _, ns in pieces for n in ns}):
        mine = pl.ds(own_place(right, blocks, links, length, n), length)
        lanes = slice((n - 1) * length, n * length)
        for d in range(1, 3):
            rows[d, :, lanes] = jnp.broadcast_to(4.0 * own[d : d + 1, mine], (8, length))
        for h, ns in pieces:
            if n not in ns:
                continue
            k = links - n + h
            ours = own[3 + k : 4 + k, mine]
            theirs = received[at + 3 + k : at + 4 + k, pl.ds(halo_place(right, links, length, h), length)]
            coord = 4.0 * own[0:1, mine]
            coord = jnp.where(jnp.where(right, ours, theirs) == 1.0, coord, coord + FAR)
            rows[3 + h, :, lanes] = jnp.broadcast_to(coord, (8, length))


def fill_halo(right, received, columns, pieces, out, halves, rows, links, beside):
    probe_count = out.shape[0]
    length = received.shape[1] // links
    blocks = out.shape[1] // length
    for h in range(max(h for h, _, _ in pieces) + 1):
        place = pl.ds(halo_place(right, links, length, h), length)
        store_halves(halves, h * length, received[0:probe_count, place])

    def product(h, n, k_high, k_low, lanes):
        own = pl.ds(own_place(right, blocks, links, length, n), length)
        at = slice(h * length, (h + 1) * length)

        def step():
            out[:, own] = out[:, own] + multiply(halves[:, at], k_high[:, lanes], k_low[:, lanes])

        return step

    for h, ns, (k_high, k_low) in pieces:
        lanes = slice((ns[0] - 1) * length, ns[-1] * length)
        fill_tiles(k_high, k_low, 0, columns, h * length, length, rows, 3 + h, lanes, 0, beside)
        beside = []
        for n in ns:
            beside.append(product(h, n, k_high, k_low, slice((n - ns[0]) * length, (n - ns[0] + 1) * length)))
    return beside


def part_of(tables, rows, lanes):
    return tuple(table.at[rows, lanes] for table in tables)


def early_tables(tables, links, length):
    return {n: part_of(tables, slice(0, n * length), slice((n - 1) * length, n * length)) for n in range(1, links)}


def halo_product(right, load, tables, out, halves, links):
    length = halves.shape[1] // links
    blocks = out.shape[1] // length
    for h in range(max(tables)):
        store_halves(halves, h * length, load(pl.ds(halo_place(right, links, length, h), length)))
    for n, (k_high, k_low) in tables.items():
        own = pl.ds(own_place(right, blocks, links, length, n), length)
        out[:, own] = out[:, own] + multiply(halves[:, 0 : n * length], k_high[...], k_low[...])


def own_product(right, vector, tables, out, halves, blocks):
    span = out.shape[1]
    length = vector.shape[1] // blocks
    links = span // length
    k_high, k_low = tables
    for n in range(1, links + 1):
        own = pl.ds(own_place(right, blocks, links, length, n), length)
        store_halves(halves, (n - 1) * length, vector[:, own])
    for h in range(links):
        deep, at = slice(h * length, span), slice(h * length, (h + 1) * length)
        place = pl.ds(halo_place(right, links, length, h), length)
        out[:, place] = multiply(halves[:, deep], k_high[at, deep], k_low[at, deep], turned=True)


def store_send(right, vector, send):
    here, span = vector.shape[1], send.shape[1]
    rows = vector.shape[0]
    send[0:rows, :] = vector[:, pl.ds(send_place(right, here, span), span)]
    if send.shape[0] > rows:
        send[rows:, :] = jnp.zeros((send.shape[0] - rows, span), F32)


def store_tiles(right, vector, send):
    here, count = vector.shape[1], vector.shape[0] // 8
    wide = (send.shape[0] - 1) // count
    start = send_place(right, here, wide * 128)
    for c in range(wide):
        lanes = pl.ds(pl.multiple_of(start + c * 128, 128), 128)
        send[c * count : (c + 1) * count] = vector[:, lanes].reshape(count, 8, 128)
    send[wide * count :] = jnp.zeros((1, 8, 128), F32)


def load_tiles(received, rows, at):
    count = rows // 8
    parts = []
    for c in range(at.size // 128):
        tile = (at.start // 128 + c) * count
        parts.append(received[pl.ds(tile, count)].reshape(rows, 128))
    return jnp.concatenate(parts, axis=1)


def mate_first_kernel(own, partial, received, k_high, k_low, out, to_next, columns, halves, rows, *, links):
    right = is_right(True)
    length = halves.shape[1] // links
    at = out.shape[0]
    pieces = [(h, range(h + 1, links)) for h in range(links - 1)]
    steps = []
    for h in range(links):
        steps += halo_columns(right, received, at, columns, links, h)
    for step in steps[0:2]:
        step()
    own_rows(right, own, received, at, rows, links, pieces)
    out[...] = partial[...]
    tables = (k_high, k_low)
    pieces = [
        (h, ns, part_of(tables, slice(h * length, (h + 1) * length), slice(h * length, (links - 1) * length)))
        for h, ns in pieces
    ]
    for step in fill_halo(right, received, columns, pieces, out, halves, rows, links, steps[2:]):
        step()
    store_send(is_right(False), out, to_next)


def next_first_kernel(
    own,
    partial,
    mate,
    mate_columns,
    received,
    mate_high,
    mate_low,
    k_high,
    k_low,
    out,
    to_mate,
    mate_halves,
    mate_rows,
    halves,
    rows,
    columns,
    *,
    links,
):
    length = halves.shape[1] // links
    at = out.shape[0]
    out[...] = partial[...]
    left, right = is_right(True), is_right(False)
    late = [(h, range(links, links + 1)) for h in range(links)]
    all_of = [(h, range(h + 1, links + 1)) for h in range(links)]
    own_rows(left, own, mate, at, mate_rows, links, late)
    own_rows(right, own, received, at, rows, links, all_of)
    steps = []
    for h in range(links):
        steps += halo_columns(right, received, at, columns, links, h)
    tables = (mate_high, mate_low)
    pieces = [(h, ns, part_of(tables, slice(h * length, (h + 1) * length), slice(0, length))) for h, ns in late]
    steps = fill_halo(left, mate, mate_columns, pieces, out, mate_halves, mate_rows, links, steps)
    tables = (k_high, k_low)
    pieces = [
        (h, ns, part_of(tables, slice(h * length, (h + 1) * length), slice(h * length, links * length)))
        for h, ns in all_of
    ]
    for step in fill_halo(right, received, columns, pieces, out, halves, rows, links, steps):
        step()
    store_send(is_right(True), out, to_mate)


def sum_rows(terms):
    rows = []
    for left, right in terms:
        part = None
        for at in range(0, left.shape[1], 128):
            term = left[:, at : at + 128] * right[:, at : at + 128]
            part = term if part is None else part + term
        rows.append(jnp.sum(jnp.transpose(part), axis=0, keepdims=True))
    return rows


def local_second_kernel(own, first, second, k_high, k_low, next_high, next_low, out, given, halves, own_halves, *, length):
    local_product(own, second, k_high, k_low, out, halves, length)
    own_product(is_right(False), first, (next_high, next_low), given, own_halves, out.shape[1] // length)


def local_third_kernel(
    own, first, second, third, k_high, k_low, next_high, next_low, out, given, table, halves, own_halves, *, length
):
    local_product(own, third, k_high, k_low, out, halves, length)
    own_product(is_right(False), second, (next_high, next_low), given, own_halves, out.shape[1] // length)
    found = sum_rows(((first, first), (first, second), (second, second), (second, third), (third, third)))
    table[...] = jnp.concatenate(found + [jnp.zeros_like(found[0])] * 3, axis=0)


def mate_second_kernel(partial, mate, k_high, k_low, out, to_next, halves, *, links):
    length = halves.shape[1] // links
    out[...] = partial[...]
    tables = early_tables((k_high, k_low), links, length)
    halo_product(is_right(True), lambda at: mate[:, at], tables, out, halves, links)
    store_tiles(is_right(False), out, to_next)


def next_tables(tables, links, length):
    return {n: part_of(tables, slice(0, n * length), slice((n - 1) * length, n * length)) for n in range(1, links + 1)}


def next_second_kernel(
    partial, mate, ahead, given, mate_high, mate_low, k_high, k_low, out, to_mate, halves, *, links
):
    length = halves.shape[1] // links
    right = is_right(False)
    out[...] = partial[...]
    halo_product(is_right(True), lambda at: mate[:, at], {links: (mate_high, mate_low)}, out, halves, links)
    tables = next_tables((k_high, k_low), links, length)
    halo_product(right, received_share(ahead, given), tables, out, halves, links)
    store_send(is_right(True), out, to_mate)


def received_share(received, given):
    return lambda at: received[0 : given.shape[0], at] + given[:, at]


def mate_third_kernel(partial, mate, early_high, early_low, late_high, late_low, out, halves, *, links):
    length = halves.shape[1] // links
    out[...] = partial[...]
    tables = early_tables((early_high, early_low), links, length)
    tables[links] = (late_high, late_low)
    halo_product(is_right(True), lambda at: mate[:, at], tables, out, halves, links)


def next_third_kernel(partial, after, given, k_high, k_low, third, table, out, sums, halves, *, links):
    length = halves.shape[1] // links
    out[...] = partial[...]
    tables = next_tables((k_high, k_low), links, length)
    share = lambda at: load_tiles(after, out.shape[0], at) + given[:, at]
    halo_product(is_right(False), share, tables, out, halves, links)
    late = sum_rows(((third, out), (out, out)))
    upper = jnp.concatenate([table[4:5, :]] + late + [jnp.zeros_like(late[0])], axis=0)
    compact = jnp.concatenate([table[0:4, :], upper], axis=1)
    sums[...] = jnp.broadcast_to(compact[None], sums.shape)


def polynomials(moment):
    def dot(p, q):
        total, size = 0.0, 0.0
        for i, x in enumerate(p):
            for j, y in enumerate(q):
                term = x * y * moment[i + j]
                total, size = total + term, size + jnp.abs(term)
        return total, size

    def add(p, q, factor):
        count = max(len(p), len(q))
        p, q = p + [0.0] * (count - len(p)), q + [0.0] * (count - len(q))
        return [x + factor * y for x, y in zip(p, q)]

    one = jnp.ones_like(moment[0])
    solution, residual, direction = [jnp.zeros_like(one)], [one], [one]
    norm = moment[0]
    good = norm > 0.0
    for step in range(ITERS):
        image = add([0.0 * one] + direction, direction, SHIFT)
        curvature, size = dot(direction, image)
        good = good & (size <= MAX_AMP * curvature)
        step_size = norm / curvature
        solution = add(solution, direction, step_size)
        residual = add(residual, image, -step_size)
        new, size = dot(residual, residual)
        if step < ITERS - 1:
            good = good & (size <= MAX_AMP * new)
            direction = add(residual, direction, new / norm)
        norm = new
    size = sum(jnp.abs(x) * jnp.sqrt(moment[2 * i]) for i, x in enumerate(residual))
    good = good & (size * size <= MAX_NORM * MAX_NORM * norm)
    return solution, residual, good


def finish_kernel(sums, first, second, third, fourth, solution, residual, good):
    total = jnp.sum(sums[...], axis=0)
    rows = first.shape[0]
    moment = [total[k : k + 1, 0:rows] for k in range(4)] + [total[k : k + 1, rows : 2 * rows] for k in range(3)]
    mix_solution, mix_residual, fine = polynomials(moment)
    table = jnp.concatenate(mix_solution + mix_residual + [jnp.zeros_like(moment[0])], axis=0)
    table = jnp.concatenate([table, jnp.zeros_like(table)], axis=1)
    table = jnp.transpose(jnp.concatenate([table, jnp.zeros((120, 128), F32)], axis=0))[0:rows]
    basis = (first[...], second[...], third[...], fourth[...])

    def mix(at, count):
        total = table[:, at : at + 1] * basis[0]
        for k in range(1, count):
            total = total + table[:, at + k : at + k + 1] * basis[k]
        return total

    solution[...] = mix(0, ITERS)
    residual[...] = mix(ITERS, ITERS + 1)
    good[0, 0] = jnp.min(jnp.where(fine, 1.0, 0.0))


VMEM = pl.BlockSpec(memory_space=pltpu.VMEM)
SMEM = pl.BlockSpec(memory_space=pltpu.SMEM)
ANY = pl.BlockSpec(memory_space=pl.ANY)


def call(kernel, name, out_shape, in_specs, scratch_shapes=(), out_specs=None):
    kwargs = {} if out_specs is None else {"out_specs": out_specs}
    return pl.pallas_call(
        kernel,
        out_shape=out_shape,
        in_specs=in_specs,
        scratch_shapes=scratch_shapes,
        compiler_params=pltpu.CompilerParams(vmem_limit_bytes=VMEM_LIMIT),
        name=name,
        **kwargs,
    )


def swap_mate(array):
    return lax.ppermute(array, AXES, [(i, i ^ 1) for i in range(lax.axis_size(AXES))])


def swap_next(array):
    return lax.ppermute(array, AXES, [(i, i + 1 if i % 2 else i - 1) for i in range(1, lax.axis_size(AXES) - 1)])


def per_device(coords, noise_var, pair_list, probes):
    rows, here = probes.shape
    links, blocks = pair_list.shape
    length = here // blocks
    span = links * length
    noise = noise_var.reshape(1, here)

    whole = jax.ShapeDtypeStruct((rows, here), F32)
    part = jax.ShapeDtypeStruct((rows, span), F32)
    packed = jax.ShapeDtypeStruct((rows + 8, span), F32)
    wide_packed = jax.ShapeDtypeStruct((rows + 16, span), F32)
    wide_part = jax.ShapeDtypeStruct((rows + 8, span), F32)
    tiled_part = jax.ShapeDtypeStruct((rows // 8 * (span // 128) + 1, 8, 128), F32)
    sums_table = jax.ShapeDtypeStruct((8, rows), F32)
    local_table = jax.ShapeDtypeStruct((here, here), BF16)
    halo_table = jax.ShapeDtypeStruct((span, span), BF16)
    local_halves = pltpu.VMEM((2 * rows, here), BF16)
    halo_halves = pltpu.VMEM((2 * rows, span), BF16)

    to_mate, to_next, own = call(
        pack_kernel,
        "pack",
        (packed, wide_packed, jax.ShapeDtypeStruct((8, here), F32)),
        [ANY] * 4,
        [
            pltpu.VMEM((3, here), F32),
            pltpu.SMEM((links, blocks), jnp.int32),
            pltpu.VMEM((1, here), F32),
            pltpu.SemaphoreType.DMA((5,)),
        ],
    )(coords, pair_list, noise, probes)
    mate, beyond = swap_mate(to_mate), swap_next(to_next)
    k_high, k_low, partial, first = call(
        functools.partial(local_first_kernel, links=links),
        "local_first",
        (local_table, local_table, whole, whole),
        [VMEM, ANY],
        [
            local_halves,
            pltpu.VMEM((3, here, 128), F32),
            pltpu.VMEM((3 + blocks, 8, here), F32),
            pltpu.SemaphoreType.DMA((1,)),
        ],
    )(own, probes)
    halo_scratch = [halo_halves, pltpu.VMEM((3 + links, 8, span), F32)]
    early_table = jax.ShapeDtypeStruct((span - length, span - length), BF16)
    late_table = jax.ShapeDtypeStruct((span, length), BF16)
    halo_columns_of = jax.ShapeDtypeStruct((3, span, 128), F32)
    early_high, early_low, partial, to_next, mate_columns = call(
        functools.partial(mate_first_kernel, links=links),
        "mate_first",
        (early_table, early_table, whole, wide_part, halo_columns_of),
        [VMEM] * 3,
        halo_scratch,
    )(own, partial, mate)
    ahead = swap_next(to_next)
    late_high, late_low, next_high, next_low, second, to_mate = call(
        functools.partial(next_first_kernel, links=links),
        "next_first",
        (late_table, late_table, halo_table, halo_table, whole, part),
        [VMEM] * 5,
        halo_scratch + halo_scratch + [pltpu.VMEM((3, span, 128), F32)],
    )(own, partial, mate, mate_columns, beyond)

    mate = swap_mate(to_mate)
    partial, given = call(
        functools.partial(local_second_kernel, length=length),
        "local_second",
        (whole, part),
        [VMEM] * 7,
        [local_halves, halo_halves],
    )(own, first, second, k_high, k_low, next_high, next_low)
    partial, to_next = call(
        functools.partial(mate_second_kernel, links=links), "mate_second", (whole, tiled_part), [VMEM] * 4, [halo_halves]
    )(partial, mate, early_high, early_low)
    after = swap_next(to_next)
    third, to_mate = call(
        functools.partial(next_second_kernel, links=links),
        "next_second",
        (whole, part),
        [VMEM] * 8,
        [halo_halves],
    )(partial, mate, ahead, given, late_high, late_low, next_high, next_low)

    mate = swap_mate(to_mate)
    partial, given, table = call(
        functools.partial(local_third_kernel, length=length),
        "local_third",
        (whole, part, sums_table),
        [VMEM] * 8,
        [local_halves, halo_halves],
    )(own, first, second, third, k_high, k_low, next_high, next_low)
    regions, subs = lax.axis_size("region"), lax.axis_size("sub")
    partial = call(
        functools.partial(mate_third_kernel, links=links), "mate_third", whole, [VMEM] * 6, [halo_halves]
    )(partial, mate, early_high, early_low, late_high, late_low)
    fourth, sums = call(
        functools.partial(next_third_kernel, links=links),
        "next_third",
        (whole, jax.ShapeDtypeStruct((regions, 4, 128), F32)),
        [VMEM] * 7,
        [halo_halves],
    )(partial, after, given, next_high, next_low, third, table)

    sums = jnp.sum(lax.all_to_all(sums, "region", 0, 0), axis=0)
    sums = lax.all_to_all(jnp.broadcast_to(sums[None], (subs, 4, 128)), "sub", 0, 0)
    solution, residual, good = call(
        finish_kernel,
        "finish",
        (whole, whole, jax.ShapeDtypeStruct((1, 1), F32)),
        [VMEM] * 5,
        out_specs=(VMEM, VMEM, SMEM),
    )(sums, first, second, third, fourth)

    def again(state):
        solution, residual = plain(coords, noise_var, pair_list, probes)
        return jnp.ones_like(state[0]), solution, residual

    _, solution, residual = lax.while_loop(lambda state: state[0][0, 0] < 0.5, again, (good, solution, residual))
    return solution, residual


def solution(mesh):
    in_specs = (P(None, AXES), P(AXES), P(None, AXES), P(None, AXES))
    out_specs = (P(None, AXES), P(None, AXES))
    return jax.shard_map(per_device, mesh=mesh, in_specs=in_specs, out_specs=out_specs, check_vma=False)
```
